128 devices in a mesh: tm: 16 (over z, y), scene: 8 (over x, core).
Axes of the slice: x: 4, y: 4, z: 4, core: 2. Of those that a mesh axis runs over, the one named last changes fastest.
Arguments:
- frames: bfloat16 [1024, 2, 64, 384], P('tm', None, 'scene'), may hold values from -6 to 6
- conv_weight: bfloat16 [3, 3, 3, 384, 384], replicated, may hold values from -0.0625 to 0.0625
- down_weight: bfloat16 [8, 384, 384], replicated, may hold values from -0.109375 to 0.109375
- w_query: bfloat16 [384, 384], replicated, may hold values from -64 to 64
- w_key: bfloat16 [384, 384], replicated, may hold values from -2 to 2
- w_value: bfloat16 [384, 384], replicated, may hold values from -0.3125 to 0.3125
- w_out: bfloat16 [384, 384], replicated, may hold values from -0.3125 to 0.3125
- shot_lengths: int32 [8], replicated, may hold values from 1 to 64, 128 in all
- scene_label: int32 [128, 1], P('tm'), may hold values from 0 to 7; in each aligned block of 8 rows (0 to 7, 8 to 15, ...) at most 2 rows name the same one
- out_grad: bfloat16 [1024, 2, 64, 384], P('tm', None, 'scene'), may hold values from -6 to 6
Outputs:
- latent_out: bfloat16 [128, 2, 64, 384], P('tm', None, 'scene')
- frame_grad: bfloat16 [1024, 2, 64, 384], P('tm', None, 'scene')
The draws below stay inside these ranges and needn't reach their ends.
Inputs may be any that keep to these rules, and one draw needn't show every extreme that they name: `shot_lengths`: the lengths sum to 128; the longest is exactly 64. `scene_label`: within each aligned block of 8 latent frames (those of one index of tm) no label occurs more than 2 times; in some block one label occurs exactly 2 times.
All inputs are finite; a program needn't handle non-finite values.
Results may differ from the reference program's by a relative error of at most 0.008.
Values may be sent and summed in bfloat16 or wider, within the bound.
No kernel may reach another device: no remote copies, remote signals or barrier semaphores. Data moves between devices by JAX's collectives and lax.ppermute only.
A program may use at most 128 MiB of HBM per device.

```python
import math
import jax
import jax.numpy as jnp
import numpy as np
from jax import lax

C = 384
HEAD = 64
H = 2
SHOTS = 8
LF = 8
LAT = 128
FRAMES = 1024
W = 64
MOST = 64
CAP = 2
N_SCENE = 8


def shared_base(key):
    raw = jax.random.normal(jax.random.fold_in(key, 7), (C, C), jnp.float32)
    return jnp.clip(raw, -6.0, 6.0) / math.sqrt(C)


def draw_w_key(key, part):
    return shared_base(key).astype(jnp.bfloat16)


def draw_w_query(key, part):
    raw = jax.random.normal(jax.random.fold_in(key, 9), (C, C), jnp.float32)
    own = jnp.clip(raw, -6.0, 6.0) / math.sqrt(C)
    return own.astype(jnp.bfloat16)


def levels(stream_key, extent, split, low, largest):
    def one(position, shards_of):
        steps = jax.random.uniform(jax.random.fold_in(jax.random.fold_in(stream_key, 6), position), (shards_of,), jnp.float32, low / len(split), largest / len(split))
        return jnp.repeat(jnp.exp(steps), extent[position] // shards_of).reshape((-1,) + (1,) * (len(extent) - position - 1))

    loudness = one(*split[0])
    for cut in split[1:]:
        loudness = loudness * one(*cut)
    return loudness


def length_profile(count, total, bound, lean):
    portions = [(1 << 20) // math.isqrt(standing ** lean) + 1 for standing in range(2, count + 1)]
    surplus, holding = total - bound - (count - 1), [1] * (count - 1)
    while surplus > 0:
        free = [i for i in range(count - 1) if holding[i] < bound]
        whole, remaining = sum([portions[i] for i in free]), surplus
        for i in free:
            extra = min(bound - holding[i], max(1, remaining * portions[i] // whole), surplus)
            holding[i] = holding[i] + extra
            surplus = surplus - extra
    return np.array([bound] + holding)


def ragged_sizes(key, amount, total, limit, lean):
    if amount == 2:
        one = jax.random.randint(key, (), max(1, total - limit), min(limit, total - 1) + 1)
        return jnp.stack([one, total - one])
    sizes = jnp.asarray(length_profile(amount, total, limit, lean), jnp.int32)
    pairs = (amount - 1) // 2
    donor, receiver = sizes[1:1 + 2 * pairs:2], sizes[2:2 + 2 * pairs:2]
    margin = jnp.minimum(donor - 1, limit - receiver)
    moved = jax.random.randint(jax.random.fold_in(key, 1), (pairs,), 0, 1 << 20) % (margin + 1)
    sizes = sizes.at[1:1 + 2 * pairs:2].set(donor - moved).at[2:2 + 2 * pairs:2].set(receiver + moved)
    return sizes[jax.random.permutation(jax.random.fold_in(key, 2), amount)]


def assign_block(rng, own, number, rows, number_of, top, bound, slope):
    ranking = jax.random.permutation(rng, number_of)
    crowded, common = load_shares(number_of, rows * top, bound, slope, True), load_shares(number_of, rows * top, bound, slope, False)
    places = jnp.arange(number_of)

    def named(tallies, offset_by):
        used = int((tallies > 0).sum())
        fixed = max(1, used // 4)
        moved = fixed + (places - fixed + offset_by * (used - fixed)) % max(1, number_of - fixed)
        return jnp.zeros((number_of,), jnp.int32).at[ranking[jnp.where(places < fixed, places, moved)]].set(jnp.asarray(tallies, jnp.int32))

    tallies = jnp.where(number % 4 == 0, named(crowded, number // 4), named(common, number - number // 4 - 1))
    mixed = jax.random.permutation(jax.random.fold_in(own, 3), number_of)
    donor, receiver = mixed[0:number_of // 2 * 2:2], mixed[1:number_of // 2 * 2:2]
    slack = jnp.minimum(tallies[donor] - 1, bound - tallies[receiver]) // 2
    slack = jnp.where((donor == ranking[0]) | (receiver == ranking[0]) | (tallies[receiver] == 0), 0, jnp.maximum(slack, 0))
    moved = jax.random.randint(jax.random.fold_in(own, 4), (number_of // 2,), 0, 1 << 20) % (slack + 1)
    tallies = tallies.at[donor].add(-moved).at[receiver].add(moved)
    items = jnp.searchsorted(jnp.cumsum(tallies), jnp.arange(rows * top), side="right").astype(jnp.int32)
    listing = items.reshape(top, rows).T
    listing = listing[jax.random.permutation(jax.random.fold_in(own, 1), rows)]
    offset_by = jax.random.randint(jax.random.fold_in(own, 2), (rows, 1), 0, top)
    return jnp.take_along_axis(listing, (jnp.arange(top)[None, :] + offset_by) % top, axis=1)


def load_shares(count, total, limit, skew, full):
    weights = [(1 << 20) // math.isqrt(standing ** skew) + 1 for standing in range(1, count + 1)]
    largest = limit if full else min(limit, max(-(-total // count), total * weights[0] // sum(weights)))
    least = 1 if total - largest >= count - 1 else 0
    given, spare = [largest] + [least] * (count - 1), total - largest - least * (count - 1)
    while spare > 0:
        free = [i for i in range(1, count) if given[i] < largest] or [i for i in range(1, count) if given[i] < limit]
        pool, budget = sum([weights[i] for i in free]), spare
        for i in free:
            addition = min(limit - given[i], max(1, budget * weights[i] // pool), spare)
            given[i] = given[i] + addition
            spare = spare - addition
    return np.array(given)


def bell_draw(stream_key, extent, width, most, shards=(), kind=jnp.bfloat16):
    entries = width * jax.random.normal(stream_key, extent, jnp.float32)
    if shards:
        entries = entries * levels(stream_key, extent, shards, -0.22, 0.18)
    return jnp.clip(entries, -most, most).astype(kind)


def setup_inputs(seed: int = 0) -> dict:
    key_of = jax.random.split(jax.random.key(seed), 11)
    frames = bell_draw(key_of[0], (FRAMES, H, W, C), 1.0, 6.0, ((0, 16), (2, 8)))
    conv_weight = bell_draw(key_of[1], (3, 3, 3, C, C), (27 * C) ** -0.5, 0.0625)
    down_weight = bell_draw(key_of[2], (8, C, C), (8 * C) ** -0.5, 0.109375)
    w_query = draw_w_query(jax.random.fold_in(key_of[10], 71), 0)
    w_key = draw_w_key(jax.random.fold_in(key_of[10], 71), 0)
    w_value = bell_draw(key_of[5], (C, C), C ** -0.5, 0.3125)
    w_out = bell_draw(key_of[6], (C, C), C ** -0.5, 0.3125)
    shot_lengths = ragged_sizes(key_of[7], SHOTS, LAT, MOST, 2).astype(jnp.int32)
    scene_label_keys = jax.random.split(jax.random.fold_in(key_of[8], 1), LAT // LF)
    scene_label_turns = jax.random.permutation(jax.random.fold_in(key_of[8], 3), LAT // LF)
    scene_label = jax.vmap(lambda own, number: assign_block(jax.random.fold_in(key_of[8], 2), own, number, LF, N_SCENE, 1, CAP, 2))(scene_label_keys, scene_label_turns).reshape((LAT, 1))
    out_grad = bell_draw(key_of[9], (FRAMES, H, W, C), 1.0, 6.0, ((0, 16), (2, 8)))
    return dict(frames=frames, conv_weight=conv_weight, down_weight=down_weight, w_query=w_query, w_key=w_key, w_value=w_value, w_out=w_out, shot_lengths=shot_lengths, scene_label=scene_label, out_grad=out_grad)


def conv_block(padded, weight):
    frame_count = padded.shape[0] - 2
    row_count = padded.shape[1] - 2
    col_count = padded.shape[2] - 2
    chans = padded.shape[3]
    total = jnp.zeros((frame_count * row_count * col_count, weight.shape[4]), jnp.float32)
    for shift_t in range(3):
        for shift_h in range(3):
            pieces = [padded[shift_t:shift_t + frame_count, shift_h:shift_h + row_count, shift_w:shift_w + col_count] for shift_w in range(3)]
            stacked = jnp.concatenate(pieces, axis=-1).reshape(-1, 3 * chans)
            total = total + jnp.dot(stacked, weight[shift_t, shift_h].reshape(3 * chans, -1), preferred_element_type=jnp.float32)
    return total.reshape(frame_count, row_count, col_count, -1)

def slope_of(pre):
    gate_value = jax.nn.sigmoid(pre)
    return gate_value * (1.0 + pre * (1.0 - gate_value))

def attend_ref(query_tok, key_tok, allowed, w_query, w_key, w_value, w_out):
    head_count = query_tok.shape[1] // HEAD
    query_proj = jnp.dot(query_tok, w_query, preferred_element_type=jnp.float32).astype(jnp.bfloat16).reshape(-1, head_count, HEAD)
    key_proj = jnp.dot(key_tok, w_key, preferred_element_type=jnp.float32).astype(jnp.bfloat16).reshape(-1, head_count, HEAD)
    value_proj = jnp.dot(key_tok, w_value, preferred_element_type=jnp.float32).astype(jnp.bfloat16).reshape(-1, head_count, HEAD)
    scores = jnp.einsum('qhd,khd->hqk', query_proj.astype(jnp.float32), key_proj.astype(jnp.float32)) * (1.0 / math.sqrt(HEAD))
    scores = jnp.where(allowed[None], scores, -1000000000.0)
    top = lax.optimization_barrier(jnp.max(scores, axis=-1, keepdims=True))
    expo = jnp.exp(scores - top)
    probs = (expo / lax.optimization_barrier(jnp.sum(expo, axis=-1, keepdims=True))).astype(jnp.bfloat16)
    heads_out = jnp.einsum('hqk,khd->qhd', probs.astype(jnp.float32), value_proj.astype(jnp.float32)).astype(jnp.bfloat16)
    heads_out = heads_out.reshape(-1, head_count * HEAD)
    return (query_tok.astype(jnp.float32) + jnp.dot(heads_out, w_out, preferred_element_type=jnp.float32)).astype(jnp.bfloat16)

def reference(frames, conv_weight, down_weight, w_query, w_key, w_value, w_out, shot_lengths, scene_label, out_grad):
    padded = jnp.pad(frames, ((2, 0), (1, 1), (1, 1), (0, 0)))
    pre = conv_block(padded, conv_weight)
    act = (frames.astype(jnp.float32) + jax.nn.silu(pre)).astype(jnp.bfloat16)
    grouped = act.reshape(LAT, 8, H, W, C)
    latent = jnp.einsum('jkhwc,kcd->jhwd', grouped.astype(jnp.float32), down_weight.astype(jnp.float32)).astype(jnp.bfloat16)
    starts = (jnp.cumsum(shot_lengths) - shot_lengths).astype(jnp.int32)
    times = jnp.arange(LAT, dtype=jnp.int32)
    is_start = jnp.any(starts[None, :] == times[:, None], axis=1)
    begin = lax.optimization_barrier(jnp.max(jnp.where(starts[None, :] <= times[:, None], starts[None, :], 0), axis=1)).astype(jnp.int32)
    counts = (times - begin + 1).astype(jnp.float32)

    def advance(carry, inputs):
        frame_lat, flag = inputs
        fresh = jnp.where(flag, frame_lat.astype(jnp.float32), carry + frame_lat.astype(jnp.float32))
        return (fresh, fresh)
    _, shot_sum = lax.scan(advance, jnp.zeros((H, W, C), jnp.float32), (latent, is_start))
    mixed = (latent.astype(jnp.float32) + shot_sum / counts[:, None, None, None]).astype(jnp.bfloat16)
    block_count = LAT // LF
    tokens = mixed.reshape(block_count, LF * H * W, C)
    labels = scene_label[:, 0].reshape(block_count, LF)
    order = jnp.arange(LF, dtype=jnp.int32)

    def per_block(inputs):
        block_tok, block_lab = inputs
        same_frame = (block_lab[None, :] == block_lab[:, None]) & (order[None, :] <= order[:, None])
        allowed = jnp.repeat(jnp.repeat(same_frame, H * W, axis=0), H * W, axis=1)
        return attend_ref(block_tok, block_tok, allowed, w_query, w_key, w_value, w_out)
    latent_out = lax.map(per_block, (tokens, labels)).reshape(LAT, H, W, C)
    act_grad = (out_grad.astype(jnp.float32) * slope_of(pre)).astype(jnp.bfloat16)
    grad_pad = jnp.pad(act_grad, ((0, 2), (1, 1), (1, 1), (0, 0)))
    flipped = jnp.swapaxes(jnp.flip(conv_weight, (0, 1, 2)), 3, 4)
    frame_grad = (out_grad.astype(jnp.float32) + conv_block(grad_pad, flipped)).astype(jnp.bfloat16)
    return (latent_out, frame_grad)
```

```python
import math

import jax
import jax.numpy as jnp
from jax import lax
from jax.experimental import pallas as pl
from jax.experimental.pallas import tpu as pltpu
from jax.sharding import PartitionSpec as P

HEAD = 64
BF16 = jnp.bfloat16
F32 = jnp.float32
VMEM = pl.BlockSpec(memory_space=pltpu.VMEM)
SMEM = pl.BlockSpec(memory_space=pltpu.SMEM)
ANY = pl.BlockSpec(memory_space=pl.ANY)
NT = (((1,), (1,)), ((), ()))
NN = (((1,), (0,)), ((), ()))

TAPS = [(off, side) for side in (1, 0, 2) for off in (0, 2, 1)]


def dot(a, b, dims=NN):
    return lax.dot_general(a, b, dims, preferred_element_type=F32)


def weight_copies(weight_ref, folded, sems, taps):
    chans = weight_ref.shape[-1]
    copies = []
    for k, (shift_t, shift_w) in enumerate(taps):
        group = []
        for h_in in range(2):
            for h_out in range(2):
                group.append(
                    pltpu.make_async_copy(
                        weight_ref.at[shift_t, h_in - h_out + 1, shift_w],
                        folded.at[k, pl.ds(h_in * chans, chans), pl.ds(h_out * chans, chans)],
                        sems.at[k, 2 * h_in + h_out],
                    )
                )
        copies.append(group)
    return copies


def build_shifted(frame_of, low, high, even, odd):
    count = even.shape[1] // 8
    width = even.shape[2]
    sub = lax.broadcasted_iota(jnp.int32, (8, width), 0)
    before = None
    for t in range(count):
        own = frame_of(t).astype(F32)
        left = jnp.where(
            sub == 0, jnp.broadcast_to(low[t : t + 1, :], (8, width)), pltpu.roll(own, 1, 0)
        )
        right = jnp.where(
            sub == 7, jnp.broadcast_to(high[t : t + 1, :], (8, width)), pltpu.roll(own, 7, 0)
        )
        now = (left, own, right)
        if t % 2 == 1:
            for s in range(3):
                even[s, 8 * (t - 1) : 8 * (t + 1), :] = jnp.concatenate(
                    [before[s], now[s]], axis=0
                ).astype(BF16)
        elif t > 0:
            for s in range(3):
                odd[s, 8 * (t - 2) : 8 * t, :] = jnp.concatenate(
                    [before[s], now[s]], axis=0
                ).astype(BF16)
        before = now


def conv_taps(even, odd, folded, copies, total, dims):
    rows = total.shape[0]
    for k, (off, side) in enumerate(TAPS):
        for copy in copies[k]:
            copy.wait()
        if off == 1:
            lhs = odd[side, :, :]
        else:
            lhs = even[side, 8 * off : 8 * off + rows, :]
        part = dot(lhs, folded[k], dims)
        if k == 0:
            total[...] = part
        else:
            total[...] += part


def pick_sides(parity, from_core, from_chip, low, high):
    core = from_core[...].astype(F32)
    chip = from_chip[...].astype(F32)
    even_core = parity == 0
    low[0 : core.shape[0], :] = jnp.where(even_core, chip, core)
    high[0 : core.shape[0], :] = jnp.where(even_core, core, chip)


def forward_kernel(
    place,
    lengths,
    frames,
    rim,
    from_core,
    from_chip,
    out_grad,
    weight,
    down,
    latent_out,
    sums_out,
    tail_out,
    grad_out,
    core_out,
    chip_out,
    block,
    grad_block,
    down_block,
    low,
    high,
    even,
    odd,
    folded,
    total,
    act,
    sems,
    weight_sems,
):
    chans = frames.shape[-1]
    count = frames.shape[0]
    first = [
        pltpu.make_async_copy(
            frames.at[:, h], block.at[:, :, pl.ds(h * chans, chans)], sems.at[h]
        )
        for h in range(2)
    ]
    for copy in first:
        copy.start()
    copies = weight_copies(weight, folded, weight_sems, TAPS)
    for copy in copies[0]:
        copy.start()
    later = [
        pltpu.make_async_copy(
            out_grad.at[:, h], grad_block.at[:, :, pl.ds(h * chans, chans)], sems.at[2 + h]
        )
        for h in range(2)
    ] + [pltpu.make_async_copy(down, down_block, sems.at[4])]
    for group in copies[1:]:
        for copy in group:
            copy.start()
    for copy in later:
        copy.start()
    parity = place[1]
    pick_sides(parity, from_core, from_chip, low, high)
    for copy in first:
        copy.wait()

    def frame_of(t):
        if t < 2:
            return rim[t]
        return block[t - 2]

    build_shifted(frame_of, low, high, even, odd)
    conv_taps(even, odd, folded, copies, total, NN)
    for copy in later:
        copy.wait()

    for j in range(count // 8):
        rows = slice(64 * j, 64 * (j + 1))
        pre = total[rows, :]
        gate = 1.0 / (1.0 + jnp.exp(-pre))
        own = block[8 * j : 8 * (j + 1)].astype(F32)
        act[j] = own + (pre * gate).reshape(own.shape)
        slope = gate * (1.0 + pre * (1.0 - gate))
        grad = grad_block[8 * j : 8 * (j + 1)].astype(F32) * slope.reshape(own.shape)
        grad_out[8 * j : 8 * (j + 1)] = grad.astype(BF16)
        first_col = grad[:, 0, :]
        last_col = grad[:, 7, :]
        core_out[8 * j : 8 * (j + 1), :] = jnp.where(parity == 0, last_col, first_col)
        chip_out[8 * j : 8 * (j + 1), :] = jnp.where(parity == 0, first_col, last_col)

    latent = jnp.zeros((2 * count, chans), F32)
    for k in range(8):
        lhs = jnp.concatenate(
            [
                act[:, k, :, h * chans : (h + 1) * chans].reshape(count, chans)
                for h in range(2)
            ],
            axis=0,
        ).astype(BF16)
        latent = latent + dot(lhs, down_block[k])
    latent = latent.astype(BF16).astype(F32)
    rounded = [
        jnp.concatenate([latent[8 * j : 8 * j + 8], latent[count + 8 * j : count + 8 * j + 8]], 0)
        for j in range(count // 8)
    ]
    running = jnp.zeros_like(rounded[0])
    for j in range(count // 8):
        now = place[0] * (count // 8) + j
        start = jnp.int32(0)
        begins = jnp.int32(0)
        for k in range(lengths.shape[0]):
            begins = jnp.where(start == now, 1, begins)
            start = start + lengths[k]
        running = jnp.where(begins > 0, rounded[j], running + rounded[j])
        sums_out[j] = running
        latent_out[j] = rounded[j]
    tail_out[...] = running


def forward(place, lengths, frames, rim, from_core, from_chip, out_grad, weight, down):
    count, _, cols, chans = frames.shape
    rows, wide = count * cols, 2 * chans
    lat = count // 8
    return pl.pallas_call(
        forward_kernel,
        out_shape=(
            jax.ShapeDtypeStruct((lat, 16, chans), F32),
            jax.ShapeDtypeStruct((lat, 16, chans), F32),
            jax.ShapeDtypeStruct((16, chans), F32),
            jax.ShapeDtypeStruct((count, cols, wide), BF16),
            jax.ShapeDtypeStruct((count, wide), F32),
            jax.ShapeDtypeStruct((count, wide), F32),
        ),
        in_specs=[SMEM, SMEM, ANY, VMEM, VMEM, VMEM, ANY, ANY, ANY],
        out_specs=[VMEM] * 6,
        scratch_shapes=[
            pltpu.VMEM((count, cols, wide), BF16),
            pltpu.VMEM((count, cols, wide), BF16),
            pltpu.VMEM(down.shape, BF16),
            pltpu.VMEM((count + 8, wide), F32),
            pltpu.VMEM((count + 8, wide), F32),
            pltpu.VMEM((3, rows + 16, wide), BF16),
            pltpu.VMEM((3, rows, wide), BF16),
            pltpu.VMEM((9, wide, wide), BF16),
            pltpu.VMEM((rows, wide), F32),
            pltpu.VMEM((lat, 8, cols, wide), F32),
            pltpu.SemaphoreType.DMA((5,)),
            pltpu.SemaphoreType.DMA((9, 4)),
        ],
        compiler_params=pltpu.CompilerParams(vmem_limit_bytes=48 * 2**20),
        cost_estimate=pl.CostEstimate(
            flops=2 * 9 * rows * wide * wide, bytes_accessed=16 * 2**20, transcendentals=rows * wide
        ),
        name="forward",
    )(place, lengths, frames, rim, from_core, from_chip, out_grad, weight, down)


def backward_kernel(
    place,
    grad,
    rim,
    from_core,
    from_chip,
    out_grad,
    weight,
    result,
    low,
    high,
    even,
    odd,
    folded,
    total,
    weight_sems,
):
    count, _, cols, chans = out_grad.shape
    copies = weight_copies(
        weight, folded, weight_sems, [(2 - off, 2 - side) for off, side in TAPS]
    )
    for group in copies:
        for copy in group:
            copy.start()
    pick_sides(place[1], from_core, from_chip, low, high)

    def frame_of(t):
        if t >= count:
            return rim[t - count]
        return grad[t]

    build_shifted(frame_of, low, high, even, odd)
    conv_taps(even, odd, folded, copies, total, NT)
    for j in range(count // 8):
        part = total[64 * j : 64 * (j + 1), :]
        for h in range(2):
            mine = part[:, h * chans : (h + 1) * chans].reshape(8, cols, chans)
            result[8 * j : 8 * (j + 1), h] = (
                out_grad[8 * j : 8 * (j + 1), h].astype(F32) + mine
            ).astype(BF16)


def backward(place, grad, rim, from_core, from_chip, out_grad, weight):
    count, _, cols, chans = out_grad.shape
    rows, wide = count * cols, 2 * chans
    return pl.pallas_call(
        backward_kernel,
        out_shape=jax.ShapeDtypeStruct(out_grad.shape, BF16),
        in_specs=[SMEM, VMEM, VMEM, VMEM, VMEM, VMEM, ANY],
        out_specs=VMEM,
        scratch_shapes=[
            pltpu.VMEM((count + 8, wide), F32),
            pltpu.VMEM((count + 8, wide), F32),
            pltpu.VMEM((3, rows + 16, wide), BF16),
            pltpu.VMEM((3, rows, wide), BF16),
            pltpu.VMEM((9, wide, wide), BF16),
            pltpu.VMEM((rows, wide), F32),
            pltpu.SemaphoreType.DMA((9, 4)),
        ],
        compiler_params=pltpu.CompilerParams(vmem_limit_bytes=40 * 2**20),
        cost_estimate=pl.CostEstimate(
            flops=2 * 9 * rows * wide * wide, bytes_accessed=12 * 2**20, transcendentals=0
        ),
        name="backward",
    )(place, grad, rim, from_core, from_chip, out_grad, weight)


def mix_kernel(place, lengths, latent, sums, tails, mixed):
    lat = latent.shape[0]
    peers = tails.shape[0]
    me = place[0]
    starts = [jnp.int32(0)]
    for k in range(lengths.shape[0] - 1):
        starts.append(starts[-1] + lengths[k])
    opened = jnp.int32(0)
    for start in starts:
        opened = jnp.where(start < me * lat, jnp.maximum(start, opened), opened)
    carried = jnp.zeros(latent.shape[1:], F32)
    for k in range(peers):
        counts = jnp.logical_and(k < me, (k + 1) * lat > opened)
        carried = carried + jnp.where(counts, tails[k], 0.0)
    for j in range(lat):
        now = me * lat + j
        begin = jnp.int32(0)
        for start in starts:
            begin = jnp.where(start <= now, jnp.maximum(start, begin), begin)
        shot = sums[j] + jnp.where(begin < me * lat, carried, 0.0)
        length = jnp.full(shot.shape, now - begin + 1, jnp.int32).astype(F32)
        mixed[16 * j : 16 * (j + 1), :] = (latent[j] + shot / length).astype(BF16)


def mix(place, lengths, latent, sums, tails):
    return pl.pallas_call(
        mix_kernel,
        out_shape=jax.ShapeDtypeStruct((latent.shape[0] * 16, latent.shape[2]), BF16),
        in_specs=[SMEM, SMEM, VMEM, VMEM, VMEM],
        out_specs=VMEM,
        name="mix",
    )(place, lengths, latent, sums, tails)


def attend_kernel(labels, mine, *refs):
    pieces, (w_query, w_key, w_value, w_out, result, keys, values) = refs[:-7], refs[-7:]
    tokens, chans = mine.shape
    lat = labels.shape[0]
    per = tokens // lat
    at = 0
    for piece in pieces:
        block = piece[...]
        size = block.shape[0]
        keys[at : at + size, :] = dot(block, w_key[...]).astype(BF16)
        values[at : at + size, :] = dot(block, w_value[...]).astype(BF16)
        at += size
    query = (dot(mine[...], w_query[...]).astype(BF16) * BF16(1.0 / math.sqrt(HEAD))).astype(BF16)
    row = lax.broadcasted_iota(jnp.int32, (tokens, 1), 0) // per
    col = (lax.broadcasted_iota(jnp.int32, (1, tokens), 1) % tokens) // per
    row_label = jnp.zeros((tokens, 1), jnp.int32)
    col_label = jnp.zeros((1, tokens), jnp.int32)
    for j in range(lat):
        row_label = jnp.where(row == j, labels[j, 0], row_label)
        col_label = jnp.where(col == j, labels[j, 0], col_label)
    same = jnp.logical_and(row_label == col_label, col <= row)
    bias = jnp.where(same, 0.0, -1e30).astype(F32)
    bias = jnp.concatenate([bias] * (at // tokens), axis=1)
    outs = []
    for head in range(chans // HEAD):
        lanes = slice(head * HEAD, (head + 1) * HEAD)
        scores = dot(query[:, lanes], keys[:, lanes], NT) + bias
        top = jnp.max(scores, axis=1, keepdims=True)
        expo = jnp.exp(scores - top)
        norm = jnp.sum(expo, axis=1, keepdims=True)
        outs.append(dot(expo.astype(BF16), values[:, lanes]) / norm)
    heads = jnp.concatenate(outs, axis=1).astype(BF16)
    final = mine[...].astype(F32) + dot(heads, w_out[...])
    for j in range(lat):
        for h in range(2):
            at = per * j + 8 * h
            result[j, h] = final[at : at + 8].astype(BF16)


def attend(labels, mine, pieces, w_query, w_key, w_value, w_out):
    tokens, chans = mine.shape
    total = sum(piece.shape[0] for piece in pieces)
    return pl.pallas_call(
        attend_kernel,
        out_shape=jax.ShapeDtypeStruct((labels.shape[0], 2, 8, chans), BF16),
        in_specs=[SMEM] + [VMEM] * (5 + len(pieces)),
        out_specs=VMEM,
        scratch_shapes=[pltpu.VMEM((total, chans), BF16), pltpu.VMEM((total, chans), BF16)],
        compiler_params=pltpu.CompilerParams(vmem_limit_bytes=32 * 2**20),
        name="attend",
    )(labels, mine, *pieces, w_query, w_key, w_value, w_out)


def shifted(value, axis, steps):
    count = lax.axis_size(axis)
    return lax.ppermute(
        value, axis, [(i, i + steps) for i in range(count) if 0 <= i + steps < count]
    )


def with_core(value):
    count = lax.axis_size("scene")
    return lax.ppermute(value, "scene", [(i, i ^ 1) for i in range(count)])


def with_chip(value):
    count = lax.axis_size("scene")
    pairs = [(i, i + 1) for i in range(1, count - 1, 2)]
    return lax.ppermute(value, "scene", pairs + [(b, a) for a, b in pairs])


def gathered(value):
    count = lax.axis_size("scene")
    chips = [
        lax.ppermute(value, "scene", [(i, (i + 2 * k) % count) for i in range(count)])
        for k in range(1, count // 2)
    ]
    own = jnp.concatenate([value, *chips], axis=0)
    return [own, with_core(own)]


def per_device(
    frames,
    conv_weight,
    down_weight,
    w_query,
    w_key,
    w_value,
    w_out,
    shot_lengths,
    scene_label,
    out_grad,
):
    count, _, cols, chans = frames.shape
    parity = lax.axis_index("scene") % 2
    place = jnp.stack([lax.axis_index("tm"), parity]).astype(jnp.int32)

    def columns(at, top):
        cut = lax.dynamic_slice_in_dim(frames, at, 1, axis=2).reshape(count, 2 * chans)
        rim_cut = lax.dynamic_slice_in_dim(top, at, 1, axis=1).reshape(2, 2 * chans)
        return jnp.concatenate([rim_cut, cut], axis=0)

    rim = shifted(frames[count - 2 :], "tm", 1)
    rim = jnp.swapaxes(rim, 1, 2).reshape(2, cols, 2 * chans)
    inner = (cols - 1) * (1 - parity)
    from_core = with_core(columns(inner, rim))
    from_chip = with_chip(columns(cols - 1 - inner, rim))
    latent, sums, tail, grad, core_cols, chip_cols = forward(
        place, shot_lengths, frames, rim, from_core, from_chip, out_grad, conv_weight, down_weight
    )

    peers = lax.axis_size("tm")
    tails = lax.all_to_all(
        jnp.broadcast_to(tail[None], (peers, *tail.shape)), "tm", 0, 0, tiled=True
    )
    mixed = mix(place, shot_lengths, latent, sums, tails)
    pieces = gathered(mixed)
    latent_out = attend(scene_label, mixed, pieces, w_query, w_key, w_value, w_out)

    rim_after = shifted(grad[:2], "tm", -1)

    def extended(own, at):
        corner = lax.dynamic_slice_in_dim(rim_after, at, 1, axis=1).reshape(2, 2 * chans)
        return jnp.concatenate([own.astype(BF16), corner], axis=0)

    grad_core = with_core(extended(core_cols, inner))
    grad_chip = with_chip(extended(chip_cols, cols - 1 - inner))
    frame_grad = backward(place, grad, rim_after, grad_core, grad_chip, out_grad, conv_weight)
    return (latent_out, frame_grad)


def solution(mesh):
    in_specs = (
        P("tm", None, "scene", None),
        P(),
        P(),
        P(),
        P(),
        P(),
        P(),
        P(),
        P("tm", None),
        P("tm", None, "scene", None),
    )
    out_specs = (P("tm", None, "scene", None), P("tm", None, "scene", None))
    return jax.shard_map(
        per_device, mesh=mesh, in_specs=in_specs, out_specs=out_specs, check_vma=False
    )
```

```python
import math

import jax
import jax.numpy as jnp
from jax import lax
from jax.experimental import pallas as pl
from jax.experimental.pallas import tpu as pltpu
from jax.sharding import PartitionSpec as P

HEAD = 64
BF16 = jnp.bfloat16
F32 = jnp.float32
VMEM = pl.BlockSpec(memory_space=pltpu.VMEM)
SMEM = pl.BlockSpec(memory_space=pltpu.SMEM)
ANY = pl.BlockSpec(memory_space=pl.ANY)
NT = (((1,), (1,)), ((), ()))
NN = (((1,), (0,)), ((), ()))

SIDES = (1, 0, 2)


def dot(a, b, dims=NN):
    return lax.dot_general(a, b, dims, preferred_element_type=F32)


def weight_copies(weight_ref, folded, sems, back):
    chans = weight_ref.shape[-1]
    copies = []
    for k, side in enumerate(SIDES):
        for off in range(3):
            for h_in in range(2):
                for h_out in range(2):
                    row, col = h_in * chans, h_out * chans
                    if back:
                        col += 2 * chans * off
                    else:
                        row += 2 * chans * off
                    copies.append(
                        pltpu.make_async_copy(
                            weight_ref.at[
                                2 - off if back else off,
                                h_in - h_out + 1,
                                2 - side if back else side,
                            ],
                            folded.at[k, pl.ds(row, chans), pl.ds(col, chans)],
                            sems.at[k, 4 * off + 2 * h_in + h_out],
                        )
                    )
    return [copies[12 * k : 12 * (k + 1)] for k in range(3)]


def store_pairs(values_of, sides, count, even, odd):
    before = None
    for t in range(count):
        now = values_of(t)
        for at, s in enumerate(sides):
            if t % 2 == 1:
                pair = jnp.concatenate([before[at], now[at]], axis=0).astype(BF16)
                even[s, 8 * (t - 1) : 8 * (t + 1), :] = pair
            elif t > 0:
                pair = jnp.concatenate([before[at], now[at]], axis=0).astype(BF16)
                odd[s, 8 * (t - 2) : 8 * t, :] = pair
        before = now


def build_centre(frame_of, count, even, odd):
    store_pairs(lambda t: (frame_of(t).astype(F32),), (1,), count, even, odd)


def build_sides(frame_of, low_of, high_of, count, even, odd):
    width = even.shape[2]
    sub = lax.broadcasted_iota(jnp.int32, (8, width), 0)

    def both(t):
        own = frame_of(t).astype(F32)
        left = jnp.where(sub == 0, jnp.broadcast_to(low_of(t), (8, width)), pltpu.roll(own, 1, 0))
        right = jnp.where(sub == 7, jnp.broadcast_to(high_of(t), (8, width)), pltpu.roll(own, 7, 0))
        return left, right

    store_pairs(both, (0, 2), count, even, odd)


def window(side, even, odd, rows, extra=None):
    parts = [even[side, 0:rows, :], odd[side, 0:rows, :], even[side, 16 : 16 + rows, :]]
    if extra is not None:
        parts = [jnp.concatenate([part, extra(side, off)], axis=0) for off, part in enumerate(parts)]
    return jnp.concatenate(parts, axis=1)


def pack_kernel(place, frames, out_grad, before, after, core_out, chip_out, wide_f, wide_g):
    count = frames.shape[0]
    chans = frames.shape[3]
    lanes = chans // 128
    for t in range(count + 4):
        for h in range(2):
            if t < 2:
                value = before[t, h]
            elif t < count + 2:
                value = frames[t - 2, h]
            else:
                value = after[t - count - 2, h]
            value = value.astype(F32)
            for k in range(lanes):
                wide_f[lanes * h + k, 8 * t : 8 * (t + 1), :] = value[:, 128 * k : 128 * (k + 1)]
    for t in range(count + 2):
        for h in range(2):
            value = (out_grad[t, h] if t < count else after[t - count + 2, h]).astype(F32)
            for k in range(lanes):
                wide_g[lanes * h + k, 8 * t : 8 * (t + 1), :] = value[:, 128 * k : 128 * (k + 1)]
    even_core = place[1] == 0

    def column(source, at, rows):
        return jnp.concatenate(
            [source[k, pl.ds(at, rows, 8), :] for k in range(2 * lanes)], axis=1
        )

    def packed(first, second, grad):
        return jnp.concatenate(
            [
                column(wide_f, first, count + 4),
                column(wide_f, second, count + 4),
                column(wide_g, grad, count + 2),
                jnp.zeros((6, 2 * chans), F32),
            ],
            axis=0,
        )

    left = packed(0, 1, 0)
    right = packed(6, 7, 7)
    core_out[...] = jnp.where(even_core, right, left).astype(BF16)
    chip_out[...] = jnp.where(even_core, left, right).astype(BF16)


def pack(place, frames, out_grad, before, after):
    count, _, cols, chans = frames.shape
    rows = 3 * count + 16
    return pl.pallas_call(
        pack_kernel,
        out_shape=[jax.ShapeDtypeStruct((rows, 2 * chans), BF16)] * 2,
        in_specs=[SMEM] + [VMEM] * 4,
        out_specs=[VMEM] * 2,
        scratch_shapes=[
            pltpu.VMEM((2 * chans // 128, cols * (count + 4), 128), F32),
            pltpu.VMEM((2 * chans // 128, cols * (count + 2), 128), F32),
        ],
        compiler_params=pltpu.CompilerParams(vmem_limit_bytes=56 * 2**20),
        name="pack",
    )(place, frames, out_grad, before, after)


def forward_kernel(
    place,
    lengths,
    frames,
    before,
    after,
    core_sent,
    chip_sent,
    core_got,
    chip_got,
    out_grad,
    weight,
    down,
    latent_out,
    sums_out,
    tail_out,
    low_out,
    high_out,
    grad_out,
    block,
    grad_block,
    grad_done,
    down_block,
    own_low,
    own_high,
    low,
    high,
    even,
    odd,
    folded,
    total,
    act,
    sems,
    weight_sems,
):
    chans = frames.shape[-1]
    count = frames.shape[0]
    ahead = count + 2
    rows = 8 * ahead
    first = [
        pltpu.make_async_copy(frames.at[:, h], block.at[:, :, pl.ds(h * chans, chans)], sems.at[h])
        for h in range(2)
    ]
    for copy in first:
        copy.start()
    copies = weight_copies(weight, folded, weight_sems, False)
    for copy in copies[0]:
        copy.start()
    later = [
        pltpu.make_async_copy(
            out_grad.at[:, h], grad_block.at[:, :, pl.ds(h * chans, chans)], sems.at[2 + h]
        )
        for h in range(2)
    ] + [pltpu.make_async_copy(down, down_block, sems.at[4])]
    for group in copies[1:]:
        for copy in group:
            copy.start()
    for copy in later:
        copy.start()
    even_core = place[1] == 0

    def pick(core, chip, at_low, at_high):
        core, chip = core[...].astype(F32), chip[...].astype(F32)
        at_low[...] = jnp.where(even_core, chip, core)
        at_high[...] = jnp.where(even_core, core, chip)

    pick(core_sent, chip_sent, own_low, own_high)
    pick(core_got, chip_got, low, high)
    for copy in first:
        copy.wait()

    def frame_of(t):
        if 2 <= t < count + 2:
            return block[t - 2]
        part = (lambda h: before[t, h]) if t < 2 else (lambda h: after[t - count - 2, h])
        return jnp.concatenate([part(0).astype(F32), part(1).astype(F32)], axis=1)

    span = count + 4

    def rim(side, off):
        left = ((low, 0), (low, span), (own_low, 0))[side]
        right = ((own_high, span), (high, 0), (high, span))[side]
        return jnp.concatenate(
            [ref[at + off : at + off + ahead + 6, :] for ref, at in (left, right)], axis=0
        ).astype(BF16)

    build_centre(frame_of, span, even, odd)
    for copy in copies[0]:
        copy.wait()
    total[...] = dot(window(1, even, odd, rows, rim), folded[0])
    build_sides(
        frame_of,
        lambda t: low[span + t : span + t + 1, :],
        lambda t: high[t : t + 1, :],
        span,
        even,
        odd,
    )
    for k in (1, 2):
        for copy in copies[k]:
            copy.wait()
        total[...] += dot(window(SIDES[k], even, odd, rows, rim), folded[k])
    for copy in later:
        copy.wait()

    def gates(pre):
        gate = 1.0 / (1.0 + jnp.exp(-pre))
        return gate, gate * (1.0 + pre * (1.0 - gate))

    for j in range(count // 8):
        pre = total[64 * j : 64 * (j + 1), :]
        gate, slope = gates(pre)
        own = block[8 * j : 8 * (j + 1)].astype(F32)
        act[j] = own + (pre * gate).reshape(own.shape)
        grad = grad_block[8 * j : 8 * (j + 1)].astype(F32) * slope.reshape(own.shape)
        grad_done[8 * j : 8 * (j + 1)] = grad.astype(BF16)
    for t in range(2):
        at = 8 * (count + t)
        _, slope = gates(total[at : at + 8, :])
        grad = jnp.concatenate([after[2 + t, 0].astype(F32), after[2 + t, 1].astype(F32)], axis=1)
        grad_done[count + t] = (grad * slope).astype(BF16)
    write = pltpu.make_async_copy(grad_done, grad_out, sems.at[5])
    write.start()
    for at, (source, target) in enumerate(((low, low_out), (high, high_out))):
        base = rows + at * (ahead + 6)
        _, slope = gates(total[base : base + ahead + 6, :])
        target[...] = slope * source[2 * span : 2 * span + ahead + 6, :]

    latent = jnp.zeros((2 * count, chans), F32)
    for k in range(8):
        lhs = jnp.concatenate(
            [
                act[:, k, :, h * chans : (h + 1) * chans].reshape(count, chans)
                for h in range(2)
            ],
            axis=0,
        ).astype(BF16)
        latent = latent + dot(lhs, down_block[k])
    latent = latent.astype(BF16).astype(F32)
    rounded = [
        jnp.concatenate([latent[8 * j : 8 * j + 8], latent[count + 8 * j : count + 8 * j + 8]], 0)
        for j in range(count // 8)
    ]
    running = jnp.zeros_like(rounded[0])
    for j in range(count // 8):
        now = place[0] * (count // 8) + j
        start = jnp.int32(0)
        begins = jnp.int32(0)
        for k in range(lengths.shape[0]):
            begins = jnp.where(start == now, 1, begins)
            start = start + lengths[k]
        running = jnp.where(begins > 0, rounded[j], running + rounded[j])
        sums_out[j] = running
        latent_out[j] = rounded[j]
    for k in range(tail_out.shape[0]):
        tail_out[k] = running
    write.wait()


def forward(peers, place, lengths, frames, before, after, columns, out_grad, weight, down):
    count, _, cols, chans = frames.shape
    wide = 2 * chans
    lat = count // 8
    ahead = count + 2
    rows = cols * ahead
    received = columns[0].shape
    return pl.pallas_call(
        forward_kernel,
        out_shape=(
            jax.ShapeDtypeStruct((lat, 16, chans), F32),
            jax.ShapeDtypeStruct((lat, 16, chans), F32),
            jax.ShapeDtypeStruct((peers, 16, chans), F32),
            jax.ShapeDtypeStruct((ahead + 6, wide), F32),
            jax.ShapeDtypeStruct((ahead + 6, wide), F32),
            jax.ShapeDtypeStruct((ahead, cols, wide), BF16),
        ),
        in_specs=[SMEM, SMEM, ANY] + [VMEM] * 6 + [ANY] * 3,
        out_specs=[VMEM] * 5 + [ANY],
        scratch_shapes=[
            pltpu.VMEM((count, cols, wide), BF16),
            pltpu.VMEM((count, cols, wide), BF16),
            pltpu.VMEM((ahead, cols, wide), BF16),
            pltpu.VMEM(down.shape, BF16),
            pltpu.VMEM(received, F32),
            pltpu.VMEM(received, F32),
            pltpu.VMEM(received, F32),
            pltpu.VMEM(received, F32),
            pltpu.VMEM((3, rows + 16, wide), BF16),
            pltpu.VMEM((3, rows, wide), BF16),
            pltpu.VMEM((3, 3 * wide, wide), BF16),
            pltpu.VMEM((rows + 2 * (ahead + 6), wide), F32),
            pltpu.VMEM((lat, 8, cols, wide), F32),
            pltpu.SemaphoreType.DMA((6,)),
            pltpu.SemaphoreType.DMA((3, 12)),
        ],
        compiler_params=pltpu.CompilerParams(vmem_limit_bytes=60 * 2**20),
        cost_estimate=pl.CostEstimate(
            flops=2 * 9 * rows * wide * wide, bytes_accessed=16 * 2**20, transcendentals=rows * wide
        ),
        name="forward",
    )(place, lengths, frames, before, after, *columns, out_grad, weight, down)


def backward_kernel(
    grad,
    low,
    high,
    out_grad,
    weight,
    result,
    block,
    source,
    done,
    even,
    odd,
    folded,
    total,
    sems,
    weight_sems,
):
    count, _, cols, chans = out_grad.shape
    first = pltpu.make_async_copy(grad, block, sems.at[0])
    first.start()
    copies = weight_copies(weight, folded, weight_sems, True)
    for group in copies:
        for copy in group:
            copy.start()
    later = pltpu.make_async_copy(out_grad, source, sems.at[1])
    later.start()
    first.wait()

    def frame_of(t):
        return block[t]

    rows = 8 * count
    build_centre(frame_of, count + 2, even, odd)
    for copy in copies[0]:
        copy.wait()
    total[...] = dot(window(1, even, odd, rows), folded[0], NT)
    build_sides(
        frame_of,
        lambda t: low[t : t + 1, :],
        lambda t: high[t : t + 1, :],
        count + 2,
        even,
        odd,
    )
    for copy in copies[1]:
        copy.wait()
    total[...] += dot(window(SIDES[1], even, odd, rows), folded[1], NT)
    for copy in copies[2]:
        copy.wait()
    later.wait()
    writes = []
    step = count // 4
    for j in range(4):
        at = slice(8 * step * j, 8 * step * (j + 1))
        lhs = jnp.concatenate(
            [
                even[2, 8 * step * j : 8 * step * (j + 1), :],
                odd[2, 8 * step * j : 8 * step * (j + 1), :],
                even[2, 16 + 8 * step * j : 16 + 8 * step * (j + 1), :],
            ],
            axis=1,
        )
        part = total[at, :] + dot(lhs, folded[2], NT)
        for h in range(2):
            mine = part[:, h * chans : (h + 1) * chans].reshape(step, cols, chans)
            done[step * j : step * (j + 1), h] = (
                source[step * j : step * (j + 1), h].astype(F32) + mine
            ).astype(BF16)
        write = pltpu.make_async_copy(
            done.at[pl.ds(step * j, step)], result.at[pl.ds(step * j, step)], sems.at[2 + j]
        )
        write.start()
        writes.append(write)
    for write in writes:
        write.wait()


def backward(grad, low, high, out_grad, weight):
    count, _, cols, chans = out_grad.shape
    rows, wide = count * cols, 2 * chans
    return pl.pallas_call(
        backward_kernel,
        out_shape=jax.ShapeDtypeStruct(out_grad.shape, BF16),
        in_specs=[ANY, VMEM, VMEM, ANY, ANY],
        out_specs=ANY,
        scratch_shapes=[
            pltpu.VMEM(grad.shape, BF16),
            pltpu.VMEM(out_grad.shape, BF16),
            pltpu.VMEM(out_grad.shape, BF16),
            pltpu.VMEM((3, rows + 16, wide), BF16),
            pltpu.VMEM((3, rows, wide), BF16),
            pltpu.VMEM((3, wide, 3 * wide), BF16),
            pltpu.VMEM((rows, wide), F32),
            pltpu.SemaphoreType.DMA((6,)),
            pltpu.SemaphoreType.DMA((3, 12)),
        ],
        compiler_params=pltpu.CompilerParams(vmem_limit_bytes=60 * 2**20),
        cost_estimate=pl.CostEstimate(
            flops=2 * 9 * rows * wide * wide, bytes_accessed=12 * 2**20, transcendentals=0
        ),
        name="backward",
    )(grad, low, high, out_grad, weight)


def mix_kernel(place, lengths, latent, sums, tails, mixed):
    lat = latent.shape[0]
    peers = tails.shape[0]
    me = place[0]
    starts = [jnp.int32(0)]
    for k in range(lengths.shape[0] - 1):
        starts.append(starts[-1] + lengths[k])
    opened = jnp.int32(0)
    for start in starts:
        opened = jnp.where(start < me * lat, jnp.maximum(start, opened), opened)
    carried = jnp.zeros(latent.shape[1:], F32)
    for k in range(peers):
        counts = jnp.logical_and(k < me, (k + 1) * lat > opened)
        carried = carried + jnp.where(counts, tails[k], 0.0)
    for j in range(lat):
        now = me * lat + j
        begin = jnp.int32(0)
        for start in starts:
            begin = jnp.where(start <= now, jnp.maximum(start, begin), begin)
        shot = sums[j] + jnp.where(begin < me * lat, carried, 0.0)
        length = jnp.full(shot.shape, now - begin + 1, jnp.int32).astype(F32)
        mixed[16 * j : 16 * (j + 1), :] = (latent[j] + shot / length).astype(BF16)


def mix(place, lengths, latent, sums, tails):
    return pl.pallas_call(
        mix_kernel,
        out_shape=jax.ShapeDtypeStruct((latent.shape[0] * 16, latent.shape[2]), BF16),
        in_specs=[SMEM, SMEM, VMEM, VMEM, VMEM],
        out_specs=VMEM,
        name="mix",
    )(place, lengths, latent, sums, tails)


def attend_kernel(labels, mine, *refs):
    pieces, (w_query, w_key, w_value, w_out, result, keys, values) = refs[:-7], refs[-7:]
    tokens, chans = mine.shape
    lat = labels.shape[0]
    per = tokens // lat
    at = 0
    for piece in pieces:
        block = piece[...]
        size = block.shape[0]
        keys[at : at + size, :] = dot(block, w_key[...]).astype(BF16)
        values[at : at + size, :] = dot(block, w_value[...]).astype(BF16)
        at += size
    query = (dot(mine[...], w_query[...]).astype(BF16) * BF16(1.0 / math.sqrt(HEAD))).astype(BF16)
    row = lax.broadcasted_iota(jnp.int32, (tokens, 1), 0) // per
    col = (lax.broadcasted_iota(jnp.int32, (1, tokens), 1) % tokens) // per
    row_label = jnp.zeros((tokens, 1), jnp.int32)
    col_label = jnp.zeros((1, tokens), jnp.int32)
    for j in range(lat):
        row_label = jnp.where(row == j, labels[j, 0], row_label)
        col_label = jnp.where(col == j, labels[j, 0], col_label)
    same = jnp.logical_and(row_label == col_label, col <= row)
    bias = jnp.where(same, 0.0, -1e30).astype(F32)
    bias = jnp.concatenate([bias] * (at // tokens), axis=1)
    outs = []
    for head in range(chans // HEAD):
        lanes = slice(head * HEAD, (head + 1) * HEAD)
        scores = dot(query[:, lanes], keys[:, lanes], NT) + bias
        top = jnp.max(scores, axis=1, keepdims=True)
        expo = jnp.exp(scores - top)
        norm = jnp.sum(expo, axis=1, keepdims=True)
        outs.append(dot(expo.astype(BF16), values[:, lanes]) / norm)
    heads = jnp.concatenate(outs, axis=1).astype(BF16)
    final = mine[...].astype(F32) + dot(heads, w_out[...])
    for j in range(lat):
        for h in range(2):
            at = per * j + 8 * h
            result[j, h] = final[at : at + 8].astype(BF16)


def attend(labels, mine, pieces, w_query, w_key, w_value, w_out):
    tokens, chans = mine.shape
    total = sum(piece.shape[0] for piece in pieces)
    return pl.pallas_call(
        attend_kernel,
        out_shape=jax.ShapeDtypeStruct((labels.shape[0], 2, 8, chans), BF16),
        in_specs=[SMEM] + [VMEM] * (5 + len(pieces)),
        out_specs=VMEM,
        scratch_shapes=[pltpu.VMEM((total, chans), BF16), pltpu.VMEM((total, chans), BF16)],
        compiler_params=pltpu.CompilerParams(vmem_limit_bytes=32 * 2**20),
        name="attend",
    )(labels, mine, *pieces, w_query, w_key, w_value, w_out)


def shifted(value, axis, steps):
    count = lax.axis_size(axis)
    return lax.ppermute(
        value, axis, [(i, i + steps) for i in range(count) if 0 <= i + steps < count]
    )


def with_core(value):
    count = lax.axis_size("scene")
    return lax.ppermute(value, "scene", [(i, i ^ 1) for i in range(count)])


def with_chip(value):
    count = lax.axis_size("scene")
    pairs = [(i, i + 1) for i in range(1, count - 1, 2)]
    return lax.ppermute(value, "scene", pairs + [(b, a) for a, b in pairs])


def gathered(value):
    count = lax.axis_size("scene")
    chips = [
        lax.ppermute(value, "scene", [(i, (i + 2 * k) % count) for i in range(count)])
        for k in range(1, count // 2)
    ]
    own = jnp.concatenate([value, *chips], axis=0)
    return [own, with_core(own)]


def per_device(
    frames,
    conv_weight,
    down_weight,
    w_query,
    w_key,
    w_value,
    w_out,
    shot_lengths,
    scene_label,
    out_grad,
):
    count = frames.shape[0]
    place = jnp.stack([lax.axis_index("tm"), lax.axis_index("scene") % 2]).astype(jnp.int32)
    before = shifted(frames[count - 2 :], "tm", 1)
    after = shifted(jnp.concatenate([frames[:2], out_grad[:2]], axis=0), "tm", -1)
    sent = pack(place, frames, out_grad, before, after)
    columns = (*sent, with_core(sent[0]), with_chip(sent[1]))
    latent, sums, tail, low, high, grad = forward(
        lax.axis_size("tm"),
        place,
        shot_lengths,
        frames,
        before,
        after,
        columns,
        out_grad,
        conv_weight,
        down_weight,
    )
    tails = lax.all_to_all(tail, "tm", 0, 0, tiled=True)
    mixed = mix(place, shot_lengths, latent, sums, tails)
    pieces = gathered(mixed)
    frame_grad = backward(grad, low, high, out_grad, conv_weight)
    latent_out = attend(scene_label, mixed, pieces, w_query, w_key, w_value, w_out)
    return (latent_out, frame_grad)


def solution(mesh):
    in_specs = (
        P("tm", None, "scene", None),
        P(),
        P(),
        P(),
        P(),
        P(),
        P(),
        P(),
        P("tm", None),
        P("tm", None, "scene", None),
    )
    out_specs = (P("tm", None, "scene", None), P("tm", None, "scene", None))
    return jax.shard_map(
        per_device, mesh=mesh, in_specs=in_specs, out_specs=out_specs, check_vma=False
    )
```

```python
import math

import jax
import jax.numpy as jnp
from jax import lax
from jax.experimental import pallas as pl
from jax.experimental.pallas import tpu as pltpu
from jax.sharding import PartitionSpec as P

HEAD = 64
BF16 = jnp.bfloat16
F32 = jnp.float32
VMEM = pl.BlockSpec(memory_space=pltpu.VMEM)
SMEM = pl.BlockSpec(memory_space=pltpu.SMEM)
ANY = pl.BlockSpec(memory_space=pl.ANY)
NT = (((1,), (1,)), ((), ()))
NN = (((1,), (0,)), ((), ()))

def dot(a, b, dims=NN):
    return lax.dot_general(a, b, dims, preferred_element_type=F32)


def fold_kernel(weight, folded, sems):
    chans = weight.shape[-1]
    copies = []
    for k in range(9):
        for h_in in range(2):
            for h_out in range(2):
                copies.append(
                    pltpu.make_async_copy(
                        weight.at[k // 3, h_in - h_out + 1, k % 3],
                        folded.at[k, pl.ds(h_in * chans, chans), pl.ds(h_out * chans, chans)],
                        sems.at[k, 2 * h_in + h_out],
                    )
                )
    for copy in copies:
        copy.start()
    for copy in copies:
        copy.wait()


def fold(weight):
    wide = 2 * weight.shape[-1]
    return pl.pallas_call(
        fold_kernel,
        out_shape=pltpu.VMEM((9, wide, wide), BF16),
        in_specs=[ANY],
        out_specs=VMEM,
        scratch_shapes=[pltpu.SemaphoreType.DMA((9, 4))],
        compiler_params=pltpu.CompilerParams(vmem_limit_bytes=4 * 2**20),
        cost_estimate=pl.CostEstimate(
            flops=0, bytes_accessed=20 * 2**20, transcendentals=0
        ),
        name="fold",
    )(weight)


def store_pairs(values_of, sides, count, even, odd):
    before = None
    for t in range(count):
        now = values_of(t)
        for at, s in enumerate(sides):
            if t % 2 == 1:
                pair = jnp.concatenate([before[at], now[at]], axis=0).astype(BF16)
                even[s, 8 * (t - 1) : 8 * (t + 1), :] = pair
            elif t > 0:
                pair = jnp.concatenate([before[at], now[at]], axis=0).astype(BF16)
                odd[s, 8 * (t - 2) : 8 * t, :] = pair
        before = now


def build_centre(frame_of, count, even, odd):
    store_pairs(lambda t: (frame_of(t).astype(F32),), (1,), count, even, odd)


def build_sides(frame_of, low_of, high_of, count, even, odd):
    width = even.shape[2]
    sub = lax.broadcasted_iota(jnp.int32, (8, width), 0)

    def both(t):
        own = frame_of(t).astype(F32)
        left = jnp.where(sub == 0, jnp.broadcast_to(low_of(t), (8, width)), pltpu.roll(own, 1, 0))
        right = jnp.where(sub == 7, jnp.broadcast_to(high_of(t), (8, width)), pltpu.roll(own, 7, 0))
        return left, right

    store_pairs(both, (0, 2), count, even, odd)


def add_taps(total, side, even, odd, weight_of, dims, extra=None):
    rows = odd.shape[1]
    for off in range(3):
        if off == 1:
            lhs = odd[side, 0:rows, :]
        else:
            lhs = even[side, 8 * off : 8 * off + rows, :]
        if extra is not None:
            lhs = jnp.concatenate([lhs, extra(side, off)], axis=0)
        part = dot(lhs, weight_of(off, side), dims)
        if (side, off) == (1, 0):
            total[...] = part
        else:
            total[...] += part


def pack_kernel(place, frames, out_grad, before, after, core_out, chip_out, wide_f, wide_g):
    count = frames.shape[0]
    chans = frames.shape[3]
    lanes = chans // 128
    for t in range(count + 4):
        for h in range(2):
            if t < 2:
                value = before[t, h]
            elif t < count + 2:
                value = frames[t - 2, h]
            else:
                value = after[t - count - 2, h]
            value = value.astype(F32)
            for k in range(lanes):
                wide_f[lanes * h + k, 8 * t : 8 * (t + 1), :] = value[:, 128 * k : 128 * (k + 1)]
    for t in range(count + 2):
        for h in range(2):
            value = (out_grad[t, h] if t < count else after[t - count + 2, h]).astype(F32)
            for k in range(lanes):
                wide_g[lanes * h + k, 8 * t : 8 * (t + 1), :] = value[:, 128 * k : 128 * (k + 1)]
    even_core = place[1] == 0

    def column(source, at, rows):
        return jnp.concatenate(
            [source[k, pl.ds(at, rows, 8), :] for k in range(2 * lanes)], axis=1
        )

    def packed(first, second, grad):
        return jnp.concatenate(
            [
                column(wide_f, first, count + 4),
                column(wide_f, second, count + 4),
                column(wide_g, grad, count + 2),
                jnp.zeros((6, 2 * chans), F32),
            ],
            axis=0,
        )

    left = packed(0, 1, 0)
    right = packed(6, 7, 7)
    core_out[...] = jnp.where(even_core, right, left).astype(BF16)
    chip_out[...] = jnp.where(even_core, left, right).astype(BF16)


def pack(place, frames, out_grad, before, after):
    count, _, cols, chans = frames.shape
    rows = 3 * count + 16
    return pl.pallas_call(
        pack_kernel,
        out_shape=[jax.ShapeDtypeStruct((rows, 2 * chans), BF16)] * 2,
        in_specs=[SMEM] + [VMEM] * 4,
        out_specs=[VMEM] * 2,
        scratch_shapes=[
            pltpu.VMEM((2 * chans // 128, cols * (count + 4), 128), F32),
            pltpu.VMEM((2 * chans // 128, cols * (count + 2), 128), F32),
        ],
        compiler_params=pltpu.CompilerParams(vmem_limit_bytes=24 * 2**20),
        name="pack",
    )(place, frames, out_grad, before, after)


def forward_kernel(
    place,
    lengths,
    frames,
    before,
    after,
    core_sent,
    chip_sent,
    core_got,
    chip_got,
    out_grad,
    down,
    folded,
    latent_out,
    sums_out,
    tail_out,
    low_out,
    high_out,
    grad_out,
    block,
    grad_block,
    grad_done,
    down_block,
    own_low,
    own_high,
    low,
    high,
    even,
    odd,
    total,
    act,
    sems,
):
    chans = frames.shape[-1]
    count = frames.shape[0]
    ahead = count + 2
    rows = 8 * ahead
    first = [
        pltpu.make_async_copy(frames.at[:, h], block.at[:, :, pl.ds(h * chans, chans)], sems.at[h])
        for h in range(2)
    ]
    for copy in first:
        copy.start()
    later = [
        pltpu.make_async_copy(
            out_grad.at[:, h], grad_block.at[:, :, pl.ds(h * chans, chans)], sems.at[2 + h]
        )
        for h in range(2)
    ] + [pltpu.make_async_copy(down, down_block, sems.at[4])]
    for copy in later:
        copy.start()
    even_core = place[1] == 0

    def pick(core, chip, at_low, at_high):
        core, chip = core[...].astype(F32), chip[...].astype(F32)
        at_low[...] = jnp.where(even_core, chip, core)
        at_high[...] = jnp.where(even_core, core, chip)

    pick(core_sent, chip_sent, own_low, own_high)
    pick(core_got, chip_got, low, high)
    for copy in first:
        copy.wait()

    def frame_of(t):
        if 2 <= t < count + 2:
            return block[t - 2]
        part = (lambda h: before[t, h]) if t < 2 else (lambda h: after[t - count - 2, h])
        return jnp.concatenate([part(0).astype(F32), part(1).astype(F32)], axis=1)

    span = count + 4

    def rim(side, off):
        left = ((low, 0), (low, span), (own_low, 0))[side]
        right = ((own_high, span), (high, 0), (high, span))[side]
        return jnp.concatenate(
            [ref[at + off : at + off + ahead + 6, :] for ref, at in (left, right)], axis=0
        ).astype(BF16)

    build_centre(frame_of, span, even, odd)
    def weight_of(off, side):
        return folded[3 * off + side]

    add_taps(total, 1, even, odd, weight_of, NN, rim)
    build_sides(
        frame_of,
        lambda t: low[span + t : span + t + 1, :],
        lambda t: high[t : t + 1, :],
        span,
        even,
        odd,
    )
    for side in (0, 2):
        add_taps(total, side, even, odd, weight_of, NN, rim)
    for copy in later:
        copy.wait()

    def gates(pre):
        gate = 1.0 / (1.0 + jnp.exp(-pre))
        return gate, gate * (1.0 + pre * (1.0 - gate))

    for j in range(count // 8):
        pre = total[64 * j : 64 * (j + 1), :]
        gate, slope = gates(pre)
        own = block[8 * j : 8 * (j + 1)].astype(F32)
        act[j] = own + (pre * gate).reshape(own.shape)
        grad = grad_block[8 * j : 8 * (j + 1)].astype(F32) * slope.reshape(own.shape)
        grad_done[8 * j : 8 * (j + 1)] = grad.astype(BF16)
    for t in range(2):
        at = 8 * (count + t)
        _, slope = gates(total[at : at + 8, :])
        grad = jnp.concatenate([after[2 + t, 0].astype(F32), after[2 + t, 1].astype(F32)], axis=1)
        grad_done[count + t] = (grad * slope).astype(BF16)
    write = pltpu.make_async_copy(grad_done, grad_out, sems.at[5])
    write.start()
    for at, (source, target) in enumerate(((low, low_out), (high, high_out))):
        base = rows + at * (ahead + 6)
        _, slope = gates(total[base : base + ahead + 6, :])
        target[...] = slope * source[2 * span : 2 * span + ahead + 6, :]

    latent = jnp.zeros((2 * count, chans), F32)
    for k in range(8):
        lhs = jnp.concatenate(
            [
                act[:, k, :, h * chans : (h + 1) * chans].reshape(count, chans)
                for h in range(2)
            ],
            axis=0,
        ).astype(BF16)
        latent = latent + dot(lhs, down_block[k])
    latent = latent.astype(BF16).astype(F32)
    rounded = [
        jnp.concatenate([latent[8 * j : 8 * j + 8], latent[count + 8 * j : count + 8 * j + 8]], 0)
        for j in range(count // 8)
    ]
    running = jnp.zeros_like(rounded[0])
    for j in range(count // 8):
        now = place[0] * (count // 8) + j
        start = jnp.int32(0)
        begins = jnp.int32(0)
        for k in range(lengths.shape[0]):
            begins = jnp.where(start == now, 1, begins)
            start = start + lengths[k]
        running = jnp.where(begins > 0, rounded[j], running + rounded[j])
        sums_out[j] = running
        latent_out[j] = rounded[j]
    for k in range(tail_out.shape[0]):
        tail_out[k] = running
    write.wait()


def forward(peers, place, lengths, frames, before, after, columns, out_grad, down, folded):
    count, _, cols, chans = frames.shape
    wide = 2 * chans
    lat = count // 8
    ahead = count + 2
    rows = cols * ahead
    received = columns[0].shape
    return pl.pallas_call(
        forward_kernel,
        out_shape=(
            jax.ShapeDtypeStruct((lat, 16, chans), F32),
            jax.ShapeDtypeStruct((lat, 16, chans), F32),
            jax.ShapeDtypeStruct((peers, 16, chans), F32),
            jax.ShapeDtypeStruct((ahead + 6, wide), F32),
            jax.ShapeDtypeStruct((ahead + 6, wide), F32),
            jax.ShapeDtypeStruct((ahead, cols, wide), BF16),
        ),
        in_specs=[SMEM, SMEM, ANY] + [VMEM] * 6 + [ANY, ANY, VMEM],
        out_specs=[VMEM] * 5 + [ANY],
        scratch_shapes=[
            pltpu.VMEM((count, cols, wide), BF16),
            pltpu.VMEM((count, cols, wide), BF16),
            pltpu.VMEM((ahead, cols, wide), BF16),
            pltpu.VMEM(down.shape, BF16),
            pltpu.VMEM(received, F32),
            pltpu.VMEM(received, F32),
            pltpu.VMEM(received, F32),
            pltpu.VMEM(received, F32),
            pltpu.VMEM((3, rows + 16, wide), BF16),
            pltpu.VMEM((3, rows, wide), BF16),
            pltpu.VMEM((rows + 2 * (ahead + 6), wide), F32),
            pltpu.VMEM((lat, 8, cols, wide), F32),
            pltpu.SemaphoreType.DMA((6,)),
        ],
        compiler_params=pltpu.CompilerParams(vmem_limit_bytes=44 * 2**20),
        cost_estimate=pl.CostEstimate(
            flops=2 * 9 * rows * wide * wide, bytes_accessed=16 * 2**20, transcendentals=rows * wide
        ),
        name="forward",
    )(place, lengths, frames, before, after, *columns, out_grad, down, pltpu.with_memory_space_constraint(folded, pltpu.VMEM))


def backward_kernel(
    grad,
    low,
    high,
    out_grad,
    folded,
    result,
    block,
    source,
    done,
    even,
    odd,
    total,
    sems,
):
    count, _, cols, chans = out_grad.shape
    first = pltpu.make_async_copy(grad, block, sems.at[0])
    first.start()
    later = pltpu.make_async_copy(out_grad, source, sems.at[1])
    later.start()
    first.wait()

    def frame_of(t):
        return block[t]

    def weight_of(off, side):
        return folded[3 * (2 - off) + 2 - side]

    build_centre(frame_of, count + 2, even, odd)
    add_taps(total, 1, even, odd, weight_of, NT)
    build_sides(
        frame_of,
        lambda t: low[t : t + 1, :],
        lambda t: high[t : t + 1, :],
        count + 2,
        even,
        odd,
    )
    add_taps(total, 0, even, odd, weight_of, NT)
    add_taps(total, 2, even, odd, weight_of, NT)
    later.wait()
    writes = []
    step = count // 4
    for j in range(4):
        at = slice(8 * step * j, 8 * step * (j + 1))
        part = total[at, :]
        for h in range(2):
            mine = part[:, h * chans : (h + 1) * chans].reshape(step, cols, chans)
            done[step * j : step * (j + 1), h] = (
                source[step * j : step * (j + 1), h].astype(F32) + mine
            ).astype(BF16)
        write = pltpu.make_async_copy(
            done.at[pl.ds(step * j, step)], result.at[pl.ds(step * j, step)], sems.at[2 + j]
        )
        write.start()
        writes.append(write)
    for write in writes:
        write.wait()


def backward(grad, low, high, out_grad, folded):
    count, _, cols, chans = out_grad.shape
    rows, wide = count * cols, 2 * chans
    return pl.pallas_call(
        backward_kernel,
        out_shape=jax.ShapeDtypeStruct(out_grad.shape, BF16),
        in_specs=[ANY, VMEM, VMEM, ANY, VMEM],
        out_specs=ANY,
        scratch_shapes=[
            pltpu.VMEM(grad.shape, BF16),
            pltpu.VMEM(out_grad.shape, BF16),
            pltpu.VMEM(out_grad.shape, BF16),
            pltpu.VMEM((3, rows + 16, wide), BF16),
            pltpu.VMEM((3, rows, wide), BF16),
            pltpu.VMEM((rows, wide), F32),
            pltpu.SemaphoreType.DMA((6,)),
        ],
        compiler_params=pltpu.CompilerParams(vmem_limit_bytes=44 * 2**20),
        cost_estimate=pl.CostEstimate(
            flops=2 * 9 * rows * wide * wide, bytes_accessed=12 * 2**20, transcendentals=0
        ),
        name="backward",
    )(grad, low, high, out_grad, pltpu.with_memory_space_constraint(folded, pltpu.VMEM))


def mix_kernel(place, lengths, latent, sums, tails, mixed):
    lat = latent.shape[0]
    peers = tails.shape[0]
    me = place[0]
    starts = [jnp.int32(0)]
    for k in range(lengths.shape[0] - 1):
        starts.append(starts[-1] + lengths[k])
    opened = jnp.int32(0)
    for start in starts:
        opened = jnp.where(start < me * lat, jnp.maximum(start, opened), opened)
    carried = jnp.zeros(latent.shape[1:], F32)
    for k in range(peers):
        counts = jnp.logical_and(k < me, (k + 1) * lat > opened)
        carried = carried + jnp.where(counts, tails[k], 0.0)
    for j in range(lat):
        now = me * lat + j
        begin = jnp.int32(0)
        for start in starts:
            begin = jnp.where(start <= now, jnp.maximum(start, begin), begin)
        shot = sums[j] + jnp.where(begin < me * lat, carried, 0.0)
        length = jnp.full(shot.shape, now - begin + 1, jnp.int32).astype(F32)
        mixed[16 * j : 16 * (j + 1), :] = (latent[j] + shot / length).astype(BF16)


def mix(place, lengths, latent, sums, tails):
    return pl.pallas_call(
        mix_kernel,
        out_shape=jax.ShapeDtypeStruct((latent.shape[0] * 16, latent.shape[2]), BF16),
        in_specs=[SMEM, SMEM, VMEM, VMEM, VMEM],
        out_specs=VMEM,
        compiler_params=pltpu.CompilerParams(vmem_limit_bytes=16 * 2**20),
        name="mix",
    )(place, lengths, latent, sums, tails)


def attend_kernel(labels, mine, *refs):
    pieces, (w_query, w_key, w_value, w_out, result, keys, values) = refs[:-7], refs[-7:]
    tokens, chans = mine.shape
    lat = labels.shape[0]
    per = tokens // lat
    at = 0
    for piece in pieces:
        block = piece[...]
        size = block.shape[0]
        keys[at : at + size, :] = dot(block, w_key[...]).astype(BF16)
        values[at : at + size, :] = dot(block, w_value[...]).astype(BF16)
        at += size
    query = (dot(mine[...], w_query[...]).astype(BF16) * BF16(1.0 / math.sqrt(HEAD))).astype(BF16)
    row = lax.broadcasted_iota(jnp.int32, (tokens, 1), 0) // per
    col = (lax.broadcasted_iota(jnp.int32, (1, tokens), 1) % tokens) // per
    row_label = jnp.zeros((tokens, 1), jnp.int32)
    col_label = jnp.zeros((1, tokens), jnp.int32)
    for j in range(lat):
        row_label = jnp.where(row == j, labels[j, 0], row_label)
        col_label = jnp.where(col == j, labels[j, 0], col_label)
    same = jnp.logical_and(row_label == col_label, col <= row)
    bias = jnp.where(same, 0.0, -1e30).astype(F32)
    bias = jnp.concatenate([bias] * (at // tokens), axis=1)
    outs = []
    for head in range(chans // HEAD):
        lanes = slice(head * HEAD, (head + 1) * HEAD)
        scores = dot(query[:, lanes], keys[:, lanes], NT) + bias
        top = jnp.max(scores, axis=1, keepdims=True)
        expo = jnp.exp(scores - top)
        norm = jnp.sum(expo, axis=1, keepdims=True)
        outs.append(dot(expo.astype(BF16), values[:, lanes]) / norm)
    heads = jnp.concatenate(outs, axis=1).astype(BF16)
    final = mine[...].astype(F32) + dot(heads, w_out[...])
    for j in range(lat):
        for h in range(2):
            at = per * j + 8 * h
            result[j, h] = final[at : at + 8].astype(BF16)


def attend(labels, mine, pieces, w_query, w_key, w_value, w_out):
    tokens, chans = mine.shape
    total = sum(piece.shape[0] for piece in pieces)
    return pl.pallas_call(
        attend_kernel,
        out_shape=jax.ShapeDtypeStruct((labels.shape[0], 2, 8, chans), BF16),
        in_specs=[SMEM] + [VMEM] * (5 + len(pieces)),
        out_specs=VMEM,
        scratch_shapes=[pltpu.VMEM((total, chans), BF16), pltpu.VMEM((total, chans), BF16)],
        compiler_params=pltpu.CompilerParams(vmem_limit_bytes=24 * 2**20),
        name="attend",
    )(labels, mine, *pieces, w_query, w_key, w_value, w_out)


def shifted(value, axis, steps):
    count = lax.axis_size(axis)
    return lax.ppermute(
        value, axis, [(i, i + steps) for i in range(count) if 0 <= i + steps < count]
    )


def with_core(value):
    count = lax.axis_size("scene")
    return lax.ppermute(value, "scene", [(i, i ^ 1) for i in range(count)])


def with_chip(value):
    count = lax.axis_size("scene")
    pairs = [(i, i + 1) for i in range(1, count - 1, 2)]
    return lax.ppermute(value, "scene", pairs + [(b, a) for a, b in pairs])


def chip_shifts(value):
    count = lax.axis_size("scene")
    return [
        lax.ppermute(value, "scene", [(i, (i + 2 * k) % count) for i in range(count)])
        for k in range(1, count // 2)
    ]


def per_device(
    frames,
    conv_weight,
    down_weight,
    w_query,
    w_key,
    w_value,
    w_out,
    shot_lengths,
    scene_label,
    out_grad,
):
    count = frames.shape[0]
    place = jnp.stack([lax.axis_index("tm"), lax.axis_index("scene") % 2]).astype(jnp.int32)
    before = shifted(frames[count - 2 :], "tm", 1)
    after = shifted(jnp.concatenate([frames[:2], out_grad[:2]], axis=0), "tm", -1)
    folded = fold(conv_weight)
    sent = pack(place, frames, out_grad, before, after)
    columns = (*sent, with_core(sent[0]), with_chip(sent[1]))
    latent, sums, tail, low, high, grad = forward(
        lax.axis_size("tm"),
        place,
        shot_lengths,
        frames,
        before,
        after,
        columns,
        out_grad,
        down_weight,
        folded,
    )
    tails = lax.all_to_all(tail, "tm", 0, 0, tiled=True)
    mixed = mix(place, shot_lengths, latent, sums, tails)
    chips = chip_shifts(mixed)
    frame_grad = backward(grad, low, high, out_grad, folded)
    chips, frame_grad = lax.optimization_barrier((chips, frame_grad))
    own = jnp.concatenate([mixed, *chips], axis=0)
    pieces = [own, with_core(own)]
    latent_out = attend(scene_label, mixed, pieces, w_query, w_key, w_value, w_out)
    return (latent_out, frame_grad)


def solution(mesh):
    in_specs = (
        P("tm", None, "scene", None),
        P(),
        P(),
        P(),
        P(),
        P(),
        P(),
        P(),
        P("tm", None),
        P("tm", None, "scene", None),
    )
    out_specs = (P("tm", None, "scene", None), P("tm", None, "scene", None))
    return jax.shard_map(
        per_device, mesh=mesh, in_specs=in_specs, out_specs=out_specs, check_vma=False
    )
```

```python
import math

import jax
import jax.numpy as jnp
from jax import lax
from jax.experimental import pallas as pl
from jax.experimental.pallas import tpu as pltpu
from jax.sharding import PartitionSpec as P

HEAD = 64
BF16 = jnp.bfloat16
F32 = jnp.float32
VMEM = pl.BlockSpec(memory_space=pltpu.VMEM)
SMEM = pl.BlockSpec(memory_space=pltpu.SMEM)
ANY = pl.BlockSpec(memory_space=pl.ANY)
NT = (((1,), (1,)), ((), ()))
NN = (((1,), (0,)), ((), ()))

def near(value):
    return pltpu.with_memory_space_constraint(value, pltpu.VMEM)


def dot(a, b, dims=NN):
    return lax.dot_general(a, b, dims, preferred_element_type=F32)


def fetch_kernel(frames, out_grad, weight, frames_out, grad_out, weight_out, sems):
    copies = [
        pltpu.make_async_copy(source, target, sems.at[k])
        for k, (source, target) in enumerate(
            ((frames, frames_out), (out_grad, grad_out), (weight, weight_out))
        )
    ]
    for copy in copies:
        copy.start()
    for copy in copies:
        copy.wait()


def fetch(frames, out_grad, weight):
    return pl.pallas_call(
        fetch_kernel,
        out_shape=[pltpu.VMEM(value.shape, BF16) for value in (frames, out_grad, weight)],
        in_specs=[ANY] * 3,
        out_specs=[VMEM] * 3,
        scratch_shapes=[pltpu.SemaphoreType.DMA((3,))],
        compiler_params=pltpu.CompilerParams(vmem_limit_bytes=52 * 2**20),
        cost_estimate=pl.CostEstimate(
            flops=0, bytes_accessed=20 * 2**20, transcendentals=0
        ),
        name="fetch",
    )(frames, out_grad, weight)


def fold_kernel(weight, folded, sems):
    chans = weight.shape[-1]
    copies = []
    for k in range(9):
        for h_in in range(2):
            for h_out in range(2):
                copies.append(
                    pltpu.make_async_copy(
                        weight.at[k // 3, h_in - h_out + 1, k % 3],
                        folded.at[k, pl.ds(h_in * chans, chans), pl.ds(h_out * chans, chans)],
                        sems.at[k, 2 * h_in + h_out],
                    )
                )
    for copy in copies:
        copy.start()
    for copy in copies:
        copy.wait()


def fold(weight):
    wide = 2 * weight.shape[-1]
    return pl.pallas_call(
        fold_kernel,
        out_shape=pltpu.VMEM((9, wide, wide), BF16),
        in_specs=[VMEM],
        out_specs=VMEM,
        scratch_shapes=[pltpu.SemaphoreType.DMA((9, 4))],
        compiler_params=pltpu.CompilerParams(vmem_limit_bytes=4 * 2**20),
        cost_estimate=pl.CostEstimate(
            flops=0, bytes_accessed=20 * 2**20, transcendentals=0
        ),
        name="fold",
    )(near(weight))


def store_pairs(values_of, sides, count, even, odd):
    before = None
    for t in range(count):
        now = values_of(t)
        for at, s in enumerate(sides):
            if t % 2 == 1:
                pair = jnp.concatenate([before[at], now[at]], axis=0).astype(BF16)
                even[s, 8 * (t - 1) : 8 * (t + 1), :] = pair
            elif t > 0:
                pair = jnp.concatenate([before[at], now[at]], axis=0).astype(BF16)
                odd[s, 8 * (t - 2) : 8 * t, :] = pair
        before = now


def build_centre(frame_of, count, even, odd):
    store_pairs(lambda t: (frame_of(t).astype(F32),), (1,), count, even, odd)


def build_sides(frame_of, low_of, high_of, count, even, odd):
    width = even.shape[2]
    sub = lax.broadcasted_iota(jnp.int32, (8, width), 0)

    def both(t):
        own = frame_of(t).astype(F32)
        left = jnp.where(sub == 0, jnp.broadcast_to(low_of(t), (8, width)), pltpu.roll(own, 1, 0))
        right = jnp.where(sub == 7, jnp.broadcast_to(high_of(t), (8, width)), pltpu.roll(own, 7, 0))
        return left, right

    store_pairs(both, (0, 2), count, even, odd)


def sum_taps(total, at, rows, sides, even, odd, weight_of, dims, extra=None):
    count = rows
    for side in sides:
        for off in range(3):
            if off == 1:
                lhs = odd[side, at : at + rows, :]
            else:
                lhs = even[side, at + 8 * off : at + 8 * off + rows, :]
            if extra is not None:
                lhs = jnp.concatenate([lhs, extra(side, off)], axis=0)
                count = lhs.shape[0]
            part = dot(lhs, weight_of(off, side), dims)
            if (side, off) == (1, 0):
                total[at : at + count, :] = part
            else:
                total[at : at + count, :] += part


def pack_kernel(place, frames, out_grad, before, after, core_out, chip_out, wide_f, wide_g):
    count = frames.shape[0]
    chans = frames.shape[3]
    lanes = chans // 128
    for t in range(count + 4):
        for h in range(2):
            if t < 2:
                value = before[t, h]
            elif t < count + 2:
                value = frames[t - 2, h]
            else:
                value = after[t - count - 2, h]
            value = value.astype(F32)
            for k in range(lanes):
                wide_f[lanes * h + k, 8 * t : 8 * (t + 1), :] = value[:, 128 * k : 128 * (k + 1)]
    for t in range(count + 2):
        for h in range(2):
            value = (out_grad[t, h] if t < count else after[t - count + 2, h]).astype(F32)
            for k in range(lanes):
                wide_g[lanes * h + k, 8 * t : 8 * (t + 1), :] = value[:, 128 * k : 128 * (k + 1)]
    even_core = place[1] == 0

    def column(source, at, rows):
        return jnp.concatenate(
            [source[k, pl.ds(at, rows, 8), :] for k in range(2 * lanes)], axis=1
        )

    def packed(first, second, grad):
        return jnp.concatenate(
            [
                column(wide_f, first, count + 4),
                column(wide_f, second, count + 4),
                column(wide_g, grad, count + 2),
                jnp.zeros((6, 2 * chans), F32),
            ],
            axis=0,
        )

    left = packed(0, 1, 0)
    right = packed(6, 7, 7)
    core_out[...] = jnp.where(even_core, right, left).astype(BF16)
    chip_out[...] = jnp.where(even_core, left, right).astype(BF16)


def pack(place, frames, out_grad, before, after):
    count, _, cols, chans = frames.shape
    rows = 3 * count + 16
    return pl.pallas_call(
        pack_kernel,
        out_shape=[pltpu.VMEM((rows, 2 * chans), BF16)] * 2,
        in_specs=[SMEM] + [VMEM] * 4,
        out_specs=[VMEM] * 2,
        scratch_shapes=[
            pltpu.VMEM((2 * chans // 128, cols * (count + 4), 128), F32),
            pltpu.VMEM((2 * chans // 128, cols * (count + 2), 128), F32),
        ],
        compiler_params=pltpu.CompilerParams(vmem_limit_bytes=24 * 2**20),
        name="pack",
    )(place, near(frames), near(out_grad), near(before), near(after))


def forward_kernel(
    place,
    lengths,
    frames,
    before,
    after,
    core_sent,
    chip_sent,
    core_got,
    chip_got,
    out_grad,
    down,
    folded,
    latent_out,
    sums_out,
    tail_out,
    low_out,
    high_out,
    grad_out,
    down_block,
    own_low,
    own_high,
    low,
    high,
    even,
    odd,
    total,
    act,
    sems,
):
    chans = frames.shape[-1]
    count = frames.shape[0]
    ahead = count + 2
    rows = 8 * ahead
    fetch_down = pltpu.make_async_copy(down, down_block, sems.at[0])
    fetch_down.start()
    even_core = place[1] == 0

    def pick(core, chip, at_low, at_high):
        core, chip = core[...].astype(F32), chip[...].astype(F32)
        at_low[...] = jnp.where(even_core, chip, core)
        at_high[...] = jnp.where(even_core, core, chip)

    pick(core_sent, chip_sent, own_low, own_high)
    pick(core_got, chip_got, low, high)

    def frame_of(t):
        if t < 2:
            part = lambda h: before[t, h]
        elif t < count + 2:
            part = lambda h: frames[t - 2, h]
        else:
            part = lambda h: after[t - count - 2, h]
        return jnp.concatenate([part(0).astype(F32), part(1).astype(F32)], axis=1)

    span = count + 4

    def rim(side, off):
        left = ((low, 0), (low, span), (own_low, 0))[side]
        right = ((own_high, span), (high, 0), (high, span))[side]
        return jnp.concatenate(
            [ref[at + off : at + off + ahead + 6, :] for ref, at in (left, right)], axis=0
        ).astype(BF16)

    build_centre(frame_of, span, even, odd)
    def weight_of(off, side):
        return folded[3 * off + side]

    def gates(pre):
        gate = 0.5 * jnp.tanh(0.5 * pre) + 0.5
        return gate, gate * (1.0 + pre * (1.0 - gate))

    def finish(first, last):
        for j in range(first, last):
            pre = total[64 * j : 64 * (j + 1), :]
            gate, slope = gates(pre)
            silu = pre * gate
            for h in range(2):
                lanes = slice(h * chans, (h + 1) * chans)
                own = frames[8 * j : 8 * (j + 1), h].astype(F32)
                act[j, :, :, lanes] = own + silu[:, lanes].reshape(own.shape)
                grad = out_grad[8 * j : 8 * (j + 1), h].astype(F32)
                grad = grad * slope[:, lanes].reshape(own.shape)
                grad_out[8 * j : 8 * (j + 1), :, lanes] = grad.astype(BF16)

    half = 64 * (count // 16)
    sum_taps(total, 0, half, (1,), even, odd, weight_of, NN)
    build_sides(
        frame_of,
        lambda t: low[span + t : span + t + 1, :],
        lambda t: high[t : t + 1, :],
        span,
        even,
        odd,
    )
    sum_taps(total, 0, half, (0, 2), even, odd, weight_of, NN)
    sum_taps(total, half, rows - half, (1, 0, 2), even, odd, weight_of, NN, rim)
    finish(0, count // 16)
    finish(count // 16, count // 8)
    for t in range(2):
        at = 8 * (count + t)
        _, slope = gates(total[at : at + 8, :])
        grad = jnp.concatenate([after[2 + t, 0].astype(F32), after[2 + t, 1].astype(F32)], axis=1)
        grad_out[count + t] = (grad * slope).astype(BF16)
    for at, (source, target) in enumerate(((low, low_out), (high, high_out))):
        base = rows + at * (ahead + 6)
        _, slope = gates(total[base : base + ahead + 6, :])
        target[...] = slope * source[2 * span : 2 * span + ahead + 6, :]

    fetch_down.wait()
    latent = jnp.zeros((2 * count, chans), F32)
    for k in range(8):
        lhs = jnp.concatenate(
            [
                act[:, k, :, h * chans : (h + 1) * chans].reshape(count, chans)
                for h in range(2)
            ],
            axis=0,
        ).astype(BF16)
        latent = latent + dot(lhs, down_block[k])
    latent = latent.astype(BF16).astype(F32)
    rounded = [
        jnp.concatenate([latent[8 * j : 8 * j + 8], latent[count + 8 * j : count + 8 * j + 8]], 0)
        for j in range(count // 8)
    ]
    running = jnp.zeros_like(rounded[0])
    for j in range(count // 8):
        now = place[0] * (count // 8) + j
        start = jnp.int32(0)
        begins = jnp.int32(0)
        for k in range(lengths.shape[0]):
            begins = jnp.where(start == now, 1, begins)
            start = start + lengths[k]
        running = jnp.where(begins > 0, rounded[j], running + rounded[j])
        sums_out[j] = running
        latent_out[j] = rounded[j]
    for k in range(tail_out.shape[0]):
        tail_out[k] = running


def forward(peers, place, lengths, frames, before, after, columns, out_grad, down, folded):
    count, _, cols, chans = frames.shape
    wide = 2 * chans
    lat = count // 8
    ahead = count + 2
    rows = cols * ahead
    received = columns[0].shape
    return pl.pallas_call(
        forward_kernel,
        out_shape=(
            pltpu.VMEM((lat, 16, chans), F32),
            pltpu.VMEM((lat, 16, chans), F32),
            pltpu.VMEM((peers, 16, chans), F32),
            pltpu.VMEM((ahead + 6, wide), F32),
            pltpu.VMEM((ahead + 6, wide), F32),
            pltpu.VMEM((ahead, cols, wide), BF16),
        ),
        in_specs=[SMEM, SMEM] + [VMEM] * 8 + [ANY, VMEM],
        out_specs=[VMEM] * 6,
        scratch_shapes=[
            pltpu.VMEM(down.shape, BF16),
            pltpu.VMEM(received, F32),
            pltpu.VMEM(received, F32),
            pltpu.VMEM(received, F32),
            pltpu.VMEM(received, F32),
            pltpu.VMEM((3, rows + 16, wide), BF16),
            pltpu.VMEM((3, rows, wide), BF16),
            pltpu.VMEM((rows + 2 * (ahead + 6), wide), F32),
            pltpu.VMEM((lat, 8, cols, wide), F32),
            pltpu.SemaphoreType.DMA((1,)),
        ],
        compiler_params=pltpu.CompilerParams(vmem_limit_bytes=28 * 2**20),
        cost_estimate=pl.CostEstimate(
            flops=2 * 9 * rows * wide * wide, bytes_accessed=16 * 2**20, transcendentals=rows * wide
        ),
        name="forward",
    )(
        place,
        lengths,
        *(near(value) for value in (frames, before, after, *columns, out_grad)),
        down,
        near(folded),
    )


def backward_kernel(
    grad,
    low,
    high,
    out_grad,
    folded,
    result,
    done,
    even,
    odd,
    total,
    sems,
):
    count, _, cols, chans = out_grad.shape

    def frame_of(t):
        return grad[t]

    def weight_of(off, side):
        return folded[3 * (2 - off) + 2 - side]

    writes = []
    half = count // 2

    def finish(first, last):
        for j in range(first, last, 8):
            part = total[8 * j : 8 * (j + 8), :]
            for h in range(2):
                mine = part[:, h * chans : (h + 1) * chans].reshape(8, cols, chans)
                done[j : j + 8, h] = (out_grad[j : j + 8, h].astype(F32) + mine).astype(BF16)
        write = pltpu.make_async_copy(
            done.at[pl.ds(first, last - first)],
            result.at[pl.ds(first, last - first)],
            sems.at[len(writes)],
        )
        write.start()
        writes.append(write)

    build_centre(frame_of, count + 2, even, odd)
    sum_taps(total, 0, 8 * half, (1,), even, odd, weight_of, NT)
    build_sides(
        frame_of,
        lambda t: low[t : t + 1, :],
        lambda t: high[t : t + 1, :],
        count + 2,
        even,
        odd,
    )
    sum_taps(total, 0, 8 * half, (0, 2), even, odd, weight_of, NT)
    sum_taps(total, 8 * half, 8 * half, (1, 0, 2), even, odd, weight_of, NT)
    finish(0, half)
    finish(half, half + half // 2)
    finish(half + half // 2, count)
    for write in writes:
        write.wait()


def backward(grad, low, high, out_grad, folded):
    count, _, cols, chans = out_grad.shape
    rows, wide = count * cols, 2 * chans
    return pl.pallas_call(
        backward_kernel,
        out_shape=jax.ShapeDtypeStruct(out_grad.shape, BF16),
        in_specs=[VMEM] * 5,
        out_specs=ANY,
        scratch_shapes=[
            pltpu.VMEM(out_grad.shape, BF16),
            pltpu.VMEM((3, rows + 16, wide), BF16),
            pltpu.VMEM((3, rows, wide), BF16),
            pltpu.VMEM((rows, wide), F32),
            pltpu.SemaphoreType.DMA((3,)),
        ],
        compiler_params=pltpu.CompilerParams(vmem_limit_bytes=24 * 2**20),
        cost_estimate=pl.CostEstimate(
            flops=2 * 9 * rows * wide * wide, bytes_accessed=12 * 2**20, transcendentals=0
        ),
        name="backward",
    )(*(near(value) for value in (grad, low, high, out_grad, folded)))


def mix_kernel(place, lengths, latent, sums, tails, mixed):
    lat = latent.shape[0]
    peers = tails.shape[0]
    me = place[0]
    starts = [jnp.int32(0)]
    for k in range(lengths.shape[0] - 1):
        starts.append(starts[-1] + lengths[k])
    opened = jnp.int32(0)
    for start in starts:
        opened = jnp.where(start < me * lat, jnp.maximum(start, opened), opened)
    carried = jnp.zeros(latent.shape[1:], F32)
    for k in range(peers):
        counts = jnp.logical_and(k < me, (k + 1) * lat > opened)
        carried = carried + jnp.where(counts, tails[k], 0.0)
    for j in range(lat):
        now = me * lat + j
        begin = jnp.int32(0)
        for start in starts:
            begin = jnp.where(start <= now, jnp.maximum(start, begin), begin)
        shot = sums[j] + jnp.where(begin < me * lat, carried, 0.0)
        length = jnp.full(shot.shape, now - begin + 1, jnp.int32).astype(F32)
        mixed[16 * j : 16 * (j + 1), :] = (latent[j] + shot / length).astype(BF16)


def mix(place, lengths, latent, sums, tails):
    return pl.pallas_call(
        mix_kernel,
        out_shape=jax.ShapeDtypeStruct((latent.shape[0] * 16, latent.shape[2]), BF16),
        in_specs=[SMEM, SMEM, VMEM, VMEM, VMEM],
        out_specs=VMEM,
        compiler_params=pltpu.CompilerParams(vmem_limit_bytes=16 * 2**20),
        name="mix",
    )(place, lengths, near(latent), near(sums), near(tails))


def attend_kernel(labels, mine, *refs):
    pieces, (w_query, w_key, w_value, w_out, result, keys, values) = refs[:-7], refs[-7:]
    tokens, chans = mine.shape
    lat = labels.shape[0]
    per = tokens // lat
    at = 0
    for piece in pieces:
        block = piece[...]
        size = block.shape[0]
        keys[at : at + size, :] = dot(block, w_key[...]).astype(BF16)
        values[at : at + size, :] = dot(block, w_value[...]).astype(BF16)
        at += size
    query = (dot(mine[...], w_query[...]).astype(BF16) * BF16(1.0 / math.sqrt(HEAD))).astype(BF16)
    row = lax.broadcasted_iota(jnp.int32, (tokens, 1), 0) // per
    col = (lax.broadcasted_iota(jnp.int32, (1, tokens), 1) % tokens) // per
    row_label = jnp.zeros((tokens, 1), jnp.int32)
    col_label = jnp.zeros((1, tokens), jnp.int32)
    for j in range(lat):
        row_label = jnp.where(row == j, labels[j, 0], row_label)
        col_label = jnp.where(col == j, labels[j, 0], col_label)
    same = jnp.logical_and(row_label == col_label, col <= row)
    bias = jnp.where(same, 0.0, -1e30).astype(F32)
    bias = jnp.concatenate([bias] * (at // tokens), axis=1)
    outs = []
    for head in range(chans // HEAD):
        lanes = slice(head * HEAD, (head + 1) * HEAD)
        scores = dot(query[:, lanes], keys[:, lanes], NT) + bias
        top = jnp.max(scores, axis=1, keepdims=True)
        expo = jnp.exp(scores - top)
        norm = jnp.sum(expo, axis=1, keepdims=True)
        outs.append(dot(expo.astype(BF16), values[:, lanes]) / norm)
    heads = jnp.concatenate(outs, axis=1).astype(BF16)
    final = mine[...].astype(F32) + dot(heads, w_out[...])
    for j in range(lat):
        for h in range(2):
            at = per * j + 8 * h
            result[j, h] = final[at : at + 8].astype(BF16)


def attend(labels, mine, pieces, w_query, w_key, w_value, w_out):
    tokens, chans = mine.shape
    total = sum(piece.shape[0] for piece in pieces)
    return pl.pallas_call(
        attend_kernel,
        out_shape=jax.ShapeDtypeStruct((labels.shape[0], 2, 8, chans), BF16),
        in_specs=[SMEM] + [VMEM] * (5 + len(pieces)),
        out_specs=VMEM,
        scratch_shapes=[pltpu.VMEM((total, chans), BF16), pltpu.VMEM((total, chans), BF16)],
        compiler_params=pltpu.CompilerParams(vmem_limit_bytes=24 * 2**20),
        name="attend",
    )(labels, mine, *pieces, w_query, w_key, w_value, w_out)


def shifted(value, axis, steps):
    count = lax.axis_size(axis)
    return lax.ppermute(
        value, axis, [(i, i + steps) for i in range(count) if 0 <= i + steps < count]
    )


def with_core(value):
    count = lax.axis_size("scene")
    return lax.ppermute(value, "scene", [(i, i ^ 1) for i in range(count)])


def with_chip(value):
    count = lax.axis_size("scene")
    pairs = [(i, i + 1) for i in range(1, count - 1, 2)]
    return lax.ppermute(value, "scene", pairs + [(b, a) for a, b in pairs])


def chip_shifts(value):
    count = lax.axis_size("scene")
    return [
        lax.ppermute(value, "scene", [(i, (i + 2 * k) % count) for i in range(count)])
        for k in range(1, count // 2)
    ]


def per_device(
    frames,
    conv_weight,
    down_weight,
    w_query,
    w_key,
    w_value,
    w_out,
    shot_lengths,
    scene_label,
    out_grad,
):
    count = frames.shape[0]
    place = jnp.stack([lax.axis_index("tm"), lax.axis_index("scene") % 2]).astype(jnp.int32)
    before = shifted(frames[count - 2 :], "tm", 1)
    after = shifted(jnp.concatenate([frames[:2], out_grad[:2]], axis=0), "tm", -1)
    near_frames, near_grad, near_weight = fetch(frames, out_grad, conv_weight)
    (before, after), near_weight = lax.optimization_barrier(((before, after), near_weight))
    sent = pack(place, near_frames, near_grad, before, after)
    received = (with_core(sent[0]), with_chip(sent[1]))
    received, folded = lax.optimization_barrier((received, fold(near_weight)))
    latent, sums, tail, low, high, grad = forward(
        lax.axis_size("tm"),
        place,
        shot_lengths,
        near_frames,
        before,
        after,
        (*sent, *received),
        near_grad,
        down_weight,
        folded,
    )
    tails = lax.all_to_all(tail, "tm", 0, 0, tiled=True)
    mixed = mix(place, shot_lengths, latent, sums, tails)
    chips = chip_shifts(mixed)
    frame_grad = backward(grad, low, high, near_grad, folded)
    chips, frame_grad = lax.optimization_barrier((chips, frame_grad))
    own = jnp.concatenate([mixed, *chips], axis=0)
    pieces = [own, with_core(own)]
    latent_out = attend(scene_label, mixed, pieces, w_query, w_key, w_value, w_out)
    return (latent_out, frame_grad)


def solution(mesh):
    in_specs = (
        P("tm", None, "scene", None),
        P(),
        P(),
        P(),
        P(),
        P(),
        P(),
        P(),
        P("tm", None),
        P("tm", None, "scene", None),
    )
    out_specs = (P("tm", None, "scene", None), P("tm", None, "scene", None))
    return jax.shard_map(
        per_device, mesh=mesh, in_specs=in_specs, out_specs=out_specs, check_vma=False
    )
```

```python
import math

import jax
import jax.numpy as jnp
from jax import lax
from jax.experimental import pallas as pl
from jax.experimental.pallas import tpu as pltpu
from jax.sharding import PartitionSpec as P

HEAD = 64
BF16 = jnp.bfloat16
F32 = jnp.float32
VMEM = pl.BlockSpec(memory_space=pltpu.VMEM)
SMEM = pl.BlockSpec(memory_space=pltpu.SMEM)
ANY = pl.BlockSpec(memory_space=pl.ANY)
NT = (((1,), (1,)), ((), ()))
NN = (((1,), (0,)), ((), ()))

def near(value):
    return pltpu.with_memory_space_constraint(value, pltpu.VMEM)


def dot(a, b, dims=NN):
    return lax.dot_general(a, b, dims, preferred_element_type=F32)


def fetch_kernel(frames, out_grad, weight, frames_out, grad_out, weight_out, sems):
    copies = [
        pltpu.make_async_copy(source, target, sems.at[k])
        for k, (source, target) in enumerate(
            ((frames, frames_out), (out_grad, grad_out), (weight, weight_out))
        )
    ]
    for copy in copies:
        copy.start()
    for copy in copies:
        copy.wait()


def fetch(frames, out_grad, weight):
    return pl.pallas_call(
        fetch_kernel,
        out_shape=[pltpu.VMEM(value.shape, BF16) for value in (frames, out_grad, weight)],
        in_specs=[ANY] * 3,
        out_specs=[VMEM] * 3,
        scratch_shapes=[pltpu.SemaphoreType.DMA((3,))],
        compiler_params=pltpu.CompilerParams(vmem_limit_bytes=52 * 2**20),
        cost_estimate=pl.CostEstimate(
            flops=0, bytes_accessed=20 * 2**20, transcendentals=0
        ),
        name="fetch",
    )(frames, out_grad, weight)


def fold_kernel(weight, folded, sems):
    chans = weight.shape[-1]
    copies = []
    for k in range(9):
        for h_in in range(2):
            for h_out in range(2):
                copies.append(
                    pltpu.make_async_copy(
                        weight.at[k // 3, h_in - h_out + 1, k % 3],
                        folded.at[k, pl.ds(h_in * chans, chans), pl.ds(h_out * chans, chans)],
                        sems.at[k, 2 * h_in + h_out],
                    )
                )
    for copy in copies:
        copy.start()
    for copy in copies:
        copy.wait()


def fold(weight):
    wide = 2 * weight.shape[-1]
    return pl.pallas_call(
        fold_kernel,
        out_shape=pltpu.VMEM((9, wide, wide), BF16),
        in_specs=[VMEM],
        out_specs=VMEM,
        scratch_shapes=[pltpu.SemaphoreType.DMA((9, 4))],
        compiler_params=pltpu.CompilerParams(vmem_limit_bytes=4 * 2**20),
        cost_estimate=pl.CostEstimate(
            flops=0, bytes_accessed=20 * 2**20, transcendentals=0
        ),
        name="fold",
    )(near(weight))


def store_pairs(values_of, sides, count, even, odd):
    before = None
    for t in range(count):
        now = values_of(t)
        for at, s in enumerate(sides):
            if t % 2 == 1:
                pair = jnp.concatenate([before[at], now[at]], axis=0).astype(BF16)
                even[s, 8 * (t - 1) : 8 * (t + 1), :] = pair
            elif t > 0:
                pair = jnp.concatenate([before[at], now[at]], axis=0).astype(BF16)
                odd[s, 8 * (t - 2) : 8 * t, :] = pair
        before = now


def build_centre(frame_of, count, even, odd):
    store_pairs(lambda t: (frame_of(t).astype(F32),), (1,), count, even, odd)


def build_sides(frame_of, low_of, high_of, count, even, odd):
    width = even.shape[2]
    sub = lax.broadcasted_iota(jnp.int32, (8, width), 0)

    def both(t):
        own = frame_of(t).astype(F32)
        left = jnp.where(sub == 0, jnp.broadcast_to(low_of(t), (8, width)), pltpu.roll(own, 1, 0))
        right = jnp.where(sub == 7, jnp.broadcast_to(high_of(t), (8, width)), pltpu.roll(own, 7, 0))
        return left, right

    store_pairs(both, (0, 2), count, even, odd)


def sum_taps(total, at, rows, sides, even, odd, weight_of, dims, extra=None):
    count = rows
    for side in sides:
        for off in range(3):
            if off == 1:
                lhs = odd[side, at : at + rows, :]
            else:
                lhs = even[side, at + 8 * off : at + 8 * off + rows, :]
            if extra is not None:
                lhs = jnp.concatenate([lhs, extra(side, off)], axis=0)
                count = lhs.shape[0]
            part = dot(lhs, weight_of(off, side), dims)
            if (side, off) == (1, 0):
                total[at : at + count, :] = part
            else:
                total[at : at + count, :] += part


def pack_kernel(place, frames, out_grad, before, after, core_out, chip_out, wide_f, wide_g):
    count = frames.shape[0]
    chans = frames.shape[3]
    lanes = chans // 128
    for t in range(count + 4):
        for h in range(2):
            if t < 2:
                value = before[t, h]
            elif t < count + 2:
                value = frames[t - 2, h]
            else:
                value = after[t - count - 2, h]
            value = value.astype(F32)
            for k in range(lanes):
                wide_f[lanes * h + k, 8 * t : 8 * (t + 1), :] = value[:, 128 * k : 128 * (k + 1)]
    for t in range(count + 2):
        for h in range(2):
            value = (out_grad[t, h] if t < count else after[t - count + 2, h]).astype(F32)
            for k in range(lanes):
                wide_g[lanes * h + k, 8 * t : 8 * (t + 1), :] = value[:, 128 * k : 128 * (k + 1)]
    even_core = place[1] == 0

    def column(source, at, rows):
        return jnp.concatenate(
            [source[k, pl.ds(at, rows, 8), :] for k in range(2 * lanes)], axis=1
        )

    def packed(first, second, grad):
        return jnp.concatenate(
            [
                column(wide_f, first, count + 4),
                column(wide_f, second, count + 4),
                column(wide_g, grad, count + 2),
                jnp.zeros((6, 2 * chans), F32),
            ],
            axis=0,
        )

    left = packed(0, 1, 0)
    right = packed(6, 7, 7)
    core_out[...] = jnp.where(even_core, right, left).astype(BF16)
    chip_out[...] = jnp.where(even_core, left, right).astype(BF16)


def pack(place, frames, out_grad, before, after):
    count, _, cols, chans = frames.shape
    rows = 3 * count + 16
    return pl.pallas_call(
        pack_kernel,
        out_shape=[pltpu.VMEM((rows, 2 * chans), BF16)] * 2,
        in_specs=[SMEM] + [VMEM] * 4,
        out_specs=[VMEM] * 2,
        scratch_shapes=[
            pltpu.VMEM((2 * chans // 128, cols * (count + 4), 128), F32),
            pltpu.VMEM((2 * chans // 128, cols * (count + 2), 128), F32),
        ],
        compiler_params=pltpu.CompilerParams(vmem_limit_bytes=24 * 2**20),
        name="pack",
    )(place, near(frames), near(out_grad), near(before), near(after))


def forward_kernel(
    place,
    lengths,
    frames,
    before,
    after,
    core_sent,
    chip_sent,
    core_got,
    chip_got,
    out_grad,
    down,
    folded,
    latent_out,
    sums_out,
    tail_out,
    low_out,
    high_out,
    grad_out,
    down_block,
    own_low,
    own_high,
    low,
    high,
    even,
    odd,
    total,
    act,
    sems,
):
    chans = frames.shape[-1]
    count = frames.shape[0]
    ahead = count + 2
    rows = 8 * ahead
    fetch_down = pltpu.make_async_copy(down, down_block, sems.at[0])
    fetch_down.start()
    even_core = place[1] == 0

    def pick(core, chip, at_low, at_high):
        core, chip = core[...].astype(F32), chip[...].astype(F32)
        at_low[...] = jnp.where(even_core, chip, core)
        at_high[...] = jnp.where(even_core, core, chip)

    pick(core_sent, chip_sent, own_low, own_high)
    pick(core_got, chip_got, low, high)

    def frame_of(t):
        if t < 2:
            part = lambda h: before[t, h]
        elif t < count + 2:
            part = lambda h: frames[t - 2, h]
        else:
            part = lambda h: after[t - count - 2, h]
        return jnp.concatenate([part(0).astype(F32), part(1).astype(F32)], axis=1)

    span = count + 4

    def rim(side, off):
        left = ((low, 0), (low, span), (own_low, 0))[side]
        right = ((own_high, span), (high, 0), (high, span))[side]
        return jnp.concatenate(
            [ref[at + off : at + off + ahead + 6, :] for ref, at in (left, right)], axis=0
        ).astype(BF16)

    build_centre(frame_of, span, even, odd)
    def weight_of(off, side):
        return folded[3 * off + side]

    def gates(pre):
        gate = 0.5 * jnp.tanh(0.5 * pre) + 0.5
        return gate, gate * (1.0 + pre * (1.0 - gate))

    def finish(first, last):
        for j in range(first, last):
            pre = total[64 * j : 64 * (j + 1), :]
            gate, slope = gates(pre)
            silu = pre * gate
            for h in range(2):
                lanes = slice(h * chans, (h + 1) * chans)
                own = frames[8 * j : 8 * (j + 1), h].astype(F32)
                act[j, :, :, lanes] = own + silu[:, lanes].reshape(own.shape)
                grad = out_grad[8 * j : 8 * (j + 1), h].astype(F32)
                grad = grad * slope[:, lanes].reshape(own.shape)
                grad_out[8 * j : 8 * (j + 1), :, lanes] = grad.astype(BF16)

    half = 64 * (count // 16)
    sum_taps(total, 0, half, (1,), even, odd, weight_of, NN)
    build_sides(
        frame_of,
        lambda t: low[span + t : span + t + 1, :],
        lambda t: high[t : t + 1, :],
        span,
        even,
        odd,
    )
    sum_taps(total, 0, half, (0, 2), even, odd, weight_of, NN)
    sum_taps(total, half, rows - half, (1, 0, 2), even, odd, weight_of, NN, rim)
    finish(0, count // 16)
    finish(count // 16, count // 8)
    for t in range(2):
        at = 8 * (count + t)
        _, slope = gates(total[at : at + 8, :])
        grad = jnp.concatenate([after[2 + t, 0].astype(F32), after[2 + t, 1].astype(F32)], axis=1)
        grad_out[count + t] = (grad * slope).astype(BF16)
    for at, (source, target) in enumerate(((low, low_out), (high, high_out))):
        base = rows + at * (ahead + 6)
        _, slope = gates(total[base : base + ahead + 6, :])
        target[...] = slope * source[2 * span : 2 * span + ahead + 6, :]

    fetch_down.wait()
    latent = jnp.zeros((2 * count, chans), F32)
    for k in range(8):
        lhs = jnp.concatenate(
            [
                act[:, k, :, h * chans : (h + 1) * chans].reshape(count, chans)
                for h in range(2)
            ],
            axis=0,
        ).astype(BF16)
        latent = latent + dot(lhs, down_block[k])
    latent = latent.astype(BF16).astype(F32)
    rounded = [
        jnp.concatenate([latent[8 * j : 8 * j + 8], latent[count + 8 * j : count + 8 * j + 8]], 0)
        for j in range(count // 8)
    ]
    running = jnp.zeros_like(rounded[0])
    for j in range(count // 8):
        now = place[0] * (count // 8) + j
        start = jnp.int32(0)
        begins = jnp.int32(0)
        for k in range(lengths.shape[0]):
            begins = jnp.where(start == now, 1, begins)
            start = start + lengths[k]
        running = jnp.where(begins > 0, rounded[j], running + rounded[j])
        sums_out[j] = running
        latent_out[j] = rounded[j]
    for k in range(tail_out.shape[0]):
        tail_out[k] = running


def forward(peers, place, lengths, frames, before, after, columns, out_grad, down, folded):
    count, _, cols, chans = frames.shape
    wide = 2 * chans
    lat = count // 8
    ahead = count + 2
    rows = cols * ahead
    received = columns[0].shape
    return pl.pallas_call(
        forward_kernel,
        out_shape=(
            pltpu.VMEM((lat, 16, chans), F32),
            pltpu.VMEM((lat, 16, chans), F32),
            pltpu.VMEM((peers, 16, chans), F32),
            pltpu.VMEM((ahead + 6, wide), F32),
            pltpu.VMEM((ahead + 6, wide), F32),
            pltpu.VMEM((ahead, cols, wide), BF16),
        ),
        in_specs=[SMEM, SMEM] + [VMEM] * 8 + [ANY, VMEM],
        out_specs=[VMEM] * 6,
        scratch_shapes=[
            pltpu.VMEM(down.shape, BF16),
            pltpu.VMEM(received, F32),
            pltpu.VMEM(received, F32),
            pltpu.VMEM(received, F32),
            pltpu.VMEM(received, F32),
            pltpu.VMEM((3, rows + 16, wide), BF16),
            pltpu.VMEM((3, rows, wide), BF16),
            pltpu.VMEM((rows + 2 * (ahead + 6), wide), F32),
            pltpu.VMEM((lat, 8, cols, wide), F32),
            pltpu.SemaphoreType.DMA((1,)),
        ],
        compiler_params=pltpu.CompilerParams(vmem_limit_bytes=28 * 2**20),
        cost_estimate=pl.CostEstimate(
            flops=2 * 9 * rows * wide * wide, bytes_accessed=16 * 2**20, transcendentals=rows * wide
        ),
        name="forward",
    )(
        place,
        lengths,
        *(near(value) for value in (frames, before, after, *columns, out_grad)),
        down,
        near(folded),
    )


def backward_kernel(
    grad,
    low,
    high,
    out_grad,
    folded,
    result,
    done,
    even,
    odd,
    total,
    sems,
):
    count, _, cols, chans = out_grad.shape

    def frame_of(t):
        return grad[t]

    def weight_of(off, side):
        return folded[3 * (2 - off) + 2 - side]

    writes = []
    half = count // 2

    def finish(first, last):
        for j in range(first, last, 8):
            part = total[8 * j : 8 * (j + 8), :]
            for h in range(2):
                mine = part[:, h * chans : (h + 1) * chans].reshape(8, cols, chans)
                done[j : j + 8, h] = (out_grad[j : j + 8, h].astype(F32) + mine).astype(BF16)
        write = pltpu.make_async_copy(
            done.at[pl.ds(first, last - first)],
            result.at[pl.ds(first, last - first)],
            sems.at[len(writes)],
        )
        write.start()
        writes.append(write)

    build_centre(frame_of, count + 2, even, odd)
    sum_taps(total, 0, 8 * half, (1,), even, odd, weight_of, NT)
    build_sides(
        frame_of,
        lambda t: low[t : t + 1, :],
        lambda t: high[t : t + 1, :],
        count + 2,
        even,
        odd,
    )
    sum_taps(total, 0, 8 * half, (0, 2), even, odd, weight_of, NT)
    sum_taps(total, 8 * half, 8 * half, (1, 0, 2), even, odd, weight_of, NT)
    finish(0, half)
    finish(half, half + half // 2)
    finish(half + half // 2, count)
    for write in writes:
        write.wait()


def backward(grad, low, high, out_grad, folded):
    count, _, cols, chans = out_grad.shape
    rows, wide = count * cols, 2 * chans
    return pl.pallas_call(
        backward_kernel,
        out_shape=jax.ShapeDtypeStruct(out_grad.shape, BF16),
        in_specs=[VMEM] * 5,
        out_specs=ANY,
        scratch_shapes=[
            pltpu.VMEM(out_grad.shape, BF16),
            pltpu.VMEM((3, rows + 16, wide), BF16),
            pltpu.VMEM((3, rows, wide), BF16),
            pltpu.VMEM((rows, wide), F32),
            pltpu.SemaphoreType.DMA((3,)),
        ],
        compiler_params=pltpu.CompilerParams(vmem_limit_bytes=24 * 2**20),
        cost_estimate=pl.CostEstimate(
            flops=2 * 9 * rows * wide * wide, bytes_accessed=12 * 2**20, transcendentals=0
        ),
        name="backward",
    )(*(near(value) for value in (grad, low, high, out_grad, folded)))


def mix_kernel(place, lengths, latent, sums, tails, mixed):
    lat = latent.shape[0]
    peers = tails.shape[0]
    me = place[0]
    starts = [jnp.int32(0)]
    for k in range(lengths.shape[0] - 1):
        starts.append(starts[-1] + lengths[k])
    opened = jnp.int32(0)
    for start in starts:
        opened = jnp.where(start < me * lat, jnp.maximum(start, opened), opened)
    carried = jnp.zeros(latent.shape[1:], F32)
    for k in range(peers):
        counts = jnp.logical_and(k < me, (k + 1) * lat > opened)
        carried = carried + jnp.where(counts, tails[k], 0.0)
    for j in range(lat):
        now = me * lat + j
        begin = jnp.int32(0)
        for start in starts:
            begin = jnp.where(start <= now, jnp.maximum(start, begin), begin)
        shot = sums[j] + jnp.where(begin < me * lat, carried, 0.0)
        length = jnp.full(shot.shape, now - begin + 1, jnp.int32).astype(F32)
        mixed[16 * j : 16 * (j + 1), :] = (latent[j] + shot / length).astype(BF16)


def mix(place, lengths, latent, sums, tails):
    return pl.pallas_call(
        mix_kernel,
        out_shape=jax.ShapeDtypeStruct((latent.shape[0] * 16, latent.shape[2]), BF16),
        in_specs=[SMEM, SMEM, VMEM, VMEM, VMEM],
        out_specs=VMEM,
        compiler_params=pltpu.CompilerParams(vmem_limit_bytes=16 * 2**20),
        name="mix",
    )(place, lengths, near(latent), near(sums), near(tails))


def attend_kernel(labels, *refs):
    pieces, (w_query, w_key, w_value, w_out, result, keys, values) = refs[:-7], refs[-7:]
    mine = pieces[0]
    tokens, chans = mine.shape
    lat = labels.shape[0]
    per = tokens // lat
    heads = chans // HEAD
    group = len(pieces) // 2
    for first in range(0, len(pieces), group):
        block = jnp.concatenate([piece[...] for piece in pieces[first : first + group]], axis=0)
        for weight, target in ((w_key, keys), (w_value, values)):
            made = dot(block, weight[...]).astype(BF16)
            for k in range(group):
                for j in range(lat):
                    row = tokens * k + per * j
                    at = per * (first + k)
                    target[j, at : at + per, :] = made[row : row + per, :]
    query = dot(mine[...], w_query[...]).astype(BF16).astype(F32) * (1.0 / math.sqrt(HEAD))
    head_of = lax.broadcasted_iota(jnp.int32, (per, chans), 1) // HEAD
    partners, scores = [], []
    for j in range(lat):
        partner = jnp.int32(-1)
        for k in range(j):
            partner = jnp.where(labels[k, 0] == labels[j, 0], k, partner)
        partners.append(jnp.maximum(partner, 0))
        own = query[per * j : per * (j + 1), :]
        stacked = jnp.concatenate(
            [jnp.where(head_of == h, own, 0.0) for h in range(heads)], axis=0
        ).astype(BF16)
        bias = jnp.where(partner >= 0, 0.0, -1e30).astype(F32)
        both = jnp.concatenate([keys[j], keys[partners[j]]], axis=0)
        made = dot(stacked, both, NT)
        half = made.shape[1] // 2
        scores.append(jnp.concatenate([made[:, :half], made[:, half:] + bias], axis=1))
    weights, norms = [], []
    for j in range(lat):
        expo = jnp.exp(scores[j] - jnp.max(scores[j], axis=1, keepdims=True))
        norms.append(jnp.sum(expo, axis=1, keepdims=True))
        weights.append(expo.astype(BF16))
    mixes = []
    for j in range(lat):
        both = jnp.concatenate([values[j], values[partners[j]]], axis=0)
        mixes.append(dot(weights[j], both))
    outs = []
    for j in range(lat):
        mixed = mixes[j] / norms[j]
        total = jnp.zeros((per, chans), F32)
        for h in range(heads):
            total = jnp.where(head_of == h, mixed[per * h : per * (h + 1), :], total)
        outs.append(total)
    attended = jnp.concatenate(outs, axis=0).astype(BF16)
    final = mine[...].astype(F32) + dot(attended, w_out[...])
    for j in range(lat):
        for h in range(2):
            at = per * j + 8 * h
            result[j, h] = final[at : at + 8].astype(BF16)


def attend(labels, pieces, w_query, w_key, w_value, w_out):
    tokens, chans = pieces[0].shape
    lat = labels.shape[0]
    held = (lat, len(pieces) * tokens // lat, chans)
    return pl.pallas_call(
        attend_kernel,
        out_shape=jax.ShapeDtypeStruct((lat, 2, 8, chans), BF16),
        in_specs=[SMEM] + [VMEM] * (4 + len(pieces)),
        out_specs=VMEM,
        scratch_shapes=[pltpu.VMEM(held, BF16), pltpu.VMEM(held, BF16)],
        compiler_params=pltpu.CompilerParams(vmem_limit_bytes=24 * 2**20),
        name="attend",
    )(labels, *(near(piece) for piece in pieces), w_query, w_key, w_value, w_out)


def shifted(value, axis, steps):
    count = lax.axis_size(axis)
    return lax.ppermute(
        value, axis, [(i, i + steps) for i in range(count) if 0 <= i + steps < count]
    )


def with_core(value):
    count = lax.axis_size("scene")
    return lax.ppermute(value, "scene", [(i, i ^ 1) for i in range(count)])


def with_chip(value):
    count = lax.axis_size("scene")
    pairs = [(i, i + 1) for i in range(1, count - 1, 2)]
    return lax.ppermute(value, "scene", pairs + [(b, a) for a, b in pairs])


def chip_shifts(value):
    count = lax.axis_size("scene")
    return [
        lax.ppermute(value, "scene", [(i, (i + 2 * k) % count) for i in range(count)])
        for k in range(1, count // 2)
    ]


def per_device(
    frames,
    conv_weight,
    down_weight,
    w_query,
    w_key,
    w_value,
    w_out,
    shot_lengths,
    scene_label,
    out_grad,
):
    count = frames.shape[0]
    place = jnp.stack([lax.axis_index("tm"), lax.axis_index("scene") % 2]).astype(jnp.int32)
    before = shifted(frames[count - 2 :], "tm", 1)
    after = shifted(jnp.concatenate([frames[:2], out_grad[:2]], axis=0), "tm", -1)
    near_frames, near_grad, near_weight = fetch(frames, out_grad, conv_weight)
    (before, after), near_weight = lax.optimization_barrier(((before, after), near_weight))
    sent = pack(place, near_frames, near_grad, before, after)
    received = (with_core(sent[0]), with_chip(sent[1]))
    received, folded = lax.optimization_barrier((received, fold(near_weight)))
    latent, sums, tail, low, high, grad = forward(
        lax.axis_size("tm"),
        place,
        shot_lengths,
        near_frames,
        before,
        after,
        (*sent, *received),
        near_grad,
        down_weight,
        folded,
    )
    tails = lax.all_to_all(tail, "tm", 0, 0, tiled=True)
    mixed = mix(place, shot_lengths, latent, sums, tails)
    chips = chip_shifts(mixed)
    beside = with_core(mixed)
    frame_grad = backward(grad, low, high, near_grad, folded)
    (chips, beside), frame_grad = lax.optimization_barrier(((chips, beside), frame_grad))
    pieces = [mixed, *chips, beside, *(with_core(piece) for piece in chips)]
    latent_out = attend(scene_label, pieces, w_query, w_key, w_value, w_out)
    return (latent_out, frame_grad)


def solution(mesh):
    in_specs = (
        P("tm", None, "scene", None),
        P(),
        P(),
        P(),
        P(),
        P(),
        P(),
        P(),
        P("tm", None),
        P("tm", None, "scene", None),
    )
    out_specs = (P("tm", None, "scene", None), P("tm", None, "scene", None))
    return jax.shard_map(
        per_device, mesh=mesh, in_specs=in_specs, out_specs=out_specs, check_vma=False
    )
```

```python
import math

import jax
import jax.numpy as jnp
from jax import lax
from jax.experimental import pallas as pl
from jax.experimental.pallas import tpu as pltpu
from jax.sharding import PartitionSpec as P

HEAD = 64
BF16 = jnp.bfloat16
F32 = jnp.float32
VMEM = pl.BlockSpec(memory_space=pltpu.VMEM)
SMEM = pl.BlockSpec(memory_space=pltpu.SMEM)
ANY = pl.BlockSpec(memory_space=pl.ANY)
NT = (((1,), (1,)), ((), ()))
NN = (((1,), (0,)), ((), ()))

def near(value):
    return pltpu.with_memory_space_constraint(value, pltpu.VMEM)


def dot(a, b, dims=NN):
    return lax.dot_general(a, b, dims, preferred_element_type=F32)


def fetch_kernel(frames, out_grad, weight, frames_out, grad_out, weight_out, sems):
    copies = [
        pltpu.make_async_copy(source, target, sems.at[k])
        for k, (source, target) in enumerate(
            ((frames, frames_out), (out_grad, grad_out), (weight, weight_out))
        )
    ]
    for copy in copies:
        copy.start()
    for copy in copies:
        copy.wait()


def fetch(frames, out_grad, weight):
    return pl.pallas_call(
        fetch_kernel,
        out_shape=[pltpu.VMEM(value.shape, BF16) for value in (frames, out_grad, weight)],
        in_specs=[ANY] * 3,
        out_specs=[VMEM] * 3,
        scratch_shapes=[pltpu.SemaphoreType.DMA((3,))],
        compiler_params=pltpu.CompilerParams(vmem_limit_bytes=48 * 2**20),
        cost_estimate=pl.CostEstimate(
            flops=0, bytes_accessed=20 * 2**20, transcendentals=0
        ),
        name="fetch",
    )(frames, out_grad, weight)


def fold_kernel(weight, folded, sems):
    chans = weight.shape[-1]
    copies = []
    for k in range(9):
        for h_in in range(2):
            for h_out in range(2):
                copies.append(
                    pltpu.make_async_copy(
                        weight.at[k // 3, h_in - h_out + 1, k % 3],
                        folded.at[k, pl.ds(h_in * chans, chans), pl.ds(h_out * chans, chans)],
                        sems.at[k, 2 * h_in + h_out],
                    )
                )
    for copy in copies:
        copy.start()
    for copy in copies:
        copy.wait()


def fold(weight):
    wide = 2 * weight.shape[-1]
    return pl.pallas_call(
        fold_kernel,
        out_shape=pltpu.VMEM((9, wide, wide), BF16),
        in_specs=[VMEM],
        out_specs=VMEM,
        scratch_shapes=[pltpu.SemaphoreType.DMA((9, 4))],
        compiler_params=pltpu.CompilerParams(vmem_limit_bytes=4 * 2**20),
        cost_estimate=pl.CostEstimate(
            flops=0, bytes_accessed=20 * 2**20, transcendentals=0
        ),
        name="fold",
    )(near(weight))


def store_pairs(values_of, sides, count, even, odd):
    before = None
    for t in range(count):
        now = values_of(t)
        for at, s in enumerate(sides):
            if t % 2 == 1:
                pair = jnp.concatenate([before[at], now[at]], axis=0).astype(BF16)
                even[s, 8 * (t - 1) : 8 * (t + 1), :] = pair
            elif t > 0:
                pair = jnp.concatenate([before[at], now[at]], axis=0).astype(BF16)
                odd[s, 8 * (t - 2) : 8 * t, :] = pair
        before = now


def build_centre(frame_of, count, even, odd):
    store_pairs(lambda t: (frame_of(t).astype(F32),), (1,), count, even, odd)


def build_sides(frame_of, low_of, high_of, count, even, odd):
    width = even.shape[2]
    sub = lax.broadcasted_iota(jnp.int32, (8, width), 0)

    def both(t):
        own = frame_of(t).astype(F32)
        left = jnp.where(sub == 0, jnp.broadcast_to(low_of(t), (8, width)), pltpu.roll(own, 1, 0))
        right = jnp.where(sub == 7, jnp.broadcast_to(high_of(t), (8, width)), pltpu.roll(own, 7, 0))
        return left, right

    store_pairs(both, (0, 2), count, even, odd)


def sum_taps(total, at, rows, sides, even, odd, weight_of, dims, extra=None):
    count = rows
    for side in sides:
        for off in range(3):
            if off == 1:
                lhs = odd[side, at : at + rows, :]
            else:
                lhs = even[side, at + 8 * off : at + 8 * off + rows, :]
            if extra is not None:
                lhs = jnp.concatenate([lhs, extra(side, off)], axis=0)
                count = lhs.shape[0]
            part = dot(lhs, weight_of(off, side), dims)
            if (side, off) == (1, 0):
                total[at : at + count, :] = part
            else:
                total[at : at + count, :] += part


def pack_kernel(place, frames, out_grad, before, after, core_out, chip_out, wide_f, wide_g):
    count = frames.shape[0]
    chans = frames.shape[3]
    lanes = chans // 128
    for t in range(count + 4):
        for h in range(2):
            if t < 2:
                value = before[t, h]
            elif t < count + 2:
                value = frames[t - 2, h]
            else:
                value = after[t - count - 2, h]
            value = value.astype(F32)
            for k in range(lanes):
                wide_f[lanes * h + k, 8 * t : 8 * (t + 1), :] = value[:, 128 * k : 128 * (k + 1)]
    for t in range(count + 2):
        for h in range(2):
            value = (out_grad[t, h] if t < count else after[t - count + 2, h]).astype(F32)
            for k in range(lanes):
                wide_g[lanes * h + k, 8 * t : 8 * (t + 1), :] = value[:, 128 * k : 128 * (k + 1)]
    even_core = place[1] == 0

    def column(source, at, rows):
        return jnp.concatenate(
            [source[k, pl.ds(at, rows, 8), :] for k in range(2 * lanes)], axis=1
        )

    def packed(first, second, grad):
        return jnp.concatenate(
            [
                column(wide_f, first, count + 4),
                column(wide_f, second, count + 4),
                column(wide_g, grad, count + 2),
                jnp.zeros((6, 2 * chans), F32),
            ],
            axis=0,
        )

    left = packed(0, 1, 0)
    right = packed(6, 7, 7)
    core_out[...] = jnp.where(even_core, right, left).astype(BF16)
    chip_out[...] = jnp.where(even_core, left, right).astype(BF16)


def pack(place, frames, out_grad, before, after):
    count, _, cols, chans = frames.shape
    rows = 3 * count + 16
    return pl.pallas_call(
        pack_kernel,
        out_shape=[pltpu.VMEM((rows, 2 * chans), BF16)] * 2,
        in_specs=[SMEM] + [VMEM] * 4,
        out_specs=[VMEM] * 2,
        scratch_shapes=[
            pltpu.VMEM((2 * chans // 128, cols * (count + 4), 128), F32),
            pltpu.VMEM((2 * chans // 128, cols * (count + 2), 128), F32),
        ],
        compiler_params=pltpu.CompilerParams(vmem_limit_bytes=12 * 2**20),
        name="pack",
    )(place, near(frames), near(out_grad), near(before), near(after))


def joined_frames(frames, before, after):
    count = frames.shape[0]

    def frame_of(t):
        if t < 2:
            part = lambda h: before[t, h]
        elif t < count + 2:
            part = lambda h: frames[t - 2, h]
        else:
            part = lambda h: after[t - count - 2, h]
        return jnp.concatenate([part(0).astype(F32), part(1).astype(F32)], axis=1)

    return frame_of


def centre_kernel(frames, before, after, folded, total, even, odd):
    build_centre(joined_frames(frames, before, after), frames.shape[0] + 4, even, odd)
    rows = total.shape[0]

    def weight_of(off, side):
        return folded[3 * off + side]

    sum_taps(total, 0, rows, (1,), even, odd, weight_of, NN)


def centre(frames, before, after, folded):
    count, _, cols, chans = frames.shape
    rows, wide = cols * (count + 2), 2 * chans
    return pl.pallas_call(
        centre_kernel,
        out_shape=pltpu.VMEM((rows, wide), F32),
        in_specs=[VMEM] * 4,
        out_specs=VMEM,
        scratch_shapes=[
            pltpu.VMEM((3, rows + 16, wide), BF16),
            pltpu.VMEM((3, rows, wide), BF16),
        ],
        compiler_params=pltpu.CompilerParams(vmem_limit_bytes=10 * 2**20),
        cost_estimate=pl.CostEstimate(
            flops=2 * 3 * rows * wide * wide, bytes_accessed=6 * 2**20, transcendentals=0
        ),
        name="centre",
    )(*(near(value) for value in (frames, before, after, folded)))


def forward_kernel(
    place,
    lengths,
    frames,
    before,
    after,
    core_sent,
    chip_sent,
    core_got,
    chip_got,
    out_grad,
    middle,
    down,
    folded,
    latent_out,
    sums_out,
    tail_out,
    low_out,
    high_out,
    grad_out,
    down_block,
    own_low,
    own_high,
    low,
    high,
    even,
    odd,
    total,
    act,
    sems,
):
    chans = frames.shape[-1]
    count = frames.shape[0]
    ahead = count + 2
    rows = 8 * ahead
    fetch_down = pltpu.make_async_copy(down, down_block, sems.at[0])
    fetch_down.start()
    even_core = place[1] == 0

    def pick(core, chip, at_low, at_high):
        core, chip = core[...].astype(F32), chip[...].astype(F32)
        at_low[...] = jnp.where(even_core, chip, core)
        at_high[...] = jnp.where(even_core, core, chip)

    pick(core_sent, chip_sent, own_low, own_high)
    pick(core_got, chip_got, low, high)

    frame_of = joined_frames(frames, before, after)
    span = count + 4

    def rim(side, off):
        left = ((low, 0), (low, span), (own_low, 0))[side]
        right = ((own_high, span), (high, 0), (high, span))[side]
        return jnp.concatenate(
            [ref[at + off : at + off + ahead + 6, :] for ref, at in (left, right)], axis=0
        ).astype(BF16)

    def weight_of(off, side):
        return folded[3 * off + side]

    def gates(pre):
        gate = 0.5 * jnp.tanh(0.5 * pre) + 0.5
        return gate, gate * (1.0 + pre * (1.0 - gate))

    def finish(first, last):
        for j in range(first, last):
            pre = total[64 * j : 64 * (j + 1), :]
            gate, slope = gates(pre)
            silu = pre * gate
            for h in range(2):
                lanes = slice(h * chans, (h + 1) * chans)
                own = frames[8 * j : 8 * (j + 1), h].astype(F32)
                act[j, :, :, lanes] = own + silu[:, lanes].reshape(own.shape)
                grad = out_grad[8 * j : 8 * (j + 1), h].astype(F32)
                grad = grad * slope[:, lanes].reshape(own.shape)
                grad_out[8 * j : 8 * (j + 1), :, lanes] = grad.astype(BF16)

    half = 64 * (count // 16)
    total[0:rows, :] = middle[...]
    build_sides(
        frame_of,
        lambda t: low[span + t : span + t + 1, :],
        lambda t: high[t : t + 1, :],
        span,
        even,
        odd,
    )
    edges = dot(rim(1, 0), folded[1])
    edges += dot(rim(1, 1), folded[4])
    edges += dot(rim(1, 2), folded[7])
    total[rows:, :] = edges
    sum_taps(total, 0, half, (0, 2), even, odd, weight_of, NN)
    sum_taps(total, half, rows - half, (0, 2), even, odd, weight_of, NN, rim)
    finish(0, count // 16)
    finish(count // 16, count // 8)
    for t in range(2):
        at = 8 * (count + t)
        _, slope = gates(total[at : at + 8, :])
        grad = jnp.concatenate([after[2 + t, 0].astype(F32), after[2 + t, 1].astype(F32)], axis=1)
        grad_out[count + t] = (grad * slope).astype(BF16)
    for at, (source, target) in enumerate(((low, low_out), (high, high_out))):
        base = rows + at * (ahead + 6)
        _, slope = gates(total[base : base + ahead + 6, :])
        target[...] = slope * source[2 * span : 2 * span + ahead + 6, :]

    fetch_down.wait()
    latent = jnp.zeros((2 * count, chans), F32)
    for k in range(8):
        lhs = jnp.concatenate(
            [
                act[:, k, :, h * chans : (h + 1) * chans].reshape(count, chans)
                for h in range(2)
            ],
            axis=0,
        ).astype(BF16)
        latent = latent + dot(lhs, down_block[k])
    latent = latent.astype(BF16).astype(F32)
    rounded = [
        jnp.concatenate([latent[8 * j : 8 * j + 8], latent[count + 8 * j : count + 8 * j + 8]], 0)
        for j in range(count // 8)
    ]
    running = jnp.zeros_like(rounded[0])
    for j in range(count // 8):
        now = place[0] * (count // 8) + j
        start = jnp.int32(0)
        begins = jnp.int32(0)
        for k in range(lengths.shape[0]):
            begins = jnp.where(start == now, 1, begins)
            start = start + lengths[k]
        running = jnp.where(begins > 0, rounded[j], running + rounded[j])
        sums_out[j] = running
        latent_out[j] = rounded[j]
    for k in range(tail_out.shape[0]):
        tail_out[k] = running


def forward(
    peers, place, lengths, frames, before, after, columns, out_grad, middle, down, folded
):
    count, _, cols, chans = frames.shape
    wide = 2 * chans
    lat = count // 8
    ahead = count + 2
    rows = cols * ahead
    received = columns[0].shape
    return pl.pallas_call(
        forward_kernel,
        out_shape=(
            pltpu.VMEM((lat, 16, chans), F32),
            pltpu.VMEM((lat, 16, chans), F32),
            pltpu.VMEM((peers, 16, chans), F32),
            pltpu.VMEM((ahead + 6, wide), F32),
            pltpu.VMEM((ahead + 6, wide), F32),
            pltpu.VMEM((ahead, cols, wide), BF16),
        ),
        in_specs=[SMEM, SMEM] + [VMEM] * 9 + [ANY, VMEM],
        out_specs=[VMEM] * 6,
        scratch_shapes=[
            pltpu.VMEM(down.shape, BF16),
            pltpu.VMEM(received, F32),
            pltpu.VMEM(received, F32),
            pltpu.VMEM(received, F32),
            pltpu.VMEM(received, F32),
            pltpu.VMEM((3, rows + 16, wide), BF16),
            pltpu.VMEM((3, rows, wide), BF16),
            pltpu.VMEM((rows + 2 * (ahead + 6), wide), F32),
            pltpu.VMEM((lat, 8, cols, wide), F32),
            pltpu.SemaphoreType.DMA((1,)),
        ],
        compiler_params=pltpu.CompilerParams(vmem_limit_bytes=22 * 2**20),
        cost_estimate=pl.CostEstimate(
            flops=2 * 9 * rows * wide * wide, bytes_accessed=16 * 2**20, transcendentals=rows * wide
        ),
        name="forward",
    )(
        place,
        lengths,
        *(near(value) for value in (frames, before, after, *columns, out_grad, middle)),
        down,
        near(folded),
    )


def backward_kernel(
    grad,
    low,
    high,
    out_grad,
    folded,
    result,
    done,
    even,
    odd,
    total,
    sems,
):
    count, _, cols, chans = out_grad.shape

    def frame_of(t):
        return grad[t]

    def weight_of(off, side):
        return folded[3 * (2 - off) + 2 - side]

    writes = []
    half = count // 2

    def finish(first, last):
        for j in range(first, last, 8):
            part = total[8 * j : 8 * (j + 8), :]
            for h in range(2):
                mine = part[:, h * chans : (h + 1) * chans].reshape(8, cols, chans)
                done[j : j + 8, h] = (out_grad[j : j + 8, h].astype(F32) + mine).astype(BF16)
        write = pltpu.make_async_copy(
            done.at[pl.ds(first, last - first)],
            result.at[pl.ds(first, last - first)],
            sems.at[len(writes)],
        )
        write.start()
        writes.append(write)

    build_centre(frame_of, count + 2, even, odd)
    sum_taps(total, 0, 8 * half, (1,), even, odd, weight_of, NT)
    build_sides(
        frame_of,
        lambda t: low[t : t + 1, :],
        lambda t: high[t : t + 1, :],
        count + 2,
        even,
        odd,
    )
    sum_taps(total, 0, 8 * half, (0, 2), even, odd, weight_of, NT)
    sum_taps(total, 8 * half, 8 * half, (1, 0, 2), even, odd, weight_of, NT)
    finish(0, half)
    finish(half, half + half // 2)
    finish(half + half // 2, count)
    for write in writes:
        write.wait()


def backward(grad, low, high, out_grad, folded):
    count, _, cols, chans = out_grad.shape
    rows, wide = count * cols, 2 * chans
    return pl.pallas_call(
        backward_kernel,
        out_shape=jax.ShapeDtypeStruct(out_grad.shape, BF16),
        in_specs=[VMEM] * 5,
        out_specs=ANY,
        scratch_shapes=[
            pltpu.VMEM(out_grad.shape, BF16),
            pltpu.VMEM((3, rows + 16, wide), BF16),
            pltpu.VMEM((3, rows, wide), BF16),
            pltpu.VMEM((rows, wide), F32),
            pltpu.SemaphoreType.DMA((3,)),
        ],
        compiler_params=pltpu.CompilerParams(vmem_limit_bytes=24 * 2**20),
        cost_estimate=pl.CostEstimate(
            flops=2 * 9 * rows * wide * wide, bytes_accessed=12 * 2**20, transcendentals=0
        ),
        name="backward",
    )(*(near(value) for value in (grad, low, high, out_grad, folded)))


def mix_kernel(place, lengths, latent, sums, tails, mixed):
    lat = latent.shape[0]
    peers = tails.shape[0]
    me = place[0]
    starts = [jnp.int32(0)]
    for k in range(lengths.shape[0] - 1):
        starts.append(starts[-1] + lengths[k])
    opened = jnp.int32(0)
    for start in starts:
        opened = jnp.where(start < me * lat, jnp.maximum(start, opened), opened)
    carried = jnp.zeros(latent.shape[1:], F32)
    for k in range(peers):
        counts = jnp.logical_and(k < me, (k + 1) * lat > opened)
        carried = carried + jnp.where(counts, tails[k], 0.0)
    for j in range(lat):
        now = me * lat + j
        begin = jnp.int32(0)
        for start in starts:
            begin = jnp.where(start <= now, jnp.maximum(start, begin), begin)
        shot = sums[j] + jnp.where(begin < me * lat, carried, 0.0)
        length = jnp.full(shot.shape, now - begin + 1, jnp.int32).astype(F32)
        mixed[16 * j : 16 * (j + 1), :] = (latent[j] + shot / length).astype(BF16)


def mix(place, lengths, latent, sums, tails):
    return pl.pallas_call(
        mix_kernel,
        out_shape=jax.ShapeDtypeStruct((latent.shape[0] * 16, latent.shape[2]), BF16),
        in_specs=[SMEM, SMEM, VMEM, VMEM, VMEM],
        out_specs=VMEM,
        compiler_params=pltpu.CompilerParams(vmem_limit_bytes=16 * 2**20),
        name="mix",
    )(place, lengths, near(latent), near(sums), near(tails))


def attend_kernel(labels, *refs):
    pieces, (w_query, w_key, w_value, w_out, result, keys, values) = refs[:-7], refs[-7:]
    mine = pieces[0]
    tokens, chans = mine.shape
    lat = labels.shape[0]
    per = tokens // lat
    heads = chans // HEAD
    group = len(pieces) // 2
    for first in range(0, len(pieces), group):
        block = jnp.concatenate([piece[...] for piece in pieces[first : first + group]], axis=0)
        for weight, target in ((w_key, keys), (w_value, values)):
            made = dot(block, weight[...]).astype(BF16)
            for k in range(group):
                for j in range(lat):
                    row = tokens * k + per * j
                    at = per * (first + k)
                    target[j, at : at + per, :] = made[row : row + per, :]
    query = dot(mine[...], w_query[...]).astype(BF16).astype(F32) * (1.0 / math.sqrt(HEAD))
    head_of = lax.broadcasted_iota(jnp.int32, (per, chans), 1) // HEAD
    partners, scores = [], []
    for j in range(lat):
        partner = jnp.int32(-1)
        for k in range(j):
            partner = jnp.where(labels[k, 0] == labels[j, 0], k, partner)
        partners.append(jnp.maximum(partner, 0))
        own = query[per * j : per * (j + 1), :]
        stacked = jnp.concatenate(
            [jnp.where(head_of == h, own, 0.0) for h in range(heads)], axis=0
        ).astype(BF16)
        bias = jnp.where(partner >= 0, 0.0, -1e30).astype(F32)
        both = jnp.concatenate([keys[j], keys[partners[j]]], axis=0)
        made = dot(stacked, both, NT)
        half = made.shape[1] // 2
        scores.append(jnp.concatenate([made[:, :half], made[:, half:] + bias], axis=1))
    weights, norms = [], []
    for j in range(lat):
        expo = jnp.exp(scores[j] - jnp.max(scores[j], axis=1, keepdims=True))
        norms.append(jnp.sum(expo, axis=1, keepdims=True))
        weights.append(expo.astype(BF16))
    mixes = []
    for j in range(lat):
        both = jnp.concatenate([values[j], values[partners[j]]], axis=0)
        mixes.append(dot(weights[j], both))
    outs = []
    for j in range(lat):
        mixed = mixes[j] / norms[j]
        total = jnp.zeros((per, chans), F32)
        for h in range(heads):
            total = jnp.where(head_of == h, mixed[per * h : per * (h + 1), :], total)
        outs.append(total)
    attended = jnp.concatenate(outs, axis=0).astype(BF16)
    final = mine[...].astype(F32) + dot(attended, w_out[...])
    for j in range(lat):
        for h in range(2):
            at = per * j + 8 * h
            result[j, h] = final[at : at + 8].astype(BF16)


def attend(labels, pieces, w_query, w_key, w_value, w_out):
    tokens, chans = pieces[0].shape
    lat = labels.shape[0]
    held = (lat, len(pieces) * tokens // lat, chans)
    return pl.pallas_call(
        attend_kernel,
        out_shape=jax.ShapeDtypeStruct((lat, 2, 8, chans), BF16),
        in_specs=[SMEM] + [VMEM] * (4 + len(pieces)),
        out_specs=VMEM,
        scratch_shapes=[pltpu.VMEM(held, BF16), pltpu.VMEM(held, BF16)],
        compiler_params=pltpu.CompilerParams(vmem_limit_bytes=24 * 2**20),
        name="attend",
    )(labels, *(near(piece) for piece in pieces), w_query, w_key, w_value, w_out)


def shifted(value, axis, steps):
    count = lax.axis_size(axis)
    return lax.ppermute(
        value, axis, [(i, i + steps) for i in range(count) if 0 <= i + steps < count]
    )


def with_core(value):
    count = lax.axis_size("scene")
    return lax.ppermute(value, "scene", [(i, i ^ 1) for i in range(count)])


def with_chip(value):
    count = lax.axis_size("scene")
    pairs = [(i, i + 1) for i in range(1, count - 1, 2)]
    return lax.ppermute(value, "scene", pairs + [(b, a) for a, b in pairs])


def chip_shifts(value):
    count = lax.axis_size("scene")
    return [
        lax.ppermute(value, "scene", [(i, (i + 2 * k) % count) for i in range(count)])
        for k in range(1, count // 2)
    ]


def per_device(
    frames,
    conv_weight,
    down_weight,
    w_query,
    w_key,
    w_value,
    w_out,
    shot_lengths,
    scene_label,
    out_grad,
):
    count = frames.shape[0]
    place = jnp.stack([lax.axis_index("tm"), lax.axis_index("scene") % 2]).astype(jnp.int32)
    before = shifted(frames[count - 2 :], "tm", 1)
    after = shifted(jnp.concatenate([frames[:2], out_grad[:2]], axis=0), "tm", -1)
    near_frames, near_grad, near_weight = fetch(frames, out_grad, conv_weight)
    (before, after), near_weight = lax.optimization_barrier(((before, after), near_weight))
    sent = pack(place, near_frames, near_grad, before, after)
    received = (with_core(sent[0]), with_chip(sent[1]))
    folded = fold(near_weight)
    middle = centre(near_frames, before, after, folded)
    received, middle = lax.optimization_barrier((received, middle))
    latent, sums, tail, low, high, grad = forward(
        lax.axis_size("tm"),
        place,
        shot_lengths,
        near_frames,
        before,
        after,
        (*sent, *received),
        near_grad,
        middle,
        down_weight,
        folded,
    )
    tails = lax.all_to_all(tail, "tm", 0, 0, tiled=True)
    mixed = mix(place, shot_lengths, latent, sums, tails)
    chips = chip_shifts(mixed)
    frame_grad = backward(grad, low, high, near_grad, folded)
    chips, frame_grad = lax.optimization_barrier((chips, frame_grad))
    pieces = [mixed, *chips]
    pieces += [with_core(piece) for piece in pieces]
    latent_out = attend(scene_label, pieces, w_query, w_key, w_value, w_out)
    return (latent_out, frame_grad)


def solution(mesh):
    in_specs = (
        P("tm", None, "scene", None),
        P(),
        P(),
        P(),
        P(),
        P(),
        P(),
        P(),
        P("tm", None),
        P("tm", None, "scene", None),
    )
    out_specs = (P("tm", None, "scene", None), P("tm", None, "scene", None))
    return jax.shard_map(
        per_device, mesh=mesh, in_specs=in_specs, out_specs=out_specs, check_vma=False
    )
```

```python
import math

import jax
import jax.numpy as jnp
from jax import lax
from jax.experimental import pallas as pl
from jax.experimental.pallas import tpu as pltpu
from jax.sharding import PartitionSpec as P

HEAD = 64
BF16 = jnp.bfloat16
F32 = jnp.float32
VMEM = pl.BlockSpec(memory_space=pltpu.VMEM)
SMEM = pl.BlockSpec(memory_space=pltpu.SMEM)
ANY = pl.BlockSpec(memory_space=pl.ANY)
NT = (((1,), (1,)), ((), ()))
NN = (((1,), (0,)), ((), ()))

def near(value):
    return pltpu.with_memory_space_constraint(value, pltpu.VMEM)


def dot(a, b, dims=NN):
    return lax.dot_general(a, b, dims, preferred_element_type=F32)


def cut_kernel(frames, out_grad, last, first, sems):
    count = frames.shape[0]
    copies = [
        pltpu.make_async_copy(frames.at[pl.ds(count - 2, 2)], last, sems.at[0]),
        pltpu.make_async_copy(frames.at[pl.ds(0, 2)], first.at[pl.ds(0, 2)], sems.at[1]),
        pltpu.make_async_copy(out_grad.at[pl.ds(0, 2)], first.at[pl.ds(2, 2)], sems.at[2]),
    ]
    for copy in copies:
        copy.start()
    for copy in copies:
        copy.wait()


def cut(frames, out_grad):
    shape = frames.shape[1:]
    return pl.pallas_call(
        cut_kernel,
        out_shape=[pltpu.VMEM((2, *shape), BF16), pltpu.VMEM((4, *shape), BF16)],
        in_specs=[pl.BlockSpec(memory_space=pltpu.HBM)] * 2,
        out_specs=[VMEM] * 2,
        scratch_shapes=[pltpu.SemaphoreType.DMA((3,))],
        compiler_params=pltpu.CompilerParams(vmem_limit_bytes=60 * 2**20),
        name="cut",
    )(frames, out_grad)


def fetch_kernel(frames, out_grad, weight, frames_out, grad_out, weight_out, sems):
    copies = [
        pltpu.make_async_copy(source, target, sems.at[k])
        for k, (source, target) in enumerate(
            ((frames, frames_out), (out_grad, grad_out), (weight, weight_out))
        )
    ]
    for copy in copies:
        copy.start()
    for copy in copies:
        copy.wait()


def fetch(frames, out_grad, weight):
    return pl.pallas_call(
        fetch_kernel,
        out_shape=[pltpu.VMEM(value.shape, BF16) for value in (frames, out_grad, weight)],
        in_specs=[ANY] * 3,
        out_specs=[VMEM] * 3,
        scratch_shapes=[pltpu.SemaphoreType.DMA((3,))],
        compiler_params=pltpu.CompilerParams(vmem_limit_bytes=48 * 2**20),
        cost_estimate=pl.CostEstimate(
            flops=0, bytes_accessed=20 * 2**20, transcendentals=0
        ),
        name="fetch",
    )(frames, out_grad, weight)


def fold_kernel(weight, folded, sems):
    chans = weight.shape[-1]
    copies = []
    for k in range(9):
        for h_in in range(2):
            for h_out in range(2):
                copies.append(
                    pltpu.make_async_copy(
                        weight.at[k // 3, h_in - h_out + 1, k % 3],
                        folded.at[k, pl.ds(h_in * chans, chans), pl.ds(h_out * chans, chans)],
                        sems.at[k, 2 * h_in + h_out],
                    )
                )
    for copy in copies:
        copy.start()
    for copy in copies:
        copy.wait()


def fold(weight):
    wide = 2 * weight.shape[-1]
    return pl.pallas_call(
        fold_kernel,
        out_shape=pltpu.VMEM((9, wide, wide), BF16),
        in_specs=[VMEM],
        out_specs=VMEM,
        scratch_shapes=[pltpu.SemaphoreType.DMA((9, 4))],
        compiler_params=pltpu.CompilerParams(vmem_limit_bytes=4 * 2**20),
        cost_estimate=pl.CostEstimate(
            flops=0, bytes_accessed=20 * 2**20, transcendentals=0
        ),
        name="fold",
    )(near(weight))


def store_pairs(values_of, sides, count, even, odd):
    before = None
    for t in range(count):
        now = values_of(t)
        for at, s in enumerate(sides):
            if t % 2 == 1:
                pair = jnp.concatenate([before[at], now[at]], axis=0).astype(BF16)
                even[s, 8 * (t - 1) : 8 * (t + 1), :] = pair
            elif t > 0:
                pair = jnp.concatenate([before[at], now[at]], axis=0).astype(BF16)
                odd[s, 8 * (t - 2) : 8 * t, :] = pair
        before = now


def build_centre(frame_of, count, even, odd):
    store_pairs(lambda t: (frame_of(t).astype(F32),), (1,), count, even, odd)


def build_sides(frame_of, low_of, high_of, count, even, odd):
    width = even.shape[2]
    sub = lax.broadcasted_iota(jnp.int32, (8, width), 0)

    def both(t):
        own = frame_of(t).astype(F32)
        left = jnp.where(sub == 0, jnp.broadcast_to(low_of(t), (8, width)), pltpu.roll(own, 1, 0))
        right = jnp.where(sub == 7, jnp.broadcast_to(high_of(t), (8, width)), pltpu.roll(own, 7, 0))
        return left, right

    store_pairs(both, (0, 2), count, even, odd)


def sum_taps(total, at, rows, sides, even, odd, weight_of, dims, extra=None):
    count = rows
    for side in sides:
        for off in range(3):
            if off == 1:
                lhs = odd[side, at : at + rows, :]
            else:
                lhs = even[side, at + 8 * off : at + 8 * off + rows, :]
            if extra is not None:
                lhs = jnp.concatenate([lhs, extra(side, off)], axis=0)
                count = lhs.shape[0]
            part = dot(lhs, weight_of(off, side), dims)
            if (side, off) == (1, 0):
                total[at : at + count, :] = part
            else:
                total[at : at + count, :] += part


def pack_kernel(place, frames, out_grad, before, after, core_out, chip_out, wide_f, wide_g):
    count = frames.shape[0]
    chans = frames.shape[3]
    lanes = chans // 128
    for t in range(count + 4):
        for h in range(2):
            if t < 2:
                value = before[t, h]
            elif t < count + 2:
                value = frames[t - 2, h]
            else:
                value = after[t - count - 2, h]
            value = value.astype(F32)
            for k in range(lanes):
                wide_f[lanes * h + k, 8 * t : 8 * (t + 1), :] = value[:, 128 * k : 128 * (k + 1)]
    for t in range(count + 2):
        for h in range(2):
            value = (out_grad[t, h] if t < count else after[t - count + 2, h]).astype(F32)
            for k in range(lanes):
                wide_g[lanes * h + k, 8 * t : 8 * (t + 1), :] = value[:, 128 * k : 128 * (k + 1)]
    even_core = place[1] == 0

    def column(source, at, rows):
        return jnp.concatenate(
            [source[k, pl.ds(at, rows, 8), :] for k in range(2 * lanes)], axis=1
        )

    def packed(first, second, grad):
        return jnp.concatenate(
            [
                column(wide_f, first, count + 4),
                column(wide_f, second, count + 4),
                column(wide_g, grad, count + 2),
                jnp.zeros((6, 2 * chans), F32),
            ],
            axis=0,
        )

    left = packed(0, 1, 0)
    right = packed(6, 7, 7)
    core_out[...] = jnp.where(even_core, right, left).astype(BF16)
    chip_out[...] = jnp.where(even_core, left, right).astype(BF16)


def pack(place, frames, out_grad, before, after):
    count, _, cols, chans = frames.shape
    rows = 3 * count + 16
    return pl.pallas_call(
        pack_kernel,
        out_shape=[pltpu.VMEM((rows, 2 * chans), BF16)] * 2,
        in_specs=[SMEM] + [VMEM] * 4,
        out_specs=[VMEM] * 2,
        scratch_shapes=[
            pltpu.VMEM((2 * chans // 128, cols * (count + 4), 128), F32),
            pltpu.VMEM((2 * chans // 128, cols * (count + 2), 128), F32),
        ],
        compiler_params=pltpu.CompilerParams(vmem_limit_bytes=12 * 2**20),
        name="pack",
    )(place, near(frames), near(out_grad), near(before), near(after))


def joined_frames(frames, before, after):
    count = frames.shape[0]

    def frame_of(t):
        if t < 2:
            part = lambda h: before[t, h]
        elif t < count + 2:
            part = lambda h: frames[t - 2, h]
        else:
            part = lambda h: after[t - count - 2, h]
        return jnp.concatenate([part(0).astype(F32), part(1).astype(F32)], axis=1)

    return frame_of


def centre_kernel(frames, before, after, folded, total, even, odd):
    build_centre(joined_frames(frames, before, after), frames.shape[0] + 4, even, odd)
    rows = total.shape[0]

    def weight_of(off, side):
        return folded[3 * off + side]

    sum_taps(total, 0, rows, (1,), even, odd, weight_of, NN)


def centre(frames, before, after, folded):
    count, _, cols, chans = frames.shape
    rows, wide = cols * (count + 2), 2 * chans
    return pl.pallas_call(
        centre_kernel,
        out_shape=pltpu.VMEM((rows, wide), F32),
        in_specs=[VMEM] * 4,
        out_specs=VMEM,
        scratch_shapes=[
            pltpu.VMEM((3, rows + 16, wide), BF16),
            pltpu.VMEM((3, rows, wide), BF16),
        ],
        compiler_params=pltpu.CompilerParams(vmem_limit_bytes=10 * 2**20),
        cost_estimate=pl.CostEstimate(
            flops=2 * 3 * rows * wide * wide, bytes_accessed=6 * 2**20, transcendentals=0
        ),
        name="centre",
    )(*(near(value) for value in (frames, before, after, folded)))


def forward_kernel(
    place,
    lengths,
    frames,
    before,
    after,
    core_sent,
    chip_sent,
    core_got,
    chip_got,
    out_grad,
    middle,
    down,
    folded,
    latent_out,
    sums_out,
    tail_out,
    low_out,
    high_out,
    grad_out,
    down_block,
    own_low,
    own_high,
    low,
    high,
    even,
    odd,
    total,
    act,
    sems,
):
    chans = frames.shape[-1]
    count = frames.shape[0]
    ahead = count + 2
    rows = 8 * ahead
    fetch_down = pltpu.make_async_copy(down, down_block, sems.at[0])
    fetch_down.start()
    even_core = place[1] == 0

    def pick(core, chip, at_low, at_high):
        core, chip = core[...].astype(F32), chip[...].astype(F32)
        at_low[...] = jnp.where(even_core, chip, core)
        at_high[...] = jnp.where(even_core, core, chip)

    pick(core_sent, chip_sent, own_low, own_high)
    pick(core_got, chip_got, low, high)

    frame_of = joined_frames(frames, before, after)
    span = count + 4

    def rim(side, off):
        left = ((low, 0), (low, span), (own_low, 0))[side]
        right = ((own_high, span), (high, 0), (high, span))[side]
        return jnp.concatenate(
            [ref[at + off : at + off + ahead + 6, :] for ref, at in (left, right)], axis=0
        ).astype(BF16)

    def weight_of(off, side):
        return folded[3 * off + side]

    def gates(pre):
        gate = 0.5 * jnp.tanh(0.5 * pre) + 0.5
        return gate, gate * (1.0 + pre * (1.0 - gate))

    def finish(first, last):
        for j in range(first, last):
            pre = total[64 * j : 64 * (j + 1), :]
            gate, slope = gates(pre)
            silu = pre * gate
            for h in range(2):
                lanes = slice(h * chans, (h + 1) * chans)
                own = frames[8 * j : 8 * (j + 1), h].astype(F32)
                act[j, :, :, lanes] = own + silu[:, lanes].reshape(own.shape)
                grad = out_grad[8 * j : 8 * (j + 1), h].astype(F32)
                grad = grad * slope[:, lanes].reshape(own.shape)
                grad_out[8 * j : 8 * (j + 1), :, lanes] = grad.astype(BF16)

    half = 64 * (count // 16)
    total[0:rows, :] = middle[...]
    build_sides(
        frame_of,
        lambda t: low[span + t : span + t + 1, :],
        lambda t: high[t : t + 1, :],
        span,
        even,
        odd,
    )
    edges = dot(rim(1, 0), folded[1])
    edges += dot(rim(1, 1), folded[4])
    edges += dot(rim(1, 2), folded[7])
    total[rows:, :] = edges
    sum_taps(total, 0, half, (0, 2), even, odd, weight_of, NN)
    sum_taps(total, half, rows - half, (0, 2), even, odd, weight_of, NN, rim)
    finish(0, count // 16)
    finish(count // 16, count // 8)
    for t in range(2):
        at = 8 * (count + t)
        _, slope = gates(total[at : at + 8, :])
        grad = jnp.concatenate([after[2 + t, 0].astype(F32), after[2 + t, 1].astype(F32)], axis=1)
        grad_out[count + t] = (grad * slope).astype(BF16)
    for at, (source, target) in enumerate(((low, low_out), (high, high_out))):
        base = rows + at * (ahead + 6)
        _, slope = gates(total[base : base + ahead + 6, :])
        target[...] = slope * source[2 * span : 2 * span + ahead + 6, :]

    fetch_down.wait()
    latent = jnp.zeros((2 * count, chans), F32)
    for k in range(8):
        lhs = jnp.concatenate(
            [
                act[:, k, :, h * chans : (h + 1) * chans].reshape(count, chans)
                for h in range(2)
            ],
            axis=0,
        ).astype(BF16)
        latent = latent + dot(lhs, down_block[k])
    latent = latent.astype(BF16).astype(F32)
    rounded = [
        jnp.concatenate([latent[8 * j : 8 * j + 8], latent[count + 8 * j : count + 8 * j + 8]], 0)
        for j in range(count // 8)
    ]
    running = jnp.zeros_like(rounded[0])
    for j in range(count // 8):
        now = place[0] * (count // 8) + j
        start = jnp.int32(0)
        begins = jnp.int32(0)
        for k in range(lengths.shape[0]):
            begins = jnp.where(start == now, 1, begins)
            start = start + lengths[k]
        running = jnp.where(begins > 0, rounded[j], running + rounded[j])
        sums_out[j] = running
        latent_out[j] = rounded[j]
    for k in range(tail_out.shape[0]):
        tail_out[k] = running


def forward(
    peers, place, lengths, frames, before, after, columns, out_grad, middle, down, folded
):
    count, _, cols, chans = frames.shape
    wide = 2 * chans
    lat = count // 8
    ahead = count + 2
    rows = cols * ahead
    received = columns[0].shape
    return pl.pallas_call(
        forward_kernel,
        out_shape=(
            pltpu.VMEM((lat, 16, chans), F32),
            pltpu.VMEM((lat, 16, chans), F32),
            pltpu.VMEM((peers, 16, chans), F32),
            pltpu.VMEM((ahead + 6, wide), F32),
            pltpu.VMEM((ahead + 6, wide), F32),
            pltpu.VMEM((ahead, cols, wide), BF16),
        ),
        in_specs=[SMEM, SMEM] + [VMEM] * 9 + [ANY, VMEM],
        out_specs=[VMEM] * 6,
        scratch_shapes=[
            pltpu.VMEM(down.shape, BF16),
            pltpu.VMEM(received, F32),
            pltpu.VMEM(received, F32),
            pltpu.VMEM(received, F32),
            pltpu.VMEM(received, F32),
            pltpu.VMEM((3, rows + 16, wide), BF16),
            pltpu.VMEM((3, rows, wide), BF16),
            pltpu.VMEM((rows + 2 * (ahead + 6), wide), F32),
            pltpu.VMEM((lat, 8, cols, wide), F32),
            pltpu.SemaphoreType.DMA((1,)),
        ],
        compiler_params=pltpu.CompilerParams(vmem_limit_bytes=22 * 2**20),
        cost_estimate=pl.CostEstimate(
            flops=2 * 9 * rows * wide * wide, bytes_accessed=16 * 2**20, transcendentals=rows * wide
        ),
        name="forward",
    )(
        place,
        lengths,
        *(near(value) for value in (frames, before, after, *columns, out_grad, middle)),
        down,
        near(folded),
    )


def backward_kernel(
    grad,
    low,
    high,
    out_grad,
    folded,
    result,
    done,
    even,
    odd,
    total,
    sems,
):
    count, _, cols, chans = out_grad.shape

    def frame_of(t):
        return grad[t]

    def weight_of(off, side):
        return folded[3 * (2 - off) + 2 - side]

    writes = []
    half = count // 2

    def finish(first, last):
        for j in range(first, last, 8):
            part = total[8 * j : 8 * (j + 8), :]
            for h in range(2):
                mine = part[:, h * chans : (h + 1) * chans].reshape(8, cols, chans)
                done[j : j + 8, h] = (out_grad[j : j + 8, h].astype(F32) + mine).astype(BF16)
        write = pltpu.make_async_copy(
            done.at[pl.ds(first, last - first)],
            result.at[pl.ds(first, last - first)],
            sems.at[len(writes)],
        )
        write.start()
        writes.append(write)

    build_centre(frame_of, count + 2, even, odd)
    sum_taps(total, 0, 8 * half, (1,), even, odd, weight_of, NT)
    build_sides(
        frame_of,
        lambda t: low[t : t + 1, :],
        lambda t: high[t : t + 1, :],
        count + 2,
        even,
        odd,
    )
    sum_taps(total, 0, 8 * half, (0, 2), even, odd, weight_of, NT)
    sum_taps(total, 8 * half, 8 * half, (1, 0, 2), even, odd, weight_of, NT)
    finish(0, half)
    finish(half, half + half // 2)
    finish(half + half // 2, count)
    for write in writes:
        write.wait()


def backward(grad, low, high, out_grad, folded):
    count, _, cols, chans = out_grad.shape
    rows, wide = count * cols, 2 * chans
    return pl.pallas_call(
        backward_kernel,
        out_shape=jax.ShapeDtypeStruct(out_grad.shape, BF16),
        in_specs=[VMEM] * 5,
        out_specs=ANY,
        scratch_shapes=[
            pltpu.VMEM(out_grad.shape, BF16),
            pltpu.VMEM((3, rows + 16, wide), BF16),
            pltpu.VMEM((3, rows, wide), BF16),
            pltpu.VMEM((rows, wide), F32),
            pltpu.SemaphoreType.DMA((3,)),
        ],
        compiler_params=pltpu.CompilerParams(vmem_limit_bytes=24 * 2**20),
        cost_estimate=pl.CostEstimate(
            flops=2 * 9 * rows * wide * wide, bytes_accessed=12 * 2**20, transcendentals=0
        ),
        name="backward",
    )(*(near(value) for value in (grad, low, high, out_grad, folded)))


def mix_kernel(place, lengths, latent, sums, tails, mixed):
    lat = latent.shape[0]
    peers = tails.shape[0]
    me = place[0]
    starts = [jnp.int32(0)]
    for k in range(lengths.shape[0] - 1):
        starts.append(starts[-1] + lengths[k])
    opened = jnp.int32(0)
    for start in starts:
        opened = jnp.where(start < me * lat, jnp.maximum(start, opened), opened)
    carried = jnp.zeros(latent.shape[1:], F32)
    for k in range(peers):
        counts = jnp.logical_and(k < me, (k + 1) * lat > opened)
        carried = carried + jnp.where(counts, tails[k], 0.0)
    for j in range(lat):
        now = me * lat + j
        begin = jnp.int32(0)
        for start in starts:
            begin = jnp.where(start <= now, jnp.maximum(start, begin), begin)
        shot = sums[j] + jnp.where(begin < me * lat, carried, 0.0)
        length = jnp.full(shot.shape, now - begin + 1, jnp.int32).astype(F32)
        mixed[16 * j : 16 * (j + 1), :] = (latent[j] + shot / length).astype(BF16)


def mix(place, lengths, latent, sums, tails):
    return pl.pallas_call(
        mix_kernel,
        out_shape=jax.ShapeDtypeStruct((latent.shape[0] * 16, latent.shape[2]), BF16),
        in_specs=[SMEM, SMEM, VMEM, VMEM, VMEM],
        out_specs=VMEM,
        compiler_params=pltpu.CompilerParams(vmem_limit_bytes=16 * 2**20),
        name="mix",
    )(place, lengths, near(latent), near(sums), near(tails))


def attend_kernel(labels, *refs):
    pieces, (w_query, w_key, w_value, w_out, result, keys, values) = refs[:-7], refs[-7:]
    mine = pieces[0]
    tokens, chans = mine.shape
    lat = labels.shape[0]
    per = tokens // lat
    heads = chans // HEAD
    group = len(pieces) // 2
    for first in range(0, len(pieces), group):
        block = jnp.concatenate([piece[...] for piece in pieces[first : first + group]], axis=0)
        for weight, target in ((w_key, keys), (w_value, values)):
            made = dot(block, weight[...]).astype(BF16)
            for k in range(group):
                for j in range(lat):
                    row = tokens * k + per * j
                    at = per * (first + k)
                    target[j, at : at + per, :] = made[row : row + per, :]
    query = dot(mine[...], w_query[...]).astype(BF16).astype(F32) * (1.0 / math.sqrt(HEAD))
    head_of = lax.broadcasted_iota(jnp.int32, (per, chans), 1) // HEAD
    partners, scores = [], []
    for j in range(lat):
        partner = jnp.int32(-1)
        for k in range(j):
            partner = jnp.where(labels[k, 0] == labels[j, 0], k, partner)
        partners.append(jnp.maximum(partner, 0))
        own = query[per * j : per * (j + 1), :]
        stacked = jnp.concatenate(
            [jnp.where(head_of == h, own, 0.0) for h in range(heads)], axis=0
        ).astype(BF16)
        bias = jnp.where(partner >= 0, 0.0, -1e30).astype(F32)
        both = jnp.concatenate([keys[j], keys[partners[j]]], axis=0)
        made = dot(stacked, both, NT)
        half = made.shape[1] // 2
        scores.append(jnp.concatenate([made[:, :half], made[:, half:] + bias], axis=1))
    weights, norms = [], []
    for j in range(lat):
        expo = jnp.exp(scores[j] - jnp.max(scores[j], axis=1, keepdims=True))
        norms.append(jnp.sum(expo, axis=1, keepdims=True))
        weights.append(expo.astype(BF16))
    mixes = []
    for j in range(lat):
        both = jnp.concatenate([values[j], values[partners[j]]], axis=0)
        mixes.append(dot(weights[j], both))
    outs = []
    for j in range(lat):
        mixed = mixes[j] / norms[j]
        total = jnp.zeros((per, chans), F32)
        for h in range(heads):
            total = jnp.where(head_of == h, mixed[per * h : per * (h + 1), :], total)
        outs.append(total)
    attended = jnp.concatenate(outs, axis=0).astype(BF16)
    final = mine[...].astype(F32) + dot(attended, w_out[...])
    for j in range(lat):
        for h in range(2):
            at = per * j + 8 * h
            result[j, h] = final[at : at + 8].astype(BF16)


def attend(labels, pieces, w_query, w_key, w_value, w_out):
    tokens, chans = pieces[0].shape
    lat = labels.shape[0]
    held = (lat, len(pieces) * tokens // lat, chans)
    return pl.pallas_call(
        attend_kernel,
        out_shape=jax.ShapeDtypeStruct((lat, 2, 8, chans), BF16),
        in_specs=[SMEM] + [VMEM] * (4 + len(pieces)),
        out_specs=VMEM,
        scratch_shapes=[pltpu.VMEM(held, BF16), pltpu.VMEM(held, BF16)],
        compiler_params=pltpu.CompilerParams(vmem_limit_bytes=24 * 2**20),
        name="attend",
    )(labels, *(near(piece) for piece in pieces), w_query, w_key, w_value, w_out)


def shifted(value, axis, steps):
    count = lax.axis_size(axis)
    return lax.ppermute(
        value, axis, [(i, i + steps) for i in range(count) if 0 <= i + steps < count]
    )


def with_core(value):
    count = lax.axis_size("scene")
    return lax.ppermute(value, "scene", [(i, i ^ 1) for i in range(count)])


def with_chip(value):
    count = lax.axis_size("scene")
    pairs = [(i, i + 1) for i in range(1, count - 1, 2)]
    return lax.ppermute(value, "scene", pairs + [(b, a) for a, b in pairs])


def chip_shifts(value):
    count = lax.axis_size("scene")
    return [
        lax.ppermute(value, "scene", [(i, (i + 2 * k) % count) for i in range(count)])
        for k in range(1, count // 2)
    ]


def per_device(
    frames,
    conv_weight,
    down_weight,
    w_query,
    w_key,
    w_value,
    w_out,
    shot_lengths,
    scene_label,
    out_grad,
):
    place = jnp.stack([lax.axis_index("tm"), lax.axis_index("scene") % 2]).astype(jnp.int32)
    last, first = cut(
        *(pltpu.with_memory_space_constraint(value, pltpu.HBM) for value in (frames, out_grad))
    )
    before = shifted(last, "tm", 1)
    after = shifted(first, "tm", -1)
    near_frames, near_grad, near_weight = fetch(frames, out_grad, conv_weight)
    (before, after), near_weight = lax.optimization_barrier(((before, after), near_weight))
    sent = pack(place, near_frames, near_grad, before, after)
    received = (with_core(sent[0]), with_chip(sent[1]))
    folded = fold(near_weight)
    middle = centre(near_frames, before, after, folded)
    received, middle = lax.optimization_barrier((received, middle))
    latent, sums, tail, low, high, grad = forward(
        lax.axis_size("tm"),
        place,
        shot_lengths,
        near_frames,
        before,
        after,
        (*sent, *received),
        near_grad,
        middle,
        down_weight,
        folded,
    )
    tails = lax.all_to_all(tail, "tm", 0, 0, tiled=True)
    mixed = mix(place, shot_lengths, latent, sums, tails)
    chips = chip_shifts(mixed)
    frame_grad = backward(grad, low, high, near_grad, folded)
    chips, frame_grad = lax.optimization_barrier((chips, frame_grad))
    pieces = [mixed, *chips]
    pieces += [with_core(piece) for piece in pieces]
    latent_out = attend(scene_label, pieces, w_query, w_key, w_value, w_out)
    return (latent_out, frame_grad)


def solution(mesh):
    in_specs = (
        P("tm", None, "scene", None),
        P(),
        P(),
        P(),
        P(),
        P(),
        P(),
        P(),
        P("tm", None),
        P("tm", None, "scene", None),
    )
    out_specs = (P("tm", None, "scene", None), P("tm", None, "scene", None))
    return jax.shard_map(
        per_device, mesh=mesh, in_specs=in_specs, out_specs=out_specs, check_vma=False
    )
```

```python
import math

import jax
import jax.numpy as jnp
from jax import lax
from jax.experimental import pallas as pl
from jax.experimental.pallas import tpu as pltpu
from jax.sharding import PartitionSpec as P

HEAD = 64
BF16 = jnp.bfloat16
F32 = jnp.float32
VMEM = pl.BlockSpec(memory_space=pltpu.VMEM)
SMEM = pl.BlockSpec(memory_space=pltpu.SMEM)
ANY = pl.BlockSpec(memory_space=pl.ANY)
NT = (((1,), (1,)), ((), ()))
NN = (((1,), (0,)), ((), ()))

def near(value):
    return pltpu.with_memory_space_constraint(value, pltpu.VMEM)


def dot(a, b, dims=NN):
    return lax.dot_general(a, b, dims, preferred_element_type=F32)


def cut_kernel(frames, out_grad, last, first, sems):
    count = frames.shape[0]
    copies = [
        pltpu.make_async_copy(frames.at[pl.ds(count - 2, 2)], last, sems.at[0]),
        pltpu.make_async_copy(frames.at[pl.ds(0, 2)], first.at[pl.ds(0, 2)], sems.at[1]),
        pltpu.make_async_copy(out_grad.at[pl.ds(0, 2)], first.at[pl.ds(2, 2)], sems.at[2]),
    ]
    for copy in copies:
        copy.start()
    for copy in copies:
        copy.wait()


def cut(frames, out_grad):
    shape = frames.shape[1:]
    return pl.pallas_call(
        cut_kernel,
        out_shape=[pltpu.VMEM((2, *shape), BF16), pltpu.VMEM((4, *shape), BF16)],
        in_specs=[pl.BlockSpec(memory_space=pltpu.HBM)] * 2,
        out_specs=[VMEM] * 2,
        scratch_shapes=[pltpu.SemaphoreType.DMA((3,))],
        compiler_params=pltpu.CompilerParams(vmem_limit_bytes=60 * 2**20),
        name="cut",
    )(frames, out_grad)


def fetch_kernel(frames, out_grad, weight, frames_out, grad_out, weight_out, sems):
    copies = [
        pltpu.make_async_copy(source, target, sems.at[k])
        for k, (source, target) in enumerate(
            ((frames, frames_out), (out_grad, grad_out), (weight.at[pl.ds(0, 2)], weight_out))
        )
    ]
    for copy in copies:
        copy.start()
    for copy in copies:
        copy.wait()


def fetch(frames, out_grad, weight):
    return pl.pallas_call(
        fetch_kernel,
        out_shape=[
            pltpu.VMEM(shape, BF16)
            for shape in (frames.shape, out_grad.shape, (2, *weight.shape[1:]))
        ],
        in_specs=[ANY] * 3,
        out_specs=[VMEM] * 3,
        scratch_shapes=[pltpu.SemaphoreType.DMA((3,))],
        compiler_params=pltpu.CompilerParams(vmem_limit_bytes=48 * 2**20),
        cost_estimate=pl.CostEstimate(
            flops=0, bytes_accessed=20 * 2**20, transcendentals=0
        ),
        name="fetch",
    )(frames, out_grad, weight)


def fold_kernel(held, weight, folded, sems):
    chans = weight.shape[-1]
    copies = []
    for k in (6, 7, 8, 0, 1, 2, 3, 4, 5):
        source = weight if k >= 6 else held
        for h_in in range(2):
            for h_out in range(2):
                copies.append(
                    pltpu.make_async_copy(
                        source.at[k // 3, h_in - h_out + 1, k % 3],
                        folded.at[k, pl.ds(h_in * chans, chans), pl.ds(h_out * chans, chans)],
                        sems.at[k, 2 * h_in + h_out],
                    )
                )
    for copy in copies:
        copy.start()
    for copy in copies:
        copy.wait()


def fold(held, weight):
    wide = 2 * weight.shape[-1]
    return pl.pallas_call(
        fold_kernel,
        out_shape=pltpu.VMEM((9, wide, wide), BF16),
        in_specs=[VMEM, pl.BlockSpec(memory_space=pltpu.HBM)],
        out_specs=VMEM,
        scratch_shapes=[pltpu.SemaphoreType.DMA((9, 4))],
        compiler_params=pltpu.CompilerParams(vmem_limit_bytes=4 * 2**20),
        cost_estimate=pl.CostEstimate(
            flops=0, bytes_accessed=20 * 2**20, transcendentals=0
        ),
        name="fold",
    )(near(held), pltpu.with_memory_space_constraint(weight, pltpu.HBM))


def store_pairs(values_of, sides, count, even, odd):
    before = None
    for t in range(count):
        now = values_of(t)
        for at, s in enumerate(sides):
            if t % 2 == 1:
                pair = jnp.concatenate([before[at], now[at]], axis=0).astype(BF16)
                even[s, 8 * (t - 1) : 8 * (t + 1), :] = pair
            elif t > 0:
                pair = jnp.concatenate([before[at], now[at]], axis=0).astype(BF16)
                odd[s, 8 * (t - 2) : 8 * t, :] = pair
        before = now


def build_centre(frame_of, count, even, odd):
    store_pairs(lambda t: (frame_of(t).astype(F32),), (1,), count, even, odd)


def build_sides(frame_of, low_of, high_of, count, even, odd):
    width = even.shape[2]
    sub = lax.broadcasted_iota(jnp.int32, (8, width), 0)

    def both(t):
        own = frame_of(t).astype(F32)
        left = jnp.where(sub == 0, jnp.broadcast_to(low_of(t), (8, width)), pltpu.roll(own, 1, 0))
        right = jnp.where(sub == 7, jnp.broadcast_to(high_of(t), (8, width)), pltpu.roll(own, 7, 0))
        return left, right

    store_pairs(both, (0, 2), count, even, odd)


def sum_taps(total, at, rows, sides, even, odd, weight_of, dims, extra=None):
    count = rows
    for side in sides:
        for off in range(3):
            if off == 1:
                lhs = odd[side, at : at + rows, :]
            else:
                lhs = even[side, at + 8 * off : at + 8 * off + rows, :]
            if extra is not None:
                lhs = jnp.concatenate([lhs, extra(side, off)], axis=0)
                count = lhs.shape[0]
            part = dot(lhs, weight_of(off, side), dims)
            if (side, off) == (1, 0):
                total[at : at + count, :] = part
            else:
                total[at : at + count, :] += part


def pack_kernel(place, frames, out_grad, before, after, core_out, chip_out, wide_f, wide_g):
    count = frames.shape[0]
    chans = frames.shape[3]
    lanes = chans // 128
    for t in range(count + 4):
        for h in range(2):
            if t < 2:
                value = before[t, h]
            elif t < count + 2:
                value = frames[t - 2, h]
            else:
                value = after[t - count - 2, h]
            value = value.astype(F32)
            for k in range(lanes):
                wide_f[lanes * h + k, 8 * t : 8 * (t + 1), :] = value[:, 128 * k : 128 * (k + 1)]
    for t in range(count + 2):
        for h in range(2):
            value = (out_grad[t, h] if t < count else after[t - count + 2, h]).astype(F32)
            for k in range(lanes):
                wide_g[lanes * h + k, 8 * t : 8 * (t + 1), :] = value[:, 128 * k : 128 * (k + 1)]
    even_core = place[1] == 0

    def column(source, at, rows):
        return jnp.concatenate(
            [source[k, pl.ds(at, rows, 8), :] for k in range(2 * lanes)], axis=1
        )

    def packed(first, second, grad):
        return jnp.concatenate(
            [
                column(wide_f, first, count + 4),
                column(wide_f, second, count + 4),
                column(wide_g, grad, count + 2),
                jnp.zeros((6, 2 * chans), F32),
            ],
            axis=0,
        )

    left = packed(0, 1, 0)
    right = packed(6, 7, 7)
    core_out[...] = jnp.where(even_core, right, left).astype(BF16)
    chip_out[...] = jnp.where(even_core, left, right).astype(BF16)


def pack(place, frames, out_grad, before, after):
    count, _, cols, chans = frames.shape
    rows = 3 * count + 16
    return pl.pallas_call(
        pack_kernel,
        out_shape=[pltpu.VMEM((rows, 2 * chans), BF16)] * 2,
        in_specs=[SMEM] + [VMEM] * 4,
        out_specs=[VMEM] * 2,
        scratch_shapes=[
            pltpu.VMEM((2 * chans // 128, cols * (count + 4), 128), F32),
            pltpu.VMEM((2 * chans // 128, cols * (count + 2), 128), F32),
        ],
        compiler_params=pltpu.CompilerParams(vmem_limit_bytes=12 * 2**20),
        name="pack",
    )(place, near(frames), near(out_grad), near(before), near(after))


def joined_frames(frames, before, after):
    count = frames.shape[0]

    def frame_of(t):
        if t < 2:
            part = lambda h: before[t, h]
        elif t < count + 2:
            part = lambda h: frames[t - 2, h]
        else:
            part = lambda h: after[t - count - 2, h]
        return jnp.concatenate([part(0).astype(F32), part(1).astype(F32)], axis=1)

    return frame_of


def centre_kernel(frames, before, after, folded, total, even, odd):
    build_centre(joined_frames(frames, before, after), frames.shape[0] + 4, even, odd)
    rows = total.shape[0]

    def weight_of(off, side):
        return folded[3 * off + side]

    sum_taps(total, 0, rows, (1,), even, odd, weight_of, NN)


def centre(frames, before, after, folded):
    count, _, cols, chans = frames.shape
    rows, wide = cols * (count + 2), 2 * chans
    return pl.pallas_call(
        centre_kernel,
        out_shape=pltpu.VMEM((rows, wide), F32),
        in_specs=[VMEM] * 4,
        out_specs=VMEM,
        scratch_shapes=[
            pltpu.VMEM((3, rows + 16, wide), BF16),
            pltpu.VMEM((3, rows, wide), BF16),
        ],
        compiler_params=pltpu.CompilerParams(vmem_limit_bytes=10 * 2**20),
        cost_estimate=pl.CostEstimate(
            flops=2 * 3 * rows * wide * wide, bytes_accessed=6 * 2**20, transcendentals=0
        ),
        name="centre",
    )(*(near(value) for value in (frames, before, after, folded)))


def forward_kernel(
    place,
    lengths,
    frames,
    before,
    after,
    core_sent,
    chip_sent,
    core_got,
    chip_got,
    out_grad,
    middle,
    down,
    folded,
    latent_out,
    sums_out,
    tail_out,
    low_out,
    high_out,
    grad_out,
    down_block,
    own_low,
    own_high,
    low,
    high,
    even,
    odd,
    total,
    act,
    sems,
):
    chans = frames.shape[-1]
    count = frames.shape[0]
    ahead = count + 2
    rows = 8 * ahead
    fetch_down = pltpu.make_async_copy(down, down_block, sems.at[0])
    fetch_down.start()
    even_core = place[1] == 0

    def pick(core, chip, at_low, at_high):
        core, chip = core[...].astype(F32), chip[...].astype(F32)
        at_low[...] = jnp.where(even_core, chip, core)
        at_high[...] = jnp.where(even_core, core, chip)

    pick(core_sent, chip_sent, own_low, own_high)
    pick(core_got, chip_got, low, high)

    frame_of = joined_frames(frames, before, after)
    span = count + 4

    def rim(side, off):
        left = ((low, 0), (low, span), (own_low, 0))[side]
        right = ((own_high, span), (high, 0), (high, span))[side]
        return jnp.concatenate(
            [ref[at + off : at + off + ahead + 6, :] for ref, at in (left, right)], axis=0
        ).astype(BF16)

    def weight_of(off, side):
        return folded[3 * off + side]

    def gates(pre):
        gate = 0.5 * jnp.tanh(0.5 * pre) + 0.5
        return gate, gate * (1.0 + pre * (1.0 - gate))

    def finish(first, last):
        for j in range(first, last):
            pre = total[64 * j : 64 * (j + 1), :]
            gate, slope = gates(pre)
            silu = pre * gate
            for h in range(2):
                lanes = slice(h * chans, (h + 1) * chans)
                own = frames[8 * j : 8 * (j + 1), h].astype(F32)
                act[j, :, :, lanes] = own + silu[:, lanes].reshape(own.shape)
                grad = out_grad[8 * j : 8 * (j + 1), h].astype(F32)
                grad = grad * slope[:, lanes].reshape(own.shape)
                grad_out[8 * j : 8 * (j + 1), :, lanes] = grad.astype(BF16)

    half = 64 * (count // 16)
    total[0:rows, :] = middle[...]
    build_sides(
        frame_of,
        lambda t: low[span + t : span + t + 1, :],
        lambda t: high[t : t + 1, :],
        span,
        even,
        odd,
    )
    edges = dot(rim(1, 0), folded[1])
    edges += dot(rim(1, 1), folded[4])
    edges += dot(rim(1, 2), folded[7])
    total[rows:, :] = edges
    sum_taps(total, 0, half, (0, 2), even, odd, weight_of, NN)
    sum_taps(total, half, rows - half, (0, 2), even, odd, weight_of, NN, rim)
    finish(0, count // 16)
    finish(count // 16, count // 8)
    for t in range(2):
        at = 8 * (count + t)
        _, slope = gates(total[at : at + 8, :])
        grad = jnp.concatenate([after[2 + t, 0].astype(F32), after[2 + t, 1].astype(F32)], axis=1)
        grad_out[count + t] = (grad * slope).astype(BF16)
    for at, (source, target) in enumerate(((low, low_out), (high, high_out))):
        base = rows + at * (ahead + 6)
        _, slope = gates(total[base : base + ahead + 6, :])
        target[...] = slope * source[2 * span : 2 * span + ahead + 6, :]

    fetch_down.wait()
    latent = jnp.zeros((2 * count, chans), F32)
    for k in range(8):
        lhs = jnp.concatenate(
            [
                act[:, k, :, h * chans : (h + 1) * chans].reshape(count, chans)
                for h in range(2)
            ],
            axis=0,
        ).astype(BF16)
        latent = latent + dot(lhs, down_block[k])
    latent = latent.astype(BF16).astype(F32)
    rounded = [
        jnp.concatenate([latent[8 * j : 8 * j + 8], latent[count + 8 * j : count + 8 * j + 8]], 0)
        for j in range(count // 8)
    ]
    running = jnp.zeros_like(rounded[0])
    for j in range(count // 8):
        now = place[0] * (count // 8) + j
        start = jnp.int32(0)
        begins = jnp.int32(0)
        for k in range(lengths.shape[0]):
            begins = jnp.where(start == now, 1, begins)
            start = start + lengths[k]
        running = jnp.where(begins > 0, rounded[j], running + rounded[j])
        sums_out[j] = running
        latent_out[j] = rounded[j]
    for k in range(tail_out.shape[0]):
        tail_out[k] = running


def forward(
    peers, place, lengths, frames, before, after, columns, out_grad, middle, down, folded
):
    count, _, cols, chans = frames.shape
    wide = 2 * chans
    lat = count // 8
    ahead = count + 2
    rows = cols * ahead
    received = columns[0].shape
    return pl.pallas_call(
        forward_kernel,
        out_shape=(
            pltpu.VMEM((lat, 16, chans), F32),
            pltpu.VMEM((lat, 16, chans), F32),
            pltpu.VMEM((peers, 16, chans), F32),
            pltpu.VMEM((ahead + 6, wide), F32),
            pltpu.VMEM((ahead + 6, wide), F32),
            pltpu.VMEM((ahead, cols, wide), BF16),
        ),
        in_specs=[SMEM, SMEM] + [VMEM] * 9 + [ANY, VMEM],
        out_specs=[VMEM] * 6,
        scratch_shapes=[
            pltpu.VMEM(down.shape, BF16),
            pltpu.VMEM(received, F32),
            pltpu.VMEM(received, F32),
            pltpu.VMEM(received, F32),
            pltpu.VMEM(received, F32),
            pltpu.VMEM((3, rows + 16, wide), BF16),
            pltpu.VMEM((3, rows, wide), BF16),
            pltpu.VMEM((rows + 2 * (ahead + 6), wide), F32),
            pltpu.VMEM((lat, 8, cols, wide), F32),
            pltpu.SemaphoreType.DMA((1,)),
        ],
        compiler_params=pltpu.CompilerParams(vmem_limit_bytes=22 * 2**20),
        cost_estimate=pl.CostEstimate(
            flops=2 * 9 * rows * wide * wide, bytes_accessed=16 * 2**20, transcendentals=rows * wide
        ),
        name="forward",
    )(
        place,
        lengths,
        *(near(value) for value in (frames, before, after, *columns, out_grad, middle)),
        down,
        near(folded),
    )


def backward_kernel(
    grad,
    low,
    high,
    out_grad,
    folded,
    result,
    done,
    even,
    odd,
    total,
    sems,
):
    count, _, cols, chans = out_grad.shape

    def frame_of(t):
        return grad[t]

    def weight_of(off, side):
        return folded[3 * (2 - off) + 2 - side]

    writes = []
    half = count // 2

    def finish(first, last):
        for j in range(first, last, 8):
            part = total[8 * j : 8 * (j + 8), :]
            for h in range(2):
                mine = part[:, h * chans : (h + 1) * chans].reshape(8, cols, chans)
                done[j : j + 8, h] = (out_grad[j : j + 8, h].astype(F32) + mine).astype(BF16)
        write = pltpu.make_async_copy(
            done.at[pl.ds(first, last - first)],
            result.at[pl.ds(first, last - first)],
            sems.at[len(writes)],
        )
        write.start()
        writes.append(write)

    build_centre(frame_of, count + 2, even, odd)
    sum_taps(total, 0, 8 * half, (1,), even, odd, weight_of, NT)
    build_sides(
        frame_of,
        lambda t: low[t : t + 1, :],
        lambda t: high[t : t + 1, :],
        count + 2,
        even,
        odd,
    )
    sum_taps(total, 0, 8 * half, (0, 2), even, odd, weight_of, NT)
    sum_taps(total, 8 * half, 8 * half, (1, 0, 2), even, odd, weight_of, NT)
    finish(0, half)
    finish(half, half + half // 2)
    finish(half + half // 2, count)
    for write in writes:
        write.wait()


def backward(grad, low, high, out_grad, folded):
    count, _, cols, chans = out_grad.shape
    rows, wide = count * cols, 2 * chans
    return pl.pallas_call(
        backward_kernel,
        out_shape=jax.ShapeDtypeStruct(out_grad.shape, BF16),
        in_specs=[VMEM] * 5,
        out_specs=ANY,
        scratch_shapes=[
            pltpu.VMEM(out_grad.shape, BF16),
            pltpu.VMEM((3, rows + 16, wide), BF16),
            pltpu.VMEM((3, rows, wide), BF16),
            pltpu.VMEM((rows, wide), F32),
            pltpu.SemaphoreType.DMA((3,)),
        ],
        compiler_params=pltpu.CompilerParams(vmem_limit_bytes=24 * 2**20),
        cost_estimate=pl.CostEstimate(
            flops=2 * 9 * rows * wide * wide, bytes_accessed=12 * 2**20, transcendentals=0
        ),
        name="backward",
    )(*(near(value) for value in (grad, low, high, out_grad, folded)))


def mix_kernel(place, lengths, latent, sums, tails, mixed):
    lat = latent.shape[0]
    peers = tails.shape[0]
    me = place[0]
    starts = [jnp.int32(0)]
    for k in range(lengths.shape[0] - 1):
        starts.append(starts[-1] + lengths[k])
    opened = jnp.int32(0)
    for start in starts:
        opened = jnp.where(start < me * lat, jnp.maximum(start, opened), opened)
    carried = jnp.zeros(latent.shape[1:], F32)
    for k in range(peers):
        counts = jnp.logical_and(k < me, (k + 1) * lat > opened)
        carried = carried + jnp.where(counts, tails[k], 0.0)
    for j in range(lat):
        now = me * lat + j
        begin = jnp.int32(0)
        for start in starts:
            begin = jnp.where(start <= now, jnp.maximum(start, begin), begin)
        shot = sums[j] + jnp.where(begin < me * lat, carried, 0.0)
        length = jnp.full(shot.shape, now - begin + 1, jnp.int32).astype(F32)
        mixed[16 * j : 16 * (j + 1), :] = (latent[j] + shot / length).astype(BF16)


def mix(place, lengths, latent, sums, tails):
    return pl.pallas_call(
        mix_kernel,
        out_shape=jax.ShapeDtypeStruct((latent.shape[0] * 16, latent.shape[2]), BF16),
        in_specs=[SMEM, SMEM, VMEM, VMEM, VMEM],
        out_specs=VMEM,
        compiler_params=pltpu.CompilerParams(vmem_limit_bytes=16 * 2**20),
        name="mix",
    )(place, lengths, near(latent), near(sums), near(tails))


def attend_kernel(labels, *refs):
    pieces, (w_query, w_key, w_value, w_out, result, keys, values) = refs[:-7], refs[-7:]
    mine = pieces[0]
    tokens, chans = mine.shape
    lat = labels.shape[0]
    per = tokens // lat
    heads = chans // HEAD
    group = len(pieces) // 2
    for first in range(0, len(pieces), group):
        block = jnp.concatenate([piece[...] for piece in pieces[first : first + group]], axis=0)
        for weight, target in ((w_key, keys), (w_value, values)):
            made = dot(block, weight[...]).astype(BF16)
            for k in range(group):
                for j in range(lat):
                    row = tokens * k + per * j
                    at = per * (first + k)
                    target[j, at : at + per, :] = made[row : row + per, :]
    query = dot(mine[...], w_query[...]).astype(BF16).astype(F32) * (1.0 / math.sqrt(HEAD))
    head_of = lax.broadcasted_iota(jnp.int32, (per, chans), 1) // HEAD
    partners, scores = [], []
    for j in range(lat):
        partner = jnp.int32(-1)
        for k in range(j):
            partner = jnp.where(labels[k, 0] == labels[j, 0], k, partner)
        partners.append(jnp.maximum(partner, 0))
        own = query[per * j : per * (j + 1), :]
        stacked = jnp.concatenate(
            [jnp.where(head_of == h, own, 0.0) for h in range(heads)], axis=0
        ).astype(BF16)
        bias = jnp.where(partner >= 0, 0.0, -1e30).astype(F32)
        both = jnp.concatenate([keys[j], keys[partners[j]]], axis=0)
        made = dot(stacked, both, NT)
        half = made.shape[1] // 2
        scores.append(jnp.concatenate([made[:, :half], made[:, half:] + bias], axis=1))
    weights, norms = [], []
    for j in range(lat):
        expo = jnp.exp(scores[j] - jnp.max(scores[j], axis=1, keepdims=True))
        norms.append(jnp.sum(expo, axis=1, keepdims=True))
        weights.append(expo.astype(BF16))
    mixes = []
    for j in range(lat):
        both = jnp.concatenate([values[j], values[partners[j]]], axis=0)
        mixes.append(dot(weights[j], both))
    outs = []
    for j in range(lat):
        mixed = mixes[j] / norms[j]
        total = jnp.zeros((per, chans), F32)
        for h in range(heads):
            total = jnp.where(head_of == h, mixed[per * h : per * (h + 1), :], total)
        outs.append(total)
    attended = jnp.concatenate(outs, axis=0).astype(BF16)
    final = mine[...].astype(F32) + dot(attended, w_out[...])
    for j in range(lat):
        for h in range(2):
            at = per * j + 8 * h
            result[j, h] = final[at : at + 8].astype(BF16)


def attend(labels, pieces, w_query, w_key, w_value, w_out):
    tokens, chans = pieces[0].shape
    lat = labels.shape[0]
    held = (lat, len(pieces) * tokens // lat, chans)
    return pl.pallas_call(
        attend_kernel,
        out_shape=jax.ShapeDtypeStruct((lat, 2, 8, chans), BF16),
        in_specs=[SMEM] + [VMEM] * (4 + len(pieces)),
        out_specs=VMEM,
        scratch_shapes=[pltpu.VMEM(held, BF16), pltpu.VMEM(held, BF16)],
        compiler_params=pltpu.CompilerParams(vmem_limit_bytes=24 * 2**20),
        name="attend",
    )(labels, *(near(piece) for piece in pieces), w_query, w_key, w_value, w_out)


def shifted(value, axis, steps):
    count = lax.axis_size(axis)
    return lax.ppermute(
        value, axis, [(i, i + steps) for i in range(count) if 0 <= i + steps < count]
    )


def with_core(value):
    count = lax.axis_size("scene")
    return lax.ppermute(value, "scene", [(i, i ^ 1) for i in range(count)])


def with_chip(value):
    count = lax.axis_size("scene")
    pairs = [(i, i + 1) for i in range(1, count - 1, 2)]
    return lax.ppermute(value, "scene", pairs + [(b, a) for a, b in pairs])


def chip_shifts(value):
    count = lax.axis_size("scene")
    return [
        lax.ppermute(value, "scene", [(i, (i + 2 * k) % count) for i in range(count)])
        for k in range(1, count // 2)
    ]


def per_device(
    frames,
    conv_weight,
    down_weight,
    w_query,
    w_key,
    w_value,
    w_out,
    shot_lengths,
    scene_label,
    out_grad,
):
    place = jnp.stack([lax.axis_index("tm"), lax.axis_index("scene") % 2]).astype(jnp.int32)
    last, first = cut(
        *(pltpu.with_memory_space_constraint(value, pltpu.HBM) for value in (frames, out_grad))
    )
    before = shifted(last, "tm", 1)
    after = shifted(first, "tm", -1)
    near_frames, near_grad, near_weight = fetch(frames, out_grad, conv_weight)
    (before, after), near_weight = lax.optimization_barrier(((before, after), near_weight))
    sent = pack(place, near_frames, near_grad, before, after)
    received = (with_core(sent[0]), with_chip(sent[1]))
    folded = fold(near_weight, conv_weight)
    middle = centre(near_frames, before, after, folded)
    received, middle = lax.optimization_barrier((received, middle))
    latent, sums, tail, low, high, grad = forward(
        lax.axis_size("tm"),
        place,
        shot_lengths,
        near_frames,
        before,
        after,
        (*sent, *received),
        near_grad,
        middle,
        down_weight,
        folded,
    )
    tails = lax.all_to_all(tail, "tm", 0, 0, tiled=True)
    mixed = mix(place, shot_lengths, latent, sums, tails)
    chips = chip_shifts(mixed)
    frame_grad = backward(grad, low, high, near_grad, folded)
    chips, frame_grad = lax.optimization_barrier((chips, frame_grad))
    pieces = [mixed, *chips]
    pieces += [with_core(piece) for piece in pieces]
    latent_out = attend(scene_label, pieces, w_query, w_key, w_value, w_out)
    return (latent_out, frame_grad)


def solution(mesh):
    in_specs = (
        P("tm", None, "scene", None),
        P(),
        P(),
        P(),
        P(),
        P(),
        P(),
        P(),
        P("tm", None),
        P("tm", None, "scene", None),
    )
    out_specs = (P("tm", None, "scene", None), P("tm", None, "scene", None))
    return jax.shard_map(
        per_device, mesh=mesh, in_specs=in_specs, out_specs=out_specs, check_vma=False
    )
```
